256 devices in a mesh: seq: 4 (over y_lo, core), fsdp: 64 (over x, z, y_hi).
Axes of the slice: x: 4, y: 4 (y_hi: 2, y_lo: 2; y = y_hi * 2 + y_lo), z: 8, core: 2. Of those that a mesh axis runs over, the one named last changes fastest.
Arguments:
- tokens: bfloat16 [2, 2048, 4096], P(None, 'seq'), may hold values from -6 to 6
- out_grad: bfloat16 [2, 2048, 4096], P(None, 'seq', 'fsdp'), may hold values from -6 to 6
- gate_weight: bfloat16 [4096, 8192], P(None, 'fsdp'), may hold values from -0.09375 to 0.09375
- up_weight: bfloat16 [4096, 8192], P(None, 'fsdp'), may hold values from -0.09375 to 0.09375
- down_weight: bfloat16 [8192, 4096], P('fsdp'), may hold values from -0.0625 to 0.0625
- proj_gate_in: bfloat16 [4096, 64], replicated, may hold values from -0.09375 to 0.09375
- proj_gate_out: bfloat16 [8192, 64], P('fsdp'), may hold values from -0.0625 to 0.0625
- proj_up_in: bfloat16 [4096, 64], replicated, may hold values from -0.09375 to 0.09375
- proj_up_out: bfloat16 [8192, 64], P('fsdp'), may hold values from -0.0625 to 0.0625
- proj_down_in: bfloat16 [8192, 64], P('fsdp'), may hold values from -0.0625 to 0.0625
- proj_down_out: bfloat16 [4096, 64], replicated, may hold values from -0.09375 to 0.09375
- lengths: int32 [2], replicated, may hold values from 512 to 2048, as said below
Outputs:
- projected: float32 [2, 3, 4096], P(None, None, 'seq')
The draws below stay inside these ranges and needn't reach their ends.
Inputs may be any that keep to these rules, and one draw needn't show every extreme that they name: `lengths`: at least one example has all 2048 tokens valid.
All inputs are finite; a program needn't handle non-finite values.
Results may differ from the reference program's by a relative error of at most 0.003.
Values may be sent and summed in bfloat16 or wider, within the bound.
No kernel may reach another device: no remote copies, remote signals or barrier semaphores. Data moves between devices by JAX's collectives and lax.ppermute only.
A program may use at most 128 MiB of HBM per device.

```python
import jax
import jax.numpy as jnp
from jax import lax

D = 4096
FF = 8192
RANK = 64
EXAMPLES = 2
SEQ = 2048


def draw_lengths(key, part):
    key = jax.random.fold_in(key, 7)
    first_key, second_key = jax.random.split(key)
    drawn_lengths = jax.random.randint(first_key, (EXAMPLES,), SEQ // 4, SEQ + 1)
    full_index = jax.random.randint(second_key, (), 0, EXAMPLES)
    return jnp.where(jnp.arange(EXAMPLES) == full_index, SEQ, drawn_lengths).astype(jnp.int32)


def levels(stream_key, shape, cuts, least, top_value):
    gain, own = 1.0, jax.random.fold_in(stream_key, 6)
    for axis_at, parts in cuts:
        heights = jnp.exp(jax.random.uniform(jax.random.fold_in(own, axis_at), (parts,), jnp.float32, least / len(cuts), top_value / len(cuts)))
        gain = gain * jnp.repeat(heights, shape[axis_at] // parts).reshape([-1 if axis == axis_at else 1 for axis in range(len(shape))])
    return gain


def centred(rng, dims, width, reach, pieces=(), held_as=jnp.bfloat16):
    gain = levels(rng, dims, pieces, -0.22, 0.18) if pieces else 1.0
    array = jax.random.normal(rng, dims, jnp.float32) * width * gain
    return jnp.minimum(jnp.maximum(array, -reach), reach).astype(held_as)


def setup_inputs(seed: int = 0) -> dict:
    seeds = jax.random.split(jax.random.key(seed), 13)
    return {
        "tokens": centred(seeds[0], (EXAMPLES, SEQ, D), 1.0, 6.0, ((1, 4),)),
        "out_grad": centred(seeds[1], (EXAMPLES, SEQ, D), 1.0, 6.0, ((1, 4), (2, 64))),
        "gate_weight": centred(seeds[2], (D, FF), D ** -0.5, 0.09375, ((1, 64),)),
        "up_weight": centred(seeds[3], (D, FF), D ** -0.5, 0.09375, ((1, 64),)),
        "down_weight": centred(seeds[4], (FF, D), FF ** -0.5, 0.0625, ((0, 64),)),
        "proj_gate_in": centred(seeds[5], (D, RANK), D ** -0.5, 0.09375),
        "proj_gate_out": centred(seeds[6], (FF, RANK), FF ** -0.5, 0.0625, ((0, 64),)),
        "proj_up_in": centred(seeds[7], (D, RANK), D ** -0.5, 0.09375),
        "proj_up_out": centred(seeds[8], (FF, RANK), FF ** -0.5, 0.0625, ((0, 64),)),
        "proj_down_in": centred(seeds[9], (FF, RANK), FF ** -0.5, 0.0625, ((0, 64),)),
        "proj_down_out": centred(seeds[10], (D, RANK), D ** -0.5, 0.09375),
        "lengths": draw_lengths(jax.random.fold_in(seeds[12], 71), 0),
    }


def project_pair(left_side, right_side, valid_mask):
    weighted = left_side * valid_mask[:, None]
    product = jnp.dot(weighted.T, right_side, precision=lax.Precision.HIGHEST, preferred_element_type=jnp.float32)
    return product.reshape(RANK * RANK)


def reference(tokens, out_grad, gate_weight, up_weight, down_weight, proj_gate_in, proj_gate_out, proj_up_in, proj_up_out, proj_down_in, proj_down_out, lengths):
    scale_factor = float(SEQ) ** -0.5

    def one_example(inputs_one):
        example_tokens, example_grad, example_length = inputs_one
        gate_value = jnp.dot(example_tokens, gate_weight, preferred_element_type=jnp.float32)
        up_value = jnp.dot(example_tokens, up_weight, preferred_element_type=jnp.float32)
        sigmoid_gate = jax.nn.sigmoid(gate_value)
        hidden = (gate_value * sigmoid_gate * up_value).astype(jnp.bfloat16)
        hidden_grad = jnp.dot(example_grad, down_weight.T, preferred_element_type=jnp.float32)
        gate_grad = (hidden_grad * up_value * sigmoid_gate * (1.0 + gate_value * (1.0 - sigmoid_gate))).astype(jnp.bfloat16)
        up_grad = (hidden_grad * gate_value * sigmoid_gate).astype(jnp.bfloat16)
        left_gate = jnp.dot(gate_grad, proj_gate_out, preferred_element_type=jnp.float32)
        right_gate = jnp.dot(example_tokens, proj_gate_in, preferred_element_type=jnp.float32)
        left_up = jnp.dot(up_grad, proj_up_out, preferred_element_type=jnp.float32)
        right_up = jnp.dot(example_tokens, proj_up_in, preferred_element_type=jnp.float32)
        left_down = jnp.dot(example_grad, proj_down_out, preferred_element_type=jnp.float32)
        right_down = jnp.dot(hidden, proj_down_in, preferred_element_type=jnp.float32)
        valid_mask = (jnp.arange(SEQ, dtype=jnp.int32) < example_length).astype(jnp.float32)
        stacked = jnp.stack([project_pair(left_gate, right_gate, valid_mask), project_pair(left_up, right_up, valid_mask), project_pair(left_down, right_down, valid_mask)])
        return stacked * scale_factor

    return lax.map(one_example, (tokens, out_grad, lengths))
```

```python
import jax
import jax.numpy as jnp
from jax import lax
from jax.sharding import Mesh, PartitionSpec as P

SEQ_PARTS = (2, 2)
FSDP_PARTS = (4, 8, 2)
NX, NZ, NY = FSDP_PARTS


def shifted(count, step):
    return [(i, (i + step) % count) for i in range(count)]


def dot32(a, b, dims, precision=None):
    return lax.dot_general(a, b, (dims, ((), ())), preferred_element_type=jnp.float32, precision=precision)


def ring_x(own):
    half = own.shape[0] // 2
    before = lax.ppermute(own, "x", shifted(NX, 1))
    after = lax.ppermute(own, "x", shifted(NX, -1))
    first = lax.ppermute(before[:half], "x", shifted(NX, 1))
    second = lax.ppermute(after[half:], "x", shifted(NX, -1))
    return [own, before, jnp.concatenate([first, second], axis=0), after]


def ring_z(own):
    up, down = [own], [own]
    for _ in range(NZ // 2 - 1):
        up.append(lax.ppermute(up[-1], "z", shifted(NZ, -1)))
        down.append(lax.ppermute(down[-1], "z", shifted(NZ, 1)))
    far = jnp.concatenate(
        [
            lax.ppermute(up[-1][:1], "z", shifted(NZ, -1)),
            lax.ppermute(down[-1][1:], "z", shifted(NZ, 1)),
        ],
        axis=0,
    )
    return up + [far] + down[:0:-1]


def sum_everywhere(partial):
    seq_count = SEQ_PARTS[0] * SEQ_PARTS[1]
    width = partial.shape[1] // (seq_count * NX)
    pieces = partial.reshape(6, seq_count * NX, width).transpose(1, 0, 2)
    pieces = lax.all_to_all(pieces, ("sy", "sc", "x"), 0, 0, tiled=True)
    own = jnp.sum(pieces, axis=0)
    spread = jnp.broadcast_to(own[None], (NZ * NY,) + own.shape)
    own = jnp.sum(lax.all_to_all(spread, ("z", "yh"), 0, 0, tiled=True), axis=0)
    spread = jnp.broadcast_to(own[None], (NX,) + own.shape)
    blocks = lax.all_to_all(spread, "x", 0, 0, tiled=True)
    return blocks.transpose(1, 0, 2).reshape(6, NX * width)


def shards(
    tokens,
    out_grad,
    gate_weight,
    up_weight,
    down_weight,
    proj_gate_in,
    proj_gate_out,
    proj_up_in,
    proj_up_out,
    proj_down_in,
    proj_down_out,
    lengths,
):
    examples, seq_dev, model_width = tokens.shape
    row_count = examples * seq_dev
    rank = proj_gate_in.shape[1]
    hidden = gate_weight.shape[1]
    x_at, z_at, y_at = lax.axis_index("x"), lax.axis_index("z"), lax.axis_index("yh")
    seq_index = lax.axis_index("sy") * SEQ_PARTS[1] + lax.axis_index("sc")
    scale_factor = float(seq_dev * SEQ_PARTS[0] * SEQ_PARTS[1]) ** (-0.5)
    class_width = model_width // NX
    block_width = class_width // NZ

    own_grad = out_grad.transpose(0, 2, 1)
    other_grad = lax.ppermute(own_grad, "yh", shifted(NY, 1))
    first_y = y_at == 0
    pair = jnp.concatenate(
        [jnp.where(first_y, own_grad, other_grad), jnp.where(first_y, other_grad, own_grad)], axis=1
    )
    blocks = ring_z(pair)

    proj_out = jnp.concatenate([proj_gate_out, proj_up_out], axis=1)
    weight_packs = []
    for step in range(NX):
        start = lax.rem(x_at + step, NX) * class_width
        piece = lax.dynamic_slice_in_dim(down_weight, start, class_width, axis=1)
        piece = jnp.concatenate([piece, proj_out], axis=1)
        weight_packs.append(piece if step == 0 else lax.ppermute(piece, "x", shifted(NX, step)))

    flat_tokens = tokens.reshape(row_count, model_width)
    gate_value = dot32(gate_weight, flat_tokens, ((0,), (1,)))
    up_value = dot32(up_weight, flat_tokens, ((0,), (1,)))
    sigmoid_gate = jax.nn.sigmoid(gate_value)
    silu = gate_value * sigmoid_gate
    factor_gate = (up_value * sigmoid_gate * (1.0 + gate_value * (1.0 - sigmoid_gate))).astype(jnp.bfloat16)
    factor_up = silu.astype(jnp.bfloat16)
    hidden_value = (silu * up_value).astype(jnp.bfloat16)
    right_down = dot32(proj_down_in, hidden_value, ((0,), (0,))).astype(jnp.bfloat16)
    factors = ring_x(jnp.concatenate([factor_gate, factor_up, right_down], axis=0))

    positions = seq_index * seq_dev + jnp.arange(seq_dev, dtype=jnp.int32)
    valid = (positions[None, :] < lengths[:, None]).astype(jnp.float32) * scale_factor
    valid = valid.reshape(1, row_count)
    proj_in = jnp.concatenate([proj_gate_in, proj_up_in], axis=1)
    right_both = dot32(proj_in, flat_tokens, ((0,), (1,))) * valid
    right_down_sum = sum(piece[2 * hidden :].astype(jnp.float32) for piece in factors) * valid

    weight = jnp.concatenate([piece[:, :class_width] for piece in weight_packs], axis=0)
    down_out = lax.dynamic_slice_in_dim(proj_down_out, x_at * class_width, class_width, axis=0)
    weight = jnp.concatenate([weight, down_out.T], axis=0)
    twice = jnp.concatenate([weight, weight], axis=1)
    weight = lax.dynamic_slice_in_dim(twice, z_at * block_width, class_width, axis=1)
    grad = jnp.concatenate(blocks, axis=1)
    grad_total = lax.dot_general(weight, grad, (((1,), (1,)), ((), ())), preferred_element_type=jnp.float32)
    grad_total = grad_total.reshape(NX * hidden + rank, row_count)
    left_down = grad_total[NX * hidden :]
    grad_total = grad_total[: NX * hidden]

    def project(factor, proj):
        product = grad_total * factor.astype(jnp.float32)
        high = product.astype(jnp.bfloat16)
        low = (product - high.astype(jnp.float32)).astype(jnp.bfloat16)
        return dot32(proj, high, ((0,), (0,))) + dot32(proj, low, ((0,), (0,)))

    left_gate = project(
        jnp.concatenate([piece[:hidden] for piece in factors], axis=0),
        jnp.concatenate([piece[:, class_width : class_width + rank] for piece in weight_packs], axis=0),
    )
    left_up = project(
        jnp.concatenate([piece[hidden : 2 * hidden] for piece in factors], axis=0),
        jnp.concatenate([piece[:, class_width + rank :] for piece in weight_packs], axis=0),
    )
    left_side = jnp.stack([left_gate, left_up, left_down]).reshape(3, rank, examples, seq_dev)
    right_side = jnp.stack([right_both[:rank], right_both[rank:], right_down_sum])
    right_side = right_side.reshape(3, rank, examples, seq_dev)
    products = jnp.einsum("mies,mjes->emij", left_side, right_side, precision=lax.Precision.HIGHEST)
    total = sum_everywhere(products.reshape(examples * 3, rank * rank))
    return total.reshape(examples, 3, -1)


def solution(mesh):
    fine = Mesh(mesh.devices.reshape(SEQ_PARTS + FSDP_PARTS), ("sy", "sc", "x", "z", "yh"))
    seq, fsdp = ("sy", "sc"), ("x", "z", "yh")
    placed = (
        P(None, seq, None),
        P(None, seq, fsdp),
        P(None, fsdp),
        P(None, fsdp),
        P(fsdp, None),
        P(),
        P(fsdp, None),
        P(),
        P(fsdp, None),
        P(fsdp, None),
        P(),
        P(),
    )
    return jax.shard_map(
        shards, mesh=fine, in_specs=placed, out_specs=P(None, None, seq), check_vma=False
    )
```

```python
import jax
import jax.numpy as jnp
from jax import lax
from jax.experimental import pallas as pl
from jax.experimental.pallas import tpu as pltpu
from jax.sharding import Mesh, PartitionSpec as P

SEQ_PARTS = (2, 2)
FSDP_PARTS = (4, 8, 2)
NX, NZ, NY = FSDP_PARTS
MIB = 1024 * 1024
VMEM = pl.BlockSpec(memory_space=pltpu.VMEM)


def shifted(count, step):
    return [(i, (i + step) % count) for i in range(count)]


def dot32(a, b, dims, precision=None):
    return lax.dot_general(a, b, (dims, ((), ())), preferred_element_type=jnp.float32, precision=precision)


def pack_kernel(weight_ref, gate_ref, up_ref, *outs):
    width = weight_ref.shape[1] // NX
    rank = gate_ref.shape[0]
    x_at = lax.axis_index("x")
    for step, out in enumerate(outs, 1):
        start = pl.multiple_of(lax.rem(x_at + step, NX) * width, width)
        out[:, :width] = weight_ref[:, pl.ds(start, width)]
        out[:rank, width:] = gate_ref[...]
        out[rank:, width:] = up_ref[...]


def pack_weights(down_weight, gate_out, up_out):
    hidden, width = down_weight.shape
    shape = jax.ShapeDtypeStruct((hidden, width // NX + hidden), jnp.bfloat16)
    return pl.pallas_call(
        pack_kernel,
        out_shape=[shape] * (NX - 1),
        in_specs=[VMEM] * 3,
        out_specs=[VMEM] * (NX - 1),
        compiler_params=pltpu.CompilerParams(vmem_limit_bytes=16 * MIB),
        name="pack_weights",
    )(down_weight, gate_out, up_out)


def token_kernel(tile, seq_dev, scale, lengths_ref, tokens_ref, gate_ref, up_ref, gate_in_ref, up_in_ref, down_in_ref, factors_ref, right_ref):
    hidden = gate_ref.shape[1]
    rank = gate_in_ref.shape[0]
    step = pl.program_id(0)
    tokens = tokens_ref[...]
    gate = jnp.dot(tokens, gate_ref[...], preferred_element_type=jnp.float32)
    up = jnp.dot(tokens, up_ref[...], preferred_element_type=jnp.float32)
    sigmoid = 1.0 / (1.0 + jnp.exp(-gate))
    silu = gate * sigmoid
    factor_gate = up * sigmoid * (1.0 + gate * (1.0 - sigmoid))
    hidden_value = (silu * up).astype(jnp.bfloat16)
    factors_ref[:hidden, :] = factor_gate.T.astype(jnp.bfloat16)
    factors_ref[hidden : 2 * hidden, :] = silu.T.astype(jnp.bfloat16)

    per_example = seq_dev // tile
    seq_index = lax.axis_index("sy") * SEQ_PARTS[1] + lax.axis_index("sc")
    first = seq_index * seq_dev + lax.rem(step, per_example) * tile
    limit = lengths_ref[step // per_example]
    columns = first + lax.broadcasted_iota(jnp.int32, (rank, tile), 1)
    right_down = dot32(down_in_ref[...], hidden_value, ((1,), (1,)))
    right_down = jnp.where(columns < limit, right_down * scale, 0.0)
    factors_ref[2 * hidden :, :] = right_down.astype(jnp.bfloat16)
    rows = first + lax.broadcasted_iota(jnp.int32, (tile, rank), 0)
    valid = rows < limit
    right_gate = dot32(tokens, gate_in_ref[...], ((1,), (1,)))
    right_up = dot32(tokens, up_in_ref[...], ((1,), (1,)))
    right_ref[:, :rank] = jnp.where(valid, right_gate * scale, 0.0)
    right_ref[:, rank:] = jnp.where(valid, right_up * scale, 0.0)


def token_stage(tokens, gate_weight, up_weight, gate_in, up_in, down_in, lengths, seq_dev, scale):
    rows, width = tokens.shape
    hidden = gate_weight.shape[1]
    rank = gate_in.shape[0]
    tile = 256
    return pl.pallas_call(
        lambda *refs: token_kernel(tile, seq_dev, scale, *refs),
        grid=(rows // tile,),
        out_shape=[
            jax.ShapeDtypeStruct((2 * hidden + rank, rows), jnp.bfloat16),
            jax.ShapeDtypeStruct((rows, 2 * rank), jnp.float32),
        ],
        in_specs=[
            pl.BlockSpec(memory_space=pltpu.SMEM),
            pl.BlockSpec((tile, width), lambda i: (i, 0)),
            VMEM,
            VMEM,
            VMEM,
            VMEM,
            VMEM,
        ],
        out_specs=[
            pl.BlockSpec((2 * hidden + rank, tile), lambda i: (0, i)),
            pl.BlockSpec((tile, 2 * rank), lambda i: (i, 0)),
        ],
        compiler_params=pltpu.CompilerParams(vmem_limit_bytes=40 * MIB),
        cost_estimate=pl.CostEstimate(flops=2 * rows * width * 384, bytes_accessed=12 * MIB, transcendentals=rows * hidden),
        name="token_stage",
    )(lengths, tokens, gate_weight, up_weight, gate_in, up_in, down_in)


def tail_kernel(weight_ref, gate_out_ref, up_out_ref, down_out_ref, right_ref, *refs):
    packs, factors, own, other = refs[:3], refs[3:7], refs[7:15], refs[15:23]
    out_ref, weights, projs, grads = refs[23:]
    hidden, model_width = weight_ref.shape
    rank = gate_out_ref.shape[0]
    width = model_width // NX
    examples, piece, seq_dev = own[0].shape
    x_at, z_at, y_at = lax.axis_index("x"), lax.axis_index("z"), lax.axis_index("yh")

    start = pl.multiple_of(x_at * width, width)
    weights[:hidden, :] = weight_ref[:, pl.ds(start, width)]
    projs[:rank, :hidden] = gate_out_ref[...]
    projs[rank:, :hidden] = up_out_ref[...]
    for step, pack in enumerate(packs, 1):
        weights[step * hidden : (step + 1) * hidden, :] = pack[:, :width]
        projs[:, step * hidden : (step + 1) * hidden] = pack[:, width:]
    weights[NX * hidden :, :] = down_out_ref[:, pl.ds(start, width)]
    for example in range(examples):
        for step in range(NZ):
            block = lax.rem(z_at + step, NZ) * (NY * piece)
            grads[pl.ds(pl.multiple_of(block + y_at * piece, piece), piece), :] = own[step][example]
            grads[pl.ds(pl.multiple_of(block + (1 - y_at) * piece, piece), piece), :] = other[step][example]
        columns = slice(example * seq_dev, (example + 1) * seq_dev)
        total = jnp.dot(weights[...], grads[...], preferred_element_type=jnp.float32)
        left = []
        for kind in range(2):
            proj = projs[kind * rank : (kind + 1) * rank, :]
            factor = jnp.concatenate(
                [part[kind * hidden : (kind + 1) * hidden, columns] for part in factors], axis=0
            )
            product = total[: NX * hidden] * factor.astype(jnp.float32)
            high = product.astype(jnp.bfloat16)
            low = (product - high.astype(jnp.float32)).astype(jnp.bfloat16)
            left.append(
                jnp.dot(proj, high, preferred_element_type=jnp.float32)
                + jnp.dot(proj, low, preferred_element_type=jnp.float32)
            )
        both = jnp.dot(
            jnp.concatenate(left, axis=0),
            right_ref[columns, :],
            precision=lax.Precision.HIGHEST,
            preferred_element_type=jnp.float32,
        )
        right_down = factors[0][2 * hidden :, columns].astype(jnp.float32)
        for part in factors[1:]:
            right_down = right_down + part[2 * hidden :, columns].astype(jnp.float32)
        out_ref[3 * example] = both[:rank, :rank]
        out_ref[3 * example + 1] = both[rank:, rank:]
        out_ref[3 * example + 2] = dot32(
            total[NX * hidden :], right_down, ((1,), (1,)), precision=lax.Precision.HIGHEST
        )


def tail_stage(down_weight, gate_out, up_out, down_out, right, packs, factors, own, other):
    hidden, model_width = down_weight.shape
    rank = gate_out.shape[0]
    examples, piece, seq_dev = own[0].shape
    width = model_width // NX
    operands = [down_weight, gate_out, up_out, down_out, right, *packs, *factors, *own, *other]
    return pl.pallas_call(
        tail_kernel,
        out_shape=jax.ShapeDtypeStruct((examples * 3, rank, rank), jnp.float32),
        in_specs=[VMEM] * len(operands),
        out_specs=VMEM,
        scratch_shapes=[
            pltpu.VMEM((NX * hidden + rank, width), jnp.bfloat16),
            pltpu.VMEM((2 * rank, NX * hidden), jnp.bfloat16),
            pltpu.VMEM((width, seq_dev), jnp.bfloat16),
        ],
        compiler_params=pltpu.CompilerParams(vmem_limit_bytes=40 * MIB),
        cost_estimate=pl.CostEstimate(flops=4 * 10**9, bytes_accessed=8 * MIB, transcendentals=0),
        name="tail_stage",
    )(*operands)


def ring_z(own, far_step):
    up, down = [own], [own]
    for _ in range(NZ // 2 - 1):
        up.append(lax.ppermute(up[-1], "z", shifted(NZ, -1)))
        down.append(lax.ppermute(down[-1], "z", shifted(NZ, 1)))
    last = up[-1] if far_step < 0 else down[-1]
    return up + [lax.ppermute(last, "z", shifted(NZ, far_step))] + down[:0:-1]


def sum_everywhere(partial):
    seq_count = SEQ_PARTS[0] * SEQ_PARTS[1]
    width = partial.shape[1] // (seq_count * NX)
    pieces = partial.reshape(6, seq_count * NX, width).transpose(1, 0, 2)
    pieces = lax.all_to_all(pieces, ("sy", "sc", "x"), 0, 0, tiled=True)
    own = jnp.sum(pieces, axis=0)
    spread = jnp.broadcast_to(own[None], (NZ * NY,) + own.shape)
    own = jnp.sum(lax.all_to_all(spread, ("z", "yh"), 0, 0, tiled=True), axis=0)
    spread = jnp.broadcast_to(own[None], (NX,) + own.shape)
    blocks = lax.all_to_all(spread, "x", 0, 0, tiled=True)
    return blocks.transpose(1, 0, 2).reshape(6, NX * width)


def shards(
    tokens,
    out_grad,
    gate_weight,
    up_weight,
    down_weight,
    proj_gate_in,
    proj_gate_out,
    proj_up_in,
    proj_up_out,
    proj_down_in,
    proj_down_out,
    lengths,
):
    examples, seq_dev, model_width = tokens.shape
    scale = float(seq_dev * SEQ_PARTS[0] * SEQ_PARTS[1]) ** (-0.5)
    gate_out, up_out = proj_gate_out.T, proj_up_out.T

    own_grad = out_grad.transpose(0, 2, 1)
    other_grad = lax.ppermute(own_grad, "yh", shifted(NY, 1))
    own = ring_z(own_grad, -1)
    other = ring_z(other_grad, 1)

    sent = pack_weights(down_weight, gate_out, up_out)
    packs = [lax.ppermute(piece, "x", shifted(NX, step)) for step, piece in enumerate(sent, 1)]

    flat_tokens = tokens.reshape(examples * seq_dev, model_width)
    factors, right = token_stage(
        flat_tokens, gate_weight, up_weight, proj_gate_in.T, proj_up_in.T, proj_down_in.T, lengths, seq_dev, scale
    )
    factors = [factors] + [lax.ppermute(factors, "x", shifted(NX, step)) for step in range(1, NX)]

    products = tail_stage(
        down_weight, gate_out, up_out, proj_down_out.T, right, packs, factors, own, other
    )
    total = sum_everywhere(products.reshape(examples * 3, -1))
    return total.reshape(examples, 3, -1)


def solution(mesh):
    fine = Mesh(mesh.devices.reshape(SEQ_PARTS + FSDP_PARTS), ("sy", "sc", "x", "z", "yh"))
    seq, fsdp = ("sy", "sc"), ("x", "z", "yh")
    placed = (
        P(None, seq, None),
        P(None, seq, fsdp),
        P(None, fsdp),
        P(None, fsdp),
        P(fsdp, None),
        P(),
        P(fsdp, None),
        P(),
        P(fsdp, None),
        P(fsdp, None),
        P(),
        P(),
    )
    return jax.shard_map(
        shards, mesh=fine, in_specs=placed, out_specs=P(None, None, seq), check_vma=False
    )
```

```python
import jax
import jax.numpy as jnp
from jax import lax
from jax.experimental import pallas as pl
from jax.experimental.pallas import tpu as pltpu
from jax.sharding import Mesh, PartitionSpec as P

SEQ_PARTS = (2, 2)
FSDP_PARTS = (4, 8, 2)
NX, NZ, NY = FSDP_PARTS
MIB = 1024 * 1024
VMEM = pl.BlockSpec(memory_space=pltpu.VMEM)
HBM = pl.BlockSpec(memory_space=pltpu.HBM)


def shifted(count, step):
    return [(i, (i + step) % count) for i in range(count)]


def dot32(a, b, dims, precision=None):
    return lax.dot_general(a, b, (dims, ((), ())), preferred_element_type=jnp.float32, precision=precision)


def pack_kernel(weight_hbm, gate_hbm, up_hbm, *refs):
    outs, sems = refs[: NX - 1], refs[NX - 1]
    width = weight_hbm.shape[1] // NX
    rank = gate_hbm.shape[0]
    x_at = lax.axis_index("x")
    copies = []
    for step, out in enumerate(outs, 1):
        start = pl.multiple_of(lax.rem(x_at + step, NX) * width, width)
        copies += [
            (weight_hbm.at[:, pl.ds(start, width)], out.at[:, pl.ds(0, width)]),
            (gate_hbm, out.at[pl.ds(0, rank), pl.ds(width, weight_hbm.shape[0])]),
            (up_hbm, out.at[pl.ds(rank, rank), pl.ds(width, weight_hbm.shape[0])]),
        ]
    copies = [pltpu.make_async_copy(a, b, sems.at[k]) for k, (a, b) in enumerate(copies)]
    for copy in copies:
        copy.start()
    for copy in copies:
        copy.wait()


def pack_weights(down_weight, gate_out, up_out):
    hidden, width = down_weight.shape
    shape = jax.ShapeDtypeStruct((hidden, width // NX + hidden), jnp.bfloat16)
    return pl.pallas_call(
        pack_kernel,
        out_shape=[shape] * (NX - 1),
        in_specs=[HBM] * 3,
        out_specs=[VMEM] * (NX - 1),
        scratch_shapes=[pltpu.SemaphoreType.DMA((3 * (NX - 1),))],
        compiler_params=pltpu.CompilerParams(vmem_limit_bytes=62 * MIB),
        cost_estimate=pl.CostEstimate(flops=0, bytes_accessed=2 * MIB, transcendentals=0),
        name="pack_weights",
    )(down_weight, gate_out, up_out)


def pair_kernel(own_ref, other_ref, after_ref, out_ref):
    piece = own_ref.shape[1]
    out_ref[:, :piece, :] = own_ref[...]
    out_ref[:, piece:, :] = other_ref[...]


def pair_up(own, other, after):
    examples, piece, seq_dev = own.shape
    return pl.pallas_call(
        pair_kernel,
        out_shape=jax.ShapeDtypeStruct((examples, NY * piece, seq_dev), own.dtype),
        in_specs=[VMEM, VMEM, HBM],
        out_specs=VMEM,
        compiler_params=pltpu.CompilerParams(vmem_limit_bytes=4 * MIB),
        name="pair_up",
    )(own, other, after)


def token_kernel(tile, seq_dev, scale, lengths_ref, tokens_hbm, gate_hbm, up_hbm, gate_in_hbm, up_in_hbm, down_in_hbm, after_ref, factors_ref, right_ref, tokens_ref, weight_ref, in_ref, down_in_ref, sems):
    model_width, hidden = gate_hbm.shape
    rank = gate_in_hbm.shape[0]
    tiles = tokens_hbm.shape[0] // tile
    pairs = [
        (gate_hbm, weight_ref.at[:, pl.ds(0, hidden)]),
        (up_hbm, weight_ref.at[:, pl.ds(hidden, hidden)]),
        (down_in_hbm, down_in_ref),
        (tokens_hbm.at[pl.ds(0, tile)], tokens_ref.at[pl.ds(0, tile)]),
        (gate_in_hbm, in_ref.at[pl.ds(0, rank)]),
        (up_in_hbm, in_ref.at[pl.ds(rank, rank)]),
    ]
    pairs += [
        (tokens_hbm.at[pl.ds(k * tile, tile)], tokens_ref.at[pl.ds(k * tile, tile)]) for k in range(1, tiles)
    ]
    copies = [pltpu.make_async_copy(a, b, sems.at[k]) for k, (a, b) in enumerate(pairs)]
    for copy in copies:
        copy.start()
    for copy in copies[:4]:
        copy.wait()
    per_example = seq_dev // tile
    seq_index = lax.axis_index("sy") * SEQ_PARTS[1] + lax.axis_index("sc")
    for step in range(tiles):
        if step > 0:
            copies[5 + step].wait()
        span = slice(step * tile, (step + 1) * tile)
        tokens = tokens_ref[span, :]
        values = jnp.dot(tokens, weight_ref[...], preferred_element_type=jnp.float32)
        gate, up = values[:, :hidden], values[:, hidden:]
        sigmoid = 1.0 / (1.0 + jnp.exp(-gate))
        silu = gate * sigmoid
        factor_gate = up * sigmoid * (1.0 + gate * (1.0 - sigmoid))
        hidden_value = (silu * up).astype(jnp.bfloat16)
        factors_ref[:hidden, span] = factor_gate.T.astype(jnp.bfloat16)
        factors_ref[hidden : 2 * hidden, span] = silu.T.astype(jnp.bfloat16)

        first = seq_index * seq_dev + (step % per_example) * tile
        limit = lengths_ref[step // per_example]
        columns = first + lax.broadcasted_iota(jnp.int32, (rank, tile), 1)
        right_down = dot32(down_in_ref[...], hidden_value, ((1,), (1,)))
        right_down = jnp.where(columns < limit, right_down * scale, 0.0)
        factors_ref[2 * hidden :, span] = right_down.astype(jnp.bfloat16)
        if step == 0:
            copies[4].wait()
            copies[5].wait()
        rows = first + lax.broadcasted_iota(jnp.int32, (tile, 2 * rank), 0)
        right = dot32(tokens, in_ref[...], ((1,), (1,)))
        right_ref[span, :] = jnp.where(rows < limit, right * scale, 0.0)


def token_stage(tokens, gate_weight, up_weight, gate_in, up_in, down_in, lengths, after, seq_dev, scale):
    rows, width = tokens.shape
    hidden = gate_weight.shape[1]
    rank = gate_in.shape[0]
    tile = 256
    return pl.pallas_call(
        lambda *refs: token_kernel(tile, seq_dev, scale, *refs),
        out_shape=[
            jax.ShapeDtypeStruct((2 * hidden + rank, rows), jnp.bfloat16),
            jax.ShapeDtypeStruct((rows, 2 * rank), jnp.float32),
        ],
        in_specs=[pl.BlockSpec(memory_space=pltpu.SMEM)] + [HBM] * 7,
        out_specs=[VMEM, VMEM],
        scratch_shapes=[
            pltpu.VMEM((rows, width), jnp.bfloat16),
            pltpu.VMEM((width, 2 * hidden), jnp.bfloat16),
            pltpu.VMEM((2 * rank, width), jnp.bfloat16),
            pltpu.VMEM((rank, hidden), jnp.bfloat16),
            pltpu.SemaphoreType.DMA((5 + rows // tile,)),
        ],
        compiler_params=pltpu.CompilerParams(vmem_limit_bytes=62 * MIB),
        cost_estimate=pl.CostEstimate(
            flops=2 * rows * width * 512, bytes_accessed=16 * MIB, transcendentals=rows * hidden
        ),
        name="token_stage",
    )(lengths, tokens, gate_weight, up_weight, gate_in, up_in, down_in, after)


def tail_kernel(weight_ref, gate_out_ref, up_out_ref, down_out_ref, right_ref, *refs):
    packs, factors, blocks = refs[:3], refs[3:7], refs[7:15]
    out_ref, weights, projs, grads = refs[15:]
    hidden, model_width = weight_ref.shape
    rank = gate_out_ref.shape[0]
    width = model_width // NX
    examples, piece, seq_dev = blocks[0].shape
    piece = piece // NY
    x_at, z_at, y_at = lax.axis_index("x"), lax.axis_index("z"), lax.axis_index("yh")

    start = pl.multiple_of(x_at * width, width)
    weights[:hidden, :] = weight_ref[:, pl.ds(start, width)]
    projs[:rank, :hidden] = gate_out_ref[...]
    projs[rank:, :hidden] = up_out_ref[...]
    for step, pack in enumerate(packs, 1):
        weights[step * hidden : (step + 1) * hidden, :] = pack[:, :width]
        projs[:, step * hidden : (step + 1) * hidden] = pack[:, width:]
    weights[NX * hidden :, :] = down_out_ref[:, pl.ds(start, width)]
    for example in range(examples):
        for step in range(NZ):
            block = lax.rem(z_at + step, NZ) * (NY * piece)
            grads[pl.ds(pl.multiple_of(block + y_at * piece, piece), piece), :] = blocks[step][example, :piece]
            grads[pl.ds(pl.multiple_of(block + (1 - y_at) * piece, piece), piece), :] = blocks[step][example, piece:]
        columns = slice(example * seq_dev, (example + 1) * seq_dev)
        total = jnp.dot(weights[...], grads[...], preferred_element_type=jnp.float32)
        left = []
        for kind in range(2):
            proj = projs[kind * rank : (kind + 1) * rank, :]
            factor = jnp.concatenate(
                [part[kind * hidden : (kind + 1) * hidden, columns] for part in factors], axis=0
            )
            product = total[: NX * hidden] * factor.astype(jnp.float32)
            high = product.astype(jnp.bfloat16)
            low = (product - high.astype(jnp.float32)).astype(jnp.bfloat16)
            left.append(
                jnp.dot(proj, high, preferred_element_type=jnp.float32)
                + jnp.dot(proj, low, preferred_element_type=jnp.float32)
            )
        both = jnp.dot(
            jnp.concatenate(left, axis=0),
            right_ref[columns, :],
            precision=lax.Precision.HIGHEST,
            preferred_element_type=jnp.float32,
        )
        right_down = factors[0][2 * hidden :, columns].astype(jnp.float32)
        for part in factors[1:]:
            right_down = right_down + part[2 * hidden :, columns].astype(jnp.float32)
        out_ref[3 * example] = both[:rank, :rank]
        out_ref[3 * example + 1] = both[rank:, rank:]
        out_ref[3 * example + 2] = dot32(
            total[NX * hidden :], right_down, ((1,), (1,)), precision=lax.Precision.HIGHEST
        )


def tail_stage(down_weight, gate_out, up_out, down_out, right, packs, factors, blocks):
    hidden, model_width = down_weight.shape
    rank = gate_out.shape[0]
    examples, piece, seq_dev = blocks[0].shape
    width = model_width // NX
    operands = [down_weight, gate_out, up_out, down_out, right, *packs, *factors, *blocks]
    return pl.pallas_call(
        tail_kernel,
        out_shape=jax.ShapeDtypeStruct((examples * 3, rank, rank), jnp.float32),
        in_specs=[VMEM] * len(operands),
        out_specs=VMEM,
        scratch_shapes=[
            pltpu.VMEM((NX * hidden + rank, width), jnp.bfloat16),
            pltpu.VMEM((2 * rank, NX * hidden), jnp.bfloat16),
            pltpu.VMEM((width, seq_dev), jnp.bfloat16),
        ],
        compiler_params=pltpu.CompilerParams(vmem_limit_bytes=40 * MIB),
        cost_estimate=pl.CostEstimate(flops=4 * 10**9, bytes_accessed=8 * MIB, transcendentals=0),
        name="tail_stage",
    )(*operands)


def ring_z(own):
    up, down = [own], [own]
    for _ in range(NZ // 2 - 1):
        up.append(lax.ppermute(up[-1], "z", shifted(NZ, -1)))
        down.append(lax.ppermute(down[-1], "z", shifted(NZ, 1)))
    return up + [lax.ppermute(up[-1], "z", shifted(NZ, -1))] + down[:0:-1]


def sum_everywhere(partial):
    seq_count = SEQ_PARTS[0] * SEQ_PARTS[1]
    width = partial.shape[1] // (seq_count * NX)
    pieces = partial.reshape(6, seq_count * NX, width).transpose(1, 0, 2)
    pieces = lax.all_to_all(pieces, ("sy", "sc", "x"), 0, 0, tiled=True)
    own = jnp.sum(pieces, axis=0)
    spread = jnp.broadcast_to(own[None], (NZ * NY,) + own.shape)
    own = jnp.sum(lax.all_to_all(spread, ("z", "yh"), 0, 0, tiled=True), axis=0)
    spread = jnp.broadcast_to(own[None], (NX,) + own.shape)
    blocks = lax.all_to_all(spread, "x", 0, 0, tiled=True)
    return blocks.transpose(1, 0, 2).reshape(6, NX * width)


def shards(
    tokens,
    out_grad,
    gate_weight,
    up_weight,
    down_weight,
    proj_gate_in,
    proj_gate_out,
    proj_up_in,
    proj_up_out,
    proj_down_in,
    proj_down_out,
    lengths,
):
    examples, seq_dev, model_width = tokens.shape
    scale = float(seq_dev * SEQ_PARTS[0] * SEQ_PARTS[1]) ** (-0.5)
    gate_out, up_out = proj_gate_out.T, proj_up_out.T

    own_grad = out_grad.transpose(0, 2, 1)
    other_grad = lax.ppermute(own_grad, "yh", shifted(NY, 1))
    sent = pack_weights(down_weight, gate_out, up_out)
    packs = [lax.ppermute(piece, "x", shifted(NX, step)) for step, piece in enumerate(sent, 1)]
    pair = pair_up(own_grad, other_grad, sent[0])
    blocks = ring_z(pair)

    flat_tokens = tokens.reshape(examples * seq_dev, model_width)
    factors, right = token_stage(
        flat_tokens,
        gate_weight,
        up_weight,
        proj_gate_in.T,
        proj_up_in.T,
        proj_down_in.T,
        lengths,
        pair,
        seq_dev,
        scale,
    )
    factors = [factors] + [lax.ppermute(factors, "x", shifted(NX, step)) for step in range(1, NX)]

    products = tail_stage(
        down_weight, gate_out, up_out, proj_down_out.T, right, packs, factors, blocks
    )
    total = sum_everywhere(products.reshape(examples * 3, -1))
    return total.reshape(examples, 3, -1)


def solution(mesh):
    fine = Mesh(mesh.devices.reshape(SEQ_PARTS + FSDP_PARTS), ("sy", "sc", "x", "z", "yh"))
    seq, fsdp = ("sy", "sc"), ("x", "z", "yh")
    placed = (
        P(None, seq, None),
        P(None, seq, fsdp),
        P(None, fsdp),
        P(None, fsdp),
        P(fsdp, None),
        P(),
        P(fsdp, None),
        P(),
        P(fsdp, None),
        P(fsdp, None),
        P(),
        P(),
    )
    return jax.shard_map(
        shards, mesh=fine, in_specs=placed, out_specs=P(None, None, seq), check_vma=False
    )
```

```python
import jax
import jax.numpy as jnp
from jax import lax
from jax.experimental import pallas as pl
from jax.experimental.pallas import tpu as pltpu
from jax.sharding import Mesh, PartitionSpec as P

SEQ_PARTS = (2, 2)
FSDP_PARTS = (4, 8, 2)
NX, NZ, NY = FSDP_PARTS
FOLD = 16
MIB = 1024 * 1024
VMEM = pl.BlockSpec(memory_space=pltpu.VMEM)
HBM = pl.BlockSpec(memory_space=pltpu.HBM)


def shifted(count, step):
    return [(i, (i + step) % count) for i in range(count)]


def dot32(a, b, dims, precision=None):
    return lax.dot_general(a, b, (dims, ((), ())), preferred_element_type=jnp.float32, precision=precision)


def pair_kernel(own_ref, other_ref, after_ref, out_ref):
    piece = own_ref.shape[1]
    out_ref[:, :piece, :] = own_ref[...]
    out_ref[:, piece:, :] = other_ref[...]


def pair_up(own, other, after):
    examples, piece, seq_dev = own.shape
    return pl.pallas_call(
        pair_kernel,
        out_shape=jax.ShapeDtypeStruct((examples, NY * piece, seq_dev), own.dtype),
        in_specs=[VMEM, VMEM, HBM],
        out_specs=VMEM,
        compiler_params=pltpu.CompilerParams(vmem_limit_bytes=4 * MIB),
        name="pair_up",
    )(own, other, after)


def token_kernel(chunk, scale, lengths_ref, tokens_hbm, gate_hbm, up_hbm, gate_in_hbm, up_in_hbm, down_in_hbm, down_hbm, gate_out_hbm, up_out_hbm, *refs):
    messages, (right_ref, done_ref) = refs[: NX - 1], refs[NX - 1 : NX + 1]
    tokens_ref, weight_ref, in_ref, down_in_ref, out_ref, total_ref, sems = refs[NX + 1 :]
    rows, model_width = tokens_hbm.shape
    hidden = gate_hbm.shape[1]
    rank = gate_in_hbm.shape[0]
    examples = lengths_ref.shape[0]
    seq_dev = rows // examples
    groups, count = [], 0
    for start in range(0, model_width, chunk):
        part = pl.ds(start, chunk)
        pairs = [
            (tokens_hbm.at[:, part], tokens_ref.at[:, part]),
            (gate_hbm.at[part], weight_ref.at[part, pl.ds(0, hidden)]),
            (up_hbm.at[part], weight_ref.at[part, pl.ds(hidden, hidden)]),
            (gate_in_hbm.at[:, part], in_ref.at[pl.ds(0, rank), part]),
            (up_in_hbm.at[:, part], in_ref.at[pl.ds(rank, rank), part]),
        ]
        if start + chunk == model_width:
            pairs.append((down_in_hbm, down_in_ref))
        groups.append([pltpu.make_async_copy(a, b, sems.at[count + k]) for k, (a, b) in enumerate(pairs)])
        count += len(pairs)
        for copy in groups[-1]:
            copy.start()
    top = 2 * hidden + rank
    width = model_width // NX
    pairs = [(gate_out_hbm, out_ref.at[pl.ds(0, rank)]), (up_out_hbm, out_ref.at[pl.ds(rank, rank)])]
    for step, message in enumerate(messages, 1):
        start = pl.multiple_of(lax.rem(lax.axis_index("x") + step, NX) * width, width)
        pairs.append((down_hbm.at[:, pl.ds(start, width)], message.at[pl.ds(top, hidden)]))
    extra = [pltpu.make_async_copy(a, b, sems.at[count + k]) for k, (a, b) in enumerate(pairs)]
    for copy in extra:
        copy.start()
    for index, group in enumerate(groups):
        for copy in group:
            copy.wait()
        part = slice(index * chunk, (index + 1) * chunk)
        values = jnp.dot(tokens_ref[:, part], weight_ref[part, :], preferred_element_type=jnp.float32)
        right = dot32(tokens_ref[:, part], in_ref[:, part], ((1,), (1,)))
        if index == 0:
            total_ref[...] = values
            right_ref[...] = right
        else:
            total_ref[...] += values
            right_ref[...] += right

    done_ref[...] = jnp.zeros_like(done_ref)
    tile = min(256, seq_dev)
    seq_index = lax.axis_index("sy") * SEQ_PARTS[1] + lax.axis_index("sc")
    for step in range(rows // tile):
        span = slice(step * tile, (step + 1) * tile)
        gate, up = total_ref[span, :hidden], total_ref[span, hidden:]
        sigmoid = 1.0 / (1.0 + jnp.exp(-gate))
        silu = gate * sigmoid
        factor_gate = up * sigmoid * (1.0 + gate * (1.0 - sigmoid))
        hidden_value = (silu * up).astype(jnp.bfloat16)
        factor_gate = factor_gate.T.astype(jnp.bfloat16)
        factor_up = silu.T.astype(jnp.bfloat16)

        first = seq_index * seq_dev + step * tile % seq_dev
        limit = lengths_ref[step * tile // seq_dev]
        columns = first + lax.broadcasted_iota(jnp.int32, (rank, tile), 1)
        right_down = dot32(down_in_ref[...], hidden_value, ((1,), (1,)))
        right_down = jnp.where(columns < limit, right_down * scale, 0.0).astype(jnp.bfloat16)
        for message in messages:
            message[:hidden, span] = factor_gate
            message[hidden : 2 * hidden, span] = factor_up
            message[2 * hidden : top, span] = right_down
        rows_at = first + lax.broadcasted_iota(jnp.int32, (tile, 2 * rank), 0)
        right_ref[span, :] = jnp.where(rows_at < limit, right_ref[span, :] * scale, 0.0)
    for copy in extra:
        copy.wait()
    for message in messages:
        for block in range(2 * rank // FOLD):
            rows_of = slice(block * FOLD, (block + 1) * FOLD)
            message[top + hidden :, block * hidden : (block + 1) * hidden] = out_ref[rows_of, :]


def token_stage(tokens, gate_weight, up_weight, gate_in, up_in, down_in, down_weight, gate_out, up_out, lengths, scale):
    rows, width = tokens.shape
    hidden = gate_weight.shape[1]
    rank = gate_in.shape[0]
    chunk = 512
    return pl.pallas_call(
        lambda *refs: token_kernel(chunk, scale, *refs),
        out_shape=[
            *[jax.ShapeDtypeStruct((3 * hidden + rank + FOLD, rows), jnp.bfloat16)] * (NX - 1),
            jax.ShapeDtypeStruct((rows, 2 * rank), jnp.float32),
            jax.ShapeDtypeStruct((8, 128), jnp.float32),
        ],
        in_specs=[pl.BlockSpec(memory_space=pltpu.SMEM)] + [HBM] * 9,
        out_specs=[VMEM] * (NX + 1),
        scratch_shapes=[
            pltpu.VMEM((rows, width), jnp.bfloat16),
            pltpu.VMEM((width, 2 * hidden), jnp.bfloat16),
            pltpu.VMEM((2 * rank, width), jnp.bfloat16),
            pltpu.VMEM((rank, hidden), jnp.bfloat16),
            pltpu.VMEM((2 * rank, hidden), jnp.bfloat16),
            pltpu.VMEM((rows, 2 * hidden), jnp.float32),
            pltpu.SemaphoreType.DMA((5 * (width // chunk) + 2 + NX,)),
        ],
        compiler_params=pltpu.CompilerParams(vmem_limit_bytes=61 * MIB),
        cost_estimate=pl.CostEstimate(
            flops=2 * rows * width * 512, bytes_accessed=16 * MIB, transcendentals=rows * hidden
        ),
        name="token_stage",
    )(lengths, tokens, gate_weight, up_weight, gate_in, up_in, down_in, down_weight, gate_out, up_out)


def tail_kernel(weight_hbm, gate_out_ref, up_out_ref, down_out_hbm, right_ref, *refs):
    messages, blocks = refs[:NX], refs[NX : NX + NZ]
    out_ref, weights, projs, grads, total, sems = refs[NX + NZ :]
    hidden, model_width = weight_hbm.shape
    rank = gate_out_ref.shape[0]
    width = model_width // NX
    examples, both, seq_dev = blocks[0].shape
    piece = both // NY
    top = 2 * hidden + rank
    x_at, z_at, y_at = lax.axis_index("x"), lax.axis_index("z"), lax.axis_index("yh")

    start = pl.multiple_of(x_at * width, width)
    pairs = [
        (weight_hbm.at[:, pl.ds(start, width)], weights.at[pl.ds(0, hidden)]),
        (down_out_hbm.at[:, pl.ds(start, width)], weights.at[pl.ds(NX * hidden, rank)]),
    ]
    for step in range(1, NX):
        pairs.append((messages[step].at[pl.ds(top, hidden)], weights.at[pl.ds(step * hidden, hidden)]))
    for step, block in enumerate(blocks):
        base = lax.rem(z_at + step, NZ) * both
        for kind, y_of in enumerate((y_at, 1 - y_at)):
            rows = pl.ds(pl.multiple_of(base + y_of * piece, piece), piece)
            pairs.append((block.at[:, pl.ds(kind * piece, piece)], grads.at[:, rows]))
    copies = [pltpu.make_async_copy(a, b, sems.at[k]) for k, (a, b) in enumerate(pairs)]
    for copy in copies:
        copy.start()
    projs[:rank, :hidden] = gate_out_ref[...]
    projs[rank:, :hidden] = up_out_ref[...]
    for step in range(1, NX):
        columns = slice(step * hidden, (step + 1) * hidden)
        for block in range(2 * rank // FOLD):
            folded = messages[step][top + hidden :, block * hidden : (block + 1) * hidden]
            projs[block * FOLD : (block + 1) * FOLD, columns] = folded
    for copy in copies:
        copy.wait()
    for example in range(examples):
        total[example] = jnp.dot(weights[...], grads[example], preferred_element_type=jnp.float32)
    for example in range(examples):
        columns = slice(example * seq_dev, (example + 1) * seq_dev)
        left = []
        for kind in range(2):
            products = []
            for step in range(NX):
                factor = messages[step][kind * hidden : (kind + 1) * hidden, columns].astype(jnp.float32)
                products.append(total[example, step * hidden : (step + 1) * hidden] * factor)
            product = jnp.concatenate(products, axis=0)
            high = product.astype(jnp.bfloat16)
            low = (product - high.astype(jnp.float32)).astype(jnp.bfloat16)
            proj = projs[kind * rank : (kind + 1) * rank, :]
            left.append(
                jnp.dot(proj, high, preferred_element_type=jnp.float32)
                + jnp.dot(proj, low, preferred_element_type=jnp.float32)
            )
        sides = jnp.dot(
            jnp.concatenate(left, axis=0),
            right_ref[columns, :],
            precision=lax.Precision.HIGHEST,
            preferred_element_type=jnp.float32,
        )
        right_down = messages[0][2 * hidden : top, columns].astype(jnp.float32)
        for step in range(1, NX):
            right_down = right_down + messages[step][2 * hidden : top, columns].astype(jnp.float32)
        out_ref[3 * example] = sides[:rank, :rank]
        out_ref[3 * example + 1] = sides[rank:, rank:]
        out_ref[3 * example + 2] = dot32(
            total[example, NX * hidden :], right_down, ((1,), (1,)), precision=lax.Precision.HIGHEST
        )


def tail_stage(down_weight, gate_out, up_out, down_out, right, messages, blocks):
    hidden, model_width = down_weight.shape
    rank = gate_out.shape[0]
    examples, _, seq_dev = blocks[0].shape
    width = model_width // NX
    operands = [down_weight, gate_out, up_out, down_out, right, *messages, *blocks]
    return pl.pallas_call(
        tail_kernel,
        out_shape=jax.ShapeDtypeStruct((examples * 3, rank, rank), jnp.float32),
        in_specs=[HBM, VMEM, VMEM, HBM, VMEM] + [VMEM] * NX + [HBM] * NZ,
        out_specs=VMEM,
        scratch_shapes=[
            pltpu.VMEM((NX * hidden + rank, width), jnp.bfloat16),
            pltpu.VMEM((2 * rank, NX * hidden), jnp.bfloat16),
            pltpu.VMEM((examples, width, seq_dev), jnp.bfloat16),
            pltpu.VMEM((examples, NX * hidden + rank, seq_dev), jnp.float32),
            pltpu.SemaphoreType.DMA((1 + NX + NZ * NY,)),
        ],
        compiler_params=pltpu.CompilerParams(vmem_limit_bytes=16 * MIB),
        cost_estimate=pl.CostEstimate(flops=4 * 10**9, bytes_accessed=8 * MIB, transcendentals=0),
        name="tail_stage",
    )(*operands)


def ring_z(own):
    up, down = [own], [own]
    for _ in range(NZ // 2 - 1):
        up.append(lax.ppermute(up[-1], "z", shifted(NZ, -1)))
        down.append(lax.ppermute(down[-1], "z", shifted(NZ, 1)))
    return up + [lax.ppermute(up[-1], "z", shifted(NZ, -1))] + down[:0:-1]


def sum_everywhere(partial):
    count, size = partial.shape
    parts = SEQ_PARTS[0] * SEQ_PARTS[1] * NZ
    width = size // parts
    pieces = partial.reshape(count, parts, width).transpose(1, 0, 2)
    pieces = lax.all_to_all(pieces, ("sy", "sc", "z"), 0, 0, tiled=True)
    own = jnp.sum(pieces, axis=0)
    spread = jnp.broadcast_to(own[None], (NX * NZ * NY,) + own.shape)
    blocks = lax.all_to_all(spread, ("x", "z", "yh"), 0, 0, tiled=True)
    blocks = blocks.reshape(NX, NZ, NY, count, width).sum(axis=(0, 2))
    return blocks.transpose(1, 0, 2).reshape(count, NZ * width)


def shards(
    tokens,
    out_grad,
    gate_weight,
    up_weight,
    down_weight,
    proj_gate_in,
    proj_gate_out,
    proj_up_in,
    proj_up_out,
    proj_down_in,
    proj_down_out,
    lengths,
):
    examples, seq_dev, model_width = tokens.shape
    scale = float(seq_dev * SEQ_PARTS[0] * SEQ_PARTS[1]) ** (-0.5)
    gate_out, up_out = proj_gate_out.T, proj_up_out.T

    own_grad = out_grad.transpose(0, 2, 1)
    other_grad = lax.ppermute(own_grad, "yh", shifted(NY, 1))
    flat_tokens = tokens.reshape(examples * seq_dev, model_width)
    sent = token_stage(
        flat_tokens,
        gate_weight,
        up_weight,
        proj_gate_in.T,
        proj_up_in.T,
        proj_down_in.T,
        down_weight,
        gate_out,
        up_out,
        lengths,
        scale,
    )
    sent, (right, done) = sent[: NX - 1], sent[NX - 1 :]
    messages = [sent[0]] + [lax.ppermute(piece, "x", shifted(NX, step)) for step, piece in enumerate(sent, 1)]
    pair = pair_up(own_grad, other_grad, done)
    blocks = ring_z(pair)
    products = tail_stage(down_weight, gate_out, up_out, proj_down_out.T, right, messages, blocks)
    total = sum_everywhere(products.reshape(examples * 3, -1))
    return total.reshape(examples, 3, -1)


def solution(mesh):
    fine = Mesh(mesh.devices.reshape(SEQ_PARTS + FSDP_PARTS), ("sy", "sc", "x", "z", "yh"))
    seq, fsdp = ("sy", "sc"), ("x", "z", "yh")
    placed = (
        P(None, seq, None),
        P(None, seq, fsdp),
        P(None, fsdp),
        P(None, fsdp),
        P(fsdp, None),
        P(),
        P(fsdp, None),
        P(),
        P(fsdp, None),
        P(fsdp, None),
        P(),
        P(),
    )
    return jax.shard_map(
        shards, mesh=fine, in_specs=placed, out_specs=P(None, None, seq), check_vma=False
    )
```

```python
import jax
import jax.numpy as jnp
from jax import lax
from jax.experimental import pallas as pl
from jax.experimental.pallas import tpu as pltpu
from jax.sharding import Mesh, PartitionSpec as P

SEQ_PARTS = (2, 2)
FSDP_PARTS = (4, 8, 2)
NX, NZ, NY = FSDP_PARTS
FOLD = 16
MIB = 1024 * 1024
VMEM = pl.BlockSpec(memory_space=pltpu.VMEM)
HBM = pl.BlockSpec(memory_space=pltpu.HBM)


def shifted(count, step):
    return [(i, (i + step) % count) for i in range(count)]


def dot32(a, b, dims, precision=None):
    return lax.dot_general(a, b, (dims, ((), ())), preferred_element_type=jnp.float32, precision=precision)


def pair_kernel(own_ref, other_ref, after_ref, out_ref):
    piece = own_ref.shape[1]
    out_ref[:, :piece, :] = own_ref[...]
    out_ref[:, piece:, :] = other_ref[...]


def pair_up(own, other, after):
    examples, piece, seq_dev = own.shape
    return pl.pallas_call(
        pair_kernel,
        out_shape=jax.ShapeDtypeStruct((examples, NY * piece, seq_dev), own.dtype),
        in_specs=[VMEM, VMEM, HBM],
        out_specs=VMEM,
        compiler_params=pltpu.CompilerParams(vmem_limit_bytes=4 * MIB),
        name="pair_up",
    )(own, other, after)


def token_kernel(chunk, scale, lengths_ref, tokens_hbm, gate_hbm, up_hbm, gate_in_hbm, up_in_hbm, down_in_hbm, down_hbm, gate_out_hbm, up_out_hbm, *refs):
    messages, (right_ref, done_ref) = refs[: NX - 1], refs[NX - 1 : NX + 1]
    tokens_ref, weight_ref, in_ref, down_in_ref, out_ref, total_ref, sems = refs[NX + 1 :]
    rows, model_width = tokens_hbm.shape
    hidden = gate_hbm.shape[1]
    rank = gate_in_hbm.shape[0]
    examples = lengths_ref.shape[0]
    seq_dev = rows // examples
    groups, count = [], 0
    for start in range(0, model_width, chunk):
        part = pl.ds(start, chunk)
        pairs = [
            (tokens_hbm.at[:, part], tokens_ref.at[:, part]),
            (gate_hbm.at[part], weight_ref.at[part, pl.ds(0, hidden)]),
            (up_hbm.at[part], weight_ref.at[part, pl.ds(hidden, hidden)]),
            (gate_in_hbm.at[:, part], in_ref.at[pl.ds(0, rank), part]),
            (up_in_hbm.at[:, part], in_ref.at[pl.ds(rank, rank), part]),
        ]
        if start + chunk == model_width:
            pairs.append((down_in_hbm, down_in_ref))
        groups.append([pltpu.make_async_copy(a, b, sems.at[count + k]) for k, (a, b) in enumerate(pairs)])
        count += len(pairs)
        for copy in groups[-1]:
            copy.start()
    top = 2 * hidden + rank
    width = model_width // NX
    pairs = [(gate_out_hbm, out_ref.at[pl.ds(0, rank)]), (up_out_hbm, out_ref.at[pl.ds(rank, rank)])]
    for step, message in enumerate(messages, 1):
        start = pl.multiple_of(lax.rem(lax.axis_index("x") + step, NX) * width, width)
        bottom = message.shape[0] - hidden - FOLD
        pairs.append((down_hbm.at[:, pl.ds(start, width)], message.at[pl.ds(bottom, hidden)]))
    extra = [pltpu.make_async_copy(a, b, sems.at[count + k]) for k, (a, b) in enumerate(pairs)]
    for copy in extra:
        copy.start()
    for index, group in enumerate(groups):
        for copy in group:
            copy.wait()
        part = slice(index * chunk, (index + 1) * chunk)
        values = jnp.dot(tokens_ref[:, part], weight_ref[part, :], preferred_element_type=jnp.float32)
        right = dot32(tokens_ref[:, part], in_ref[:, part], ((1,), (1,)))
        if index == 0:
            total_ref[...] = values
            right_ref[...] = right
        else:
            total_ref[...] += values
            right_ref[...] += right

    done_ref[...] = jnp.zeros_like(done_ref)
    tile = min(256, seq_dev)
    seq_index = lax.axis_index("sy") * SEQ_PARTS[1] + lax.axis_index("sc")
    for step in range(rows // tile):
        span = slice(step * tile, (step + 1) * tile)
        gate, up = total_ref[span, :hidden], total_ref[span, hidden:]
        sigmoid = 1.0 / (1.0 + jnp.exp(-gate))
        silu = gate * sigmoid
        factor_gate = up * sigmoid * (1.0 + gate * (1.0 - sigmoid))
        hidden_value = (silu * up).astype(jnp.bfloat16)
        factor_gate = factor_gate.T.astype(jnp.bfloat16)
        factor_up = silu.T.astype(jnp.bfloat16)

        first = seq_index * seq_dev + step * tile % seq_dev
        limit = lengths_ref[step * tile // seq_dev]
        columns = first + lax.broadcasted_iota(jnp.int32, (rank, tile), 1)
        right_down = dot32(down_in_ref[...], hidden_value, ((1,), (1,)))
        right_down = jnp.where(columns < limit, right_down * scale, 0.0).astype(jnp.bfloat16)
        for message in messages[::2]:
            message[:hidden, span] = factor_gate
            message[hidden : 2 * hidden, span] = factor_up
            message[2 * hidden : top, span] = right_down
        rows_at = first + lax.broadcasted_iota(jnp.int32, (tile, 2 * rank), 0)
        right_ref[span, :] = jnp.where(rows_at < limit, right_ref[span, :] * scale, 0.0)
    for copy in extra:
        copy.wait()
    for message in messages:
        for block in range(2 * rank // FOLD):
            rows_of = slice(block * FOLD, (block + 1) * FOLD)
            message[-FOLD:, block * hidden : (block + 1) * hidden] = out_ref[rows_of, :]


def token_stage(tokens, gate_weight, up_weight, gate_in, up_in, down_in, down_weight, gate_out, up_out, lengths, scale):
    rows, width = tokens.shape
    hidden = gate_weight.shape[1]
    rank = gate_in.shape[0]
    chunk = 512
    return pl.pallas_call(
        lambda *refs: token_kernel(chunk, scale, *refs),
        out_shape=[
            jax.ShapeDtypeStruct((3 * hidden + rank + FOLD, rows), jnp.bfloat16),
            jax.ShapeDtypeStruct((hidden + FOLD, rows), jnp.bfloat16),
            jax.ShapeDtypeStruct((3 * hidden + rank + FOLD, rows), jnp.bfloat16),
            jax.ShapeDtypeStruct((rows, 2 * rank), jnp.float32),
            jax.ShapeDtypeStruct((8, 128), jnp.float32),
        ],
        in_specs=[pl.BlockSpec(memory_space=pltpu.SMEM)] + [HBM] * 9,
        out_specs=[VMEM] * (NX + 1),
        scratch_shapes=[
            pltpu.VMEM((rows, width), jnp.bfloat16),
            pltpu.VMEM((width, 2 * hidden), jnp.bfloat16),
            pltpu.VMEM((2 * rank, width), jnp.bfloat16),
            pltpu.VMEM((rank, hidden), jnp.bfloat16),
            pltpu.VMEM((2 * rank, hidden), jnp.bfloat16),
            pltpu.VMEM((rows, 2 * hidden), jnp.float32),
            pltpu.SemaphoreType.DMA((5 * (width // chunk) + 2 + NX,)),
        ],
        compiler_params=pltpu.CompilerParams(vmem_limit_bytes=61 * MIB),
        cost_estimate=pl.CostEstimate(
            flops=2 * rows * width * 512, bytes_accessed=16 * MIB, transcendentals=rows * hidden
        ),
        name="token_stage",
    )(lengths, tokens, gate_weight, up_weight, gate_in, up_in, down_in, down_weight, gate_out, up_out)


def forward_kernel(before_ref, after_ref, first_ref, second_ref):
    half = first_ref.shape[0]
    first_ref[...] = before_ref[:half, :]
    second_ref[...] = after_ref[half : 2 * half, :]


def halves(before, after, half):
    shape = jax.ShapeDtypeStruct((half, before.shape[1]), before.dtype)
    return pl.pallas_call(
        forward_kernel,
        out_shape=[shape] * 2,
        in_specs=[VMEM] * 2,
        out_specs=[VMEM] * 2,
        compiler_params=pltpu.CompilerParams(vmem_limit_bytes=8 * MIB),
        name="halves",
    )(before, after)


def tail_kernel(weight_hbm, gate_out_ref, up_out_ref, down_out_hbm, right_ref, *refs):
    messages, far_halves, blocks = refs[:NX], refs[NX : NX + 2], refs[NX + 2 : NX + 2 + NZ]
    out_ref, weights, projs, grads, far_ref, total, sems = refs[NX + 2 + NZ :]
    factors = [messages[0], messages[1], far_ref, messages[3]]
    hidden, model_width = weight_hbm.shape
    rank = gate_out_ref.shape[0]
    width = model_width // NX
    examples, both, seq_dev = blocks[0].shape
    piece = both // NY
    top = 2 * hidden + rank
    x_at, z_at, y_at = lax.axis_index("x"), lax.axis_index("z"), lax.axis_index("yh")

    start = pl.multiple_of(x_at * width, width)
    pairs = [
        (weight_hbm.at[:, pl.ds(start, width)], weights.at[pl.ds(0, hidden)]),
        (down_out_hbm.at[:, pl.ds(start, width)], weights.at[pl.ds(NX * hidden, rank)]),
    ]
    for step in range(1, NX):
        bottom = messages[step].shape[0] - hidden - FOLD
        pairs.append((messages[step].at[pl.ds(bottom, hidden)], weights.at[pl.ds(step * hidden, hidden)]))
    for index, part in enumerate(far_halves):
        pairs.append((part, far_ref.at[pl.ds(index * part.shape[0], part.shape[0])]))
    for step, block in enumerate(blocks):
        base = lax.rem(z_at + step, NZ) * both
        for kind, y_of in enumerate((y_at, 1 - y_at)):
            rows = pl.ds(pl.multiple_of(base + y_of * piece, piece), piece)
            pairs.append((block.at[:, pl.ds(kind * piece, piece)], grads.at[:, rows]))
    copies = [pltpu.make_async_copy(a, b, sems.at[k]) for k, (a, b) in enumerate(pairs)]
    for copy in copies:
        copy.start()
    projs[:rank, :hidden] = gate_out_ref[...]
    projs[rank:, :hidden] = up_out_ref[...]
    for step in range(1, NX):
        columns = slice(step * hidden, (step + 1) * hidden)
        for block in range(2 * rank // FOLD):
            folded = messages[step][-FOLD:, block * hidden : (block + 1) * hidden]
            projs[block * FOLD : (block + 1) * FOLD, columns] = folded
    for copy in copies:
        copy.wait()
    for example in range(examples):
        total[example] = jnp.dot(weights[...], grads[example], preferred_element_type=jnp.float32)
    for example in range(examples):
        columns = slice(example * seq_dev, (example + 1) * seq_dev)
        left = []
        for kind in range(2):
            products = []
            for step in range(NX):
                factor = factors[step][kind * hidden : (kind + 1) * hidden, columns].astype(jnp.float32)
                products.append(total[example, step * hidden : (step + 1) * hidden] * factor)
            product = jnp.concatenate(products, axis=0)
            high = product.astype(jnp.bfloat16)
            low = (product - high.astype(jnp.float32)).astype(jnp.bfloat16)
            proj = projs[kind * rank : (kind + 1) * rank, :]
            left.append(
                jnp.dot(proj, high, preferred_element_type=jnp.float32)
                + jnp.dot(proj, low, preferred_element_type=jnp.float32)
            )
        sides = jnp.dot(
            jnp.concatenate(left, axis=0),
            right_ref[columns, :],
            precision=lax.Precision.HIGHEST,
            preferred_element_type=jnp.float32,
        )
        right_down = factors[0][2 * hidden : top, columns].astype(jnp.float32)
        for step in range(1, NX):
            right_down = right_down + factors[step][2 * hidden : top, columns].astype(jnp.float32)
        out_ref[3 * example] = sides[:rank, :rank]
        out_ref[3 * example + 1] = sides[rank:, rank:]
        out_ref[3 * example + 2] = dot32(
            total[example, NX * hidden :], right_down, ((1,), (1,)), precision=lax.Precision.HIGHEST
        )


def tail_stage(down_weight, gate_out, up_out, down_out, right, messages, far, blocks):
    hidden, model_width = down_weight.shape
    rank = gate_out.shape[0]
    examples, _, seq_dev = blocks[0].shape
    width = model_width // NX
    operands = [down_weight, gate_out, up_out, down_out, right, *messages, *far, *blocks]
    return pl.pallas_call(
        tail_kernel,
        out_shape=jax.ShapeDtypeStruct((examples * 3, rank, rank), jnp.float32),
        in_specs=[HBM, VMEM, VMEM, HBM, VMEM] + [VMEM] * NX + [HBM] * (2 + NZ),
        out_specs=VMEM,
        scratch_shapes=[
            pltpu.VMEM((NX * hidden + rank, width), jnp.bfloat16),
            pltpu.VMEM((2 * rank, NX * hidden), jnp.bfloat16),
            pltpu.VMEM((examples, width, seq_dev), jnp.bfloat16),
            pltpu.VMEM((2 * far[0].shape[0], examples * seq_dev), jnp.bfloat16),
            pltpu.VMEM((examples, NX * hidden + rank, seq_dev), jnp.float32),
            pltpu.SemaphoreType.DMA((3 + NX + NZ * NY,)),
        ],
        compiler_params=pltpu.CompilerParams(vmem_limit_bytes=16 * MIB),
        cost_estimate=pl.CostEstimate(flops=4 * 10**9, bytes_accessed=8 * MIB, transcendentals=0),
        name="tail_stage",
    )(*operands)


def ring_z(own):
    up, down = [own], [own]
    for _ in range(NZ // 2 - 1):
        up.append(lax.ppermute(up[-1], "z", shifted(NZ, -1)))
        down.append(lax.ppermute(down[-1], "z", shifted(NZ, 1)))
    return up + [lax.ppermute(up[-1], "z", shifted(NZ, -1))] + down[:0:-1]


def sum_everywhere(partial):
    count, size = partial.shape
    parts = SEQ_PARTS[0] * SEQ_PARTS[1] * NZ
    width = size // parts
    pieces = partial.reshape(count, parts, width).transpose(1, 0, 2)
    pieces = lax.all_to_all(pieces, ("sy", "sc", "z"), 0, 0, tiled=True)
    own = jnp.sum(pieces, axis=0)
    spread = jnp.broadcast_to(own[None], (NX * NZ * NY,) + own.shape)
    blocks = lax.all_to_all(spread, ("x", "z", "yh"), 0, 0, tiled=True)
    blocks = blocks.reshape(NX, NZ, NY, count, width).sum(axis=(0, 2))
    return blocks.transpose(1, 0, 2).reshape(count, NZ * width)


def shards(
    tokens,
    out_grad,
    gate_weight,
    up_weight,
    down_weight,
    proj_gate_in,
    proj_gate_out,
    proj_up_in,
    proj_up_out,
    proj_down_in,
    proj_down_out,
    lengths,
):
    examples, seq_dev, model_width = tokens.shape
    scale = float(seq_dev * SEQ_PARTS[0] * SEQ_PARTS[1]) ** (-0.5)
    gate_out, up_out = proj_gate_out.T, proj_up_out.T

    own_grad = out_grad.transpose(0, 2, 1)
    other_grad = lax.ppermute(own_grad, "yh", shifted(NY, 1))
    flat_tokens = tokens.reshape(examples * seq_dev, model_width)
    sent = token_stage(
        flat_tokens,
        gate_weight,
        up_weight,
        proj_gate_in.T,
        proj_up_in.T,
        proj_down_in.T,
        down_weight,
        gate_out,
        up_out,
        lengths,
        scale,
    )
    sent, (right, done) = sent[: NX - 1], sent[NX - 1 :]
    messages = [sent[0]] + [lax.ppermute(piece, "x", shifted(NX, step)) for step, piece in enumerate(sent, 1)]
    first, second = halves(messages[1], messages[3], gate_weight.shape[1] + gate_out.shape[0] // 2)
    far = [lax.ppermute(first, "x", shifted(NX, 1)), lax.ppermute(second, "x", shifted(NX, -1))]
    pair = pair_up(own_grad, other_grad, done)
    blocks = ring_z(pair)
    products = tail_stage(down_weight, gate_out, up_out, proj_down_out.T, right, messages, far, blocks)
    total = sum_everywhere(products.reshape(examples * 3, -1))
    return total.reshape(examples, 3, -1)


def solution(mesh):
    fine = Mesh(mesh.devices.reshape(SEQ_PARTS + FSDP_PARTS), ("sy", "sc", "x", "z", "yh"))
    seq, fsdp = ("sy", "sc"), ("x", "z", "yh")
    placed = (
        P(None, seq, None),
        P(None, seq, fsdp),
        P(None, fsdp),
        P(None, fsdp),
        P(fsdp, None),
        P(),
        P(fsdp, None),
        P(),
        P(fsdp, None),
        P(fsdp, None),
        P(),
        P(),
    )
    return jax.shard_map(
        shards, mesh=fine, in_specs=placed, out_specs=P(None, None, seq), check_vma=False
    )
```

```python
import jax
import jax.numpy as jnp
from jax import lax
from jax.experimental import pallas as pl
from jax.experimental.pallas import tpu as pltpu
from jax.sharding import Mesh, PartitionSpec as P

SEQ_PARTS = (2, 2)
FSDP_PARTS = (4, 8, 2)
NX, NZ, NY = FSDP_PARTS
FOLD = 16
MIB = 1024 * 1024
VMEM = pl.BlockSpec(memory_space=pltpu.VMEM)
HBM = pl.BlockSpec(memory_space=pltpu.HBM)


def shifted(count, step):
    return [(i, (i + step) % count) for i in range(count)]


def dot32(a, b, dims, precision=None):
    return lax.dot_general(a, b, (dims, ((), ())), preferred_element_type=jnp.float32, precision=precision)


def pair_kernel(own_ref, other_ref, *refs):
    out_ref = refs[-1]
    piece = own_ref.shape[1]
    out_ref[:, :piece, :] = own_ref[...]
    out_ref[:, piece:, :] = other_ref[...]


def pair_up(own, other, messages):
    examples, piece, seq_dev = own.shape
    *messages, pair = pl.pallas_call(
        pair_kernel,
        out_shape=[
            *[jax.ShapeDtypeStruct(message.shape, message.dtype) for message in messages],
            jax.ShapeDtypeStruct((examples, NY * piece, seq_dev), own.dtype),
        ],
        in_specs=[VMEM, VMEM] + [HBM] * len(messages),
        out_specs=[HBM] * len(messages) + [VMEM],
        input_output_aliases={2 + index: index for index in range(len(messages))},
        compiler_params=pltpu.CompilerParams(vmem_limit_bytes=62 * MIB),
        name="pair_up",
    )(own, other, *messages)
    return pair, messages


def token_kernel(chunk, scale, lengths_ref, tokens_hbm, gate_hbm, up_hbm, gate_in_hbm, up_in_hbm, down_in_hbm, down_hbm, gate_out_hbm, up_out_hbm, *refs):
    messages, right_ref = refs[: NX - 1], refs[NX - 1]
    tokens_ref, weight_ref, in_ref, down_in_ref, out_ref, total_ref, sems = refs[NX:]
    rows, model_width = tokens_hbm.shape
    hidden = gate_hbm.shape[1]
    rank = gate_in_hbm.shape[0]
    examples = lengths_ref.shape[0]
    seq_dev = rows // examples
    groups, count = [], 0
    for start in range(0, model_width, chunk):
        part = pl.ds(start, chunk)
        pairs = [
            (tokens_hbm.at[:, part], tokens_ref.at[:, part]),
            (gate_hbm.at[part], weight_ref.at[part, pl.ds(0, hidden)]),
            (up_hbm.at[part], weight_ref.at[part, pl.ds(hidden, hidden)]),
            (gate_in_hbm.at[:, part], in_ref.at[pl.ds(0, rank), part]),
            (up_in_hbm.at[:, part], in_ref.at[pl.ds(rank, rank), part]),
        ]
        if start + chunk == model_width:
            pairs.append((down_in_hbm, down_in_ref))
        groups.append([pltpu.make_async_copy(a, b, sems.at[count + k]) for k, (a, b) in enumerate(pairs)])
        count += len(pairs)
        for copy in groups[-1]:
            copy.start()
    top = 2 * hidden + rank
    width, half = model_width // NX, hidden // 2
    core = lax.axis_index("sc")
    pairs = [(gate_out_hbm, out_ref.at[pl.ds(0, rank)]), (up_out_hbm, out_ref.at[pl.ds(rank, rank)])]
    for step, message in enumerate(messages, 1):
        start = pl.multiple_of(lax.rem(lax.axis_index("x") + step, NX) * width, width)
        bottom = message.shape[0] - half - FOLD
        pairs.append((down_hbm.at[pl.ds(core * half, half), pl.ds(start, width)], message.at[pl.ds(bottom, half)]))
    extra = [pltpu.make_async_copy(a, b, sems.at[count + k]) for k, (a, b) in enumerate(pairs)]
    for copy in extra:
        copy.start()
    for index, group in enumerate(groups):
        for copy in group:
            copy.wait()
        part = slice(index * chunk, (index + 1) * chunk)
        values = jnp.dot(tokens_ref[:, part], weight_ref[part, :], preferred_element_type=jnp.float32)
        right = dot32(tokens_ref[:, part], in_ref[:, part], ((1,), (1,)))
        if index == 0:
            total_ref[...] = values
            right_ref[...] = right
        else:
            total_ref[...] += values
            right_ref[...] += right

    tile = min(256, seq_dev)
    seq_index = lax.axis_index("sy") * SEQ_PARTS[1] + lax.axis_index("sc")
    for step in range(rows // tile):
        span = slice(step * tile, (step + 1) * tile)
        gate, up = total_ref[span, :hidden], total_ref[span, hidden:]
        sigmoid = 1.0 / (1.0 + jnp.exp(-gate))
        silu = gate * sigmoid
        factor_gate = up * sigmoid * (1.0 + gate * (1.0 - sigmoid))
        hidden_value = (silu * up).astype(jnp.bfloat16)
        factor_gate = factor_gate.T.astype(jnp.bfloat16)
        factor_up = silu.T.astype(jnp.bfloat16)

        first = seq_index * seq_dev + step * tile % seq_dev
        limit = lengths_ref[step * tile // seq_dev]
        columns = first + lax.broadcasted_iota(jnp.int32, (rank, tile), 1)
        right_down = dot32(down_in_ref[...], hidden_value, ((1,), (1,)))
        right_down = jnp.where(columns < limit, right_down * scale, 0.0).astype(jnp.bfloat16)
        for message in messages[::2]:
            message[:hidden, span] = factor_gate
            message[hidden : 2 * hidden, span] = factor_up
            message[2 * hidden : top, span] = right_down
        rows_at = first + lax.broadcasted_iota(jnp.int32, (tile, 2 * rank), 0)
        right_ref[span, :] = jnp.where(rows_at < limit, right_ref[span, :] * scale, 0.0)
    for copy in extra:
        copy.wait()
    for message in messages:
        for block in range(2 * rank // FOLD):
            rows_of = slice(block * FOLD, (block + 1) * FOLD)
            message[-FOLD:, block * hidden : (block + 1) * hidden] = out_ref[rows_of, :]


def token_stage(tokens, gate_weight, up_weight, gate_in, up_in, down_in, down_weight, gate_out, up_out, lengths, scale):
    rows, width = tokens.shape
    hidden = gate_weight.shape[1]
    rank = gate_in.shape[0]
    chunk = 512
    return pl.pallas_call(
        lambda *refs: token_kernel(chunk, scale, *refs),
        out_shape=[
            jax.ShapeDtypeStruct((2 * hidden + hidden // 2 + rank + FOLD, rows), jnp.bfloat16),
            jax.ShapeDtypeStruct((hidden // 2 + FOLD, rows), jnp.bfloat16),
            jax.ShapeDtypeStruct((2 * hidden + hidden // 2 + rank + FOLD, rows), jnp.bfloat16),
            jax.ShapeDtypeStruct((rows, 2 * rank), jnp.float32),
        ],
        in_specs=[pl.BlockSpec(memory_space=pltpu.SMEM)] + [HBM] * 9,
        out_specs=[VMEM] * NX,
        scratch_shapes=[
            pltpu.VMEM((rows, width), jnp.bfloat16),
            pltpu.VMEM((width, 2 * hidden), jnp.bfloat16),
            pltpu.VMEM((2 * rank, width), jnp.bfloat16),
            pltpu.VMEM((rank, hidden), jnp.bfloat16),
            pltpu.VMEM((2 * rank, hidden), jnp.bfloat16),
            pltpu.VMEM((rows, 2 * hidden), jnp.float32),
            pltpu.SemaphoreType.DMA((5 * (width // chunk) + 2 + NX,)),
        ],
        compiler_params=pltpu.CompilerParams(vmem_limit_bytes=61 * MIB),
        cost_estimate=pl.CostEstimate(
            flops=2 * rows * width * 512, bytes_accessed=16 * MIB, transcendentals=rows * hidden
        ),
        name="token_stage",
    )(lengths, tokens, gate_weight, up_weight, gate_in, up_in, down_in, down_weight, gate_out, up_out)


def forward_kernel(before_ref, after_ref, first_ref, second_ref, swap_ref):
    rows = first_ref.shape[0]
    half = swap_ref.shape[0] // 2
    first_ref[...] = before_ref[:rows, :]
    second_ref[...] = after_ref[rows : 2 * rows, :]
    swap_ref[:half, :] = before_ref[2 * rows : 2 * rows + half, :]
    swap_ref[half:, :] = after_ref[2 * rows : 2 * rows + half, :]


def halves(before, after, rows, half):
    shape = jax.ShapeDtypeStruct((rows, before.shape[1]), before.dtype)
    swap = jax.ShapeDtypeStruct((2 * half, before.shape[1]), before.dtype)
    return pl.pallas_call(
        forward_kernel,
        out_shape=[shape, shape, swap],
        in_specs=[VMEM] * 2,
        out_specs=[VMEM] * 3,
        compiler_params=pltpu.CompilerParams(vmem_limit_bytes=12 * MIB),
        name="halves",
    )(before, after)


def tail_kernel(weight_hbm, gate_out_ref, up_out_ref, down_out_hbm, right_ref, *refs):
    messages, far_halves, swaps, blocks = refs[:NX], refs[NX : NX + 2], refs[NX + 2 : NX + 4], refs[NX + 4 : NX + 4 + NZ]
    out_ref, weights, projs, grads, far_ref, total, sems = refs[NX + 4 + NZ :]
    factors = [messages[0], messages[1], far_ref, messages[3]]
    hidden, model_width = weight_hbm.shape
    rank = gate_out_ref.shape[0]
    width = model_width // NX
    examples, both, seq_dev = blocks[0].shape
    piece = both // NY
    top, half, core = 2 * hidden + rank, hidden // 2, lax.axis_index("sc")
    x_at, z_at, y_at = lax.axis_index("x"), lax.axis_index("z"), lax.axis_index("yh")

    start = pl.multiple_of(x_at * width, width)
    pairs = [
        (weight_hbm.at[:, pl.ds(start, width)], weights.at[pl.ds(0, hidden)]),
        (down_out_hbm.at[:, pl.ds(start, width)], weights.at[pl.ds(NX * hidden, rank)]),
    ]
    for step in range(1, NX):
        bottom = messages[step].shape[0] - half - FOLD
        mine = pl.ds(pl.multiple_of(step * hidden + core * half, half), half)
        pairs.append((messages[step].at[pl.ds(bottom, half)], weights.at[mine]))
        theirs = pl.ds(pl.multiple_of(step * hidden + (1 - core) * half, half), half)
        swapped = swaps[1].at[pl.ds(0, half)] if step == 2 else swaps[0].at[pl.ds(step // 2 * half, half)]
        pairs.append((swapped, weights.at[theirs]))
    for index, part in enumerate(far_halves):
        pairs.append((part, far_ref.at[pl.ds(index * part.shape[0], part.shape[0])]))
    for step, block in enumerate(blocks):
        base = lax.rem(z_at + step, NZ) * both
        for kind, y_of in enumerate((y_at, 1 - y_at)):
            rows = pl.ds(pl.multiple_of(base + y_of * piece, piece), piece)
            pairs.append((block.at[:, pl.ds(kind * piece, piece)], grads.at[:, rows]))
    copies = [pltpu.make_async_copy(a, b, sems.at[k]) for k, (a, b) in enumerate(pairs)]
    for copy in copies:
        copy.start()
    projs[:rank, :hidden] = gate_out_ref[...]
    projs[rank:, :hidden] = up_out_ref[...]
    for step in range(1, NX):
        columns = slice(step * hidden, (step + 1) * hidden)
        for block in range(2 * rank // FOLD):
            folded = messages[step][-FOLD:, block * hidden : (block + 1) * hidden]
            projs[block * FOLD : (block + 1) * FOLD, columns] = folded
    for copy in copies:
        copy.wait()
    for example in range(examples):
        total[example] = jnp.dot(weights[...], grads[example], preferred_element_type=jnp.float32)
    for example in range(examples):
        columns = slice(example * seq_dev, (example + 1) * seq_dev)
        left = []
        for kind in range(2):
            products = []
            for step in range(NX):
                factor = factors[step][kind * hidden : (kind + 1) * hidden, columns].astype(jnp.float32)
                products.append(total[example, step * hidden : (step + 1) * hidden] * factor)
            product = jnp.concatenate(products, axis=0)
            high = product.astype(jnp.bfloat16)
            low = (product - high.astype(jnp.float32)).astype(jnp.bfloat16)
            proj = projs[kind * rank : (kind + 1) * rank, :]
            left.append(
                jnp.dot(proj, high, preferred_element_type=jnp.float32)
                + jnp.dot(proj, low, preferred_element_type=jnp.float32)
            )
        sides = jnp.dot(
            jnp.concatenate(left, axis=0),
            right_ref[columns, :],
            precision=lax.Precision.HIGHEST,
            preferred_element_type=jnp.float32,
        )
        right_down = factors[0][2 * hidden : top, columns].astype(jnp.float32)
        for step in range(1, NX):
            right_down = right_down + factors[step][2 * hidden : top, columns].astype(jnp.float32)
        out_ref[3 * example] = sides[:rank, :rank]
        out_ref[3 * example + 1] = sides[rank:, rank:]
        out_ref[3 * example + 2] = dot32(
            total[example, NX * hidden :], right_down, ((1,), (1,)), precision=lax.Precision.HIGHEST
        )


def tail_stage(down_weight, gate_out, up_out, down_out, right, messages, far, swaps, blocks):
    hidden, model_width = down_weight.shape
    rank = gate_out.shape[0]
    examples, _, seq_dev = blocks[0].shape
    width = model_width // NX
    operands = [down_weight, gate_out, up_out, down_out, right, *messages, *far, *swaps, *blocks]
    return pl.pallas_call(
        tail_kernel,
        out_shape=jax.ShapeDtypeStruct((examples * 3, rank, rank), jnp.float32),
        in_specs=[HBM, VMEM, VMEM, HBM, VMEM] + [VMEM] * NX + [HBM] * (4 + NZ),
        out_specs=VMEM,
        scratch_shapes=[
            pltpu.VMEM((NX * hidden + rank, width), jnp.bfloat16),
            pltpu.VMEM((2 * rank, NX * hidden), jnp.bfloat16),
            pltpu.VMEM((examples, width, seq_dev), jnp.bfloat16),
            pltpu.VMEM((2 * far[0].shape[0], examples * seq_dev), jnp.bfloat16),
            pltpu.VMEM((examples, NX * hidden + rank, seq_dev), jnp.float32),
            pltpu.SemaphoreType.DMA((2 + 2 * NX + NZ * NY,)),
        ],
        compiler_params=pltpu.CompilerParams(vmem_limit_bytes=16 * MIB),
        cost_estimate=pl.CostEstimate(flops=4 * 10**9, bytes_accessed=8 * MIB, transcendentals=0),
        name="tail_stage",
    )(*operands)


def ring_z(own):
    up, down = [own], [own]
    for _ in range(NZ // 2 - 1):
        up.append(lax.ppermute(up[-1], "z", shifted(NZ, -1)))
        down.append(lax.ppermute(down[-1], "z", shifted(NZ, 1)))
    return up + [lax.ppermute(up[-1], "z", shifted(NZ, -1))] + down[:0:-1]


def sum_everywhere(partial):
    count, size = partial.shape
    parts = SEQ_PARTS[0] * SEQ_PARTS[1] * NZ
    width = size // parts
    pieces = partial.reshape(count, parts, width).transpose(1, 0, 2)
    pieces = lax.all_to_all(pieces, ("sy", "sc", "z"), 0, 0, tiled=True)
    own = jnp.sum(pieces, axis=0)
    spread = jnp.broadcast_to(own[None], (NX * NZ * NY,) + own.shape)
    blocks = lax.all_to_all(spread, ("x", "z", "yh"), 0, 0, tiled=True)
    blocks = blocks.reshape(NX, NZ, NY, count, width).sum(axis=(0, 2))
    return blocks.transpose(1, 0, 2).reshape(count, NZ * width)


def shards(
    tokens,
    out_grad,
    gate_weight,
    up_weight,
    down_weight,
    proj_gate_in,
    proj_gate_out,
    proj_up_in,
    proj_up_out,
    proj_down_in,
    proj_down_out,
    lengths,
):
    examples, seq_dev, model_width = tokens.shape
    scale = float(seq_dev * SEQ_PARTS[0] * SEQ_PARTS[1]) ** (-0.5)
    gate_out, up_out = proj_gate_out.T, proj_up_out.T

    own_grad = out_grad.transpose(0, 2, 1)
    other_grad = lax.ppermute(own_grad, "yh", shifted(NY, 1))
    flat_tokens = tokens.reshape(examples * seq_dev, model_width)
    sent = token_stage(
        flat_tokens,
        gate_weight,
        up_weight,
        proj_gate_in.T,
        proj_up_in.T,
        proj_down_in.T,
        down_weight,
        gate_out,
        up_out,
        lengths,
        scale,
    )
    sent, right = sent[: NX - 1], sent[NX - 1]
    pair, sent = pair_up(own_grad, other_grad, sent)
    messages = [sent[0]] + [lax.ppermute(piece, "x", shifted(NX, step)) for step, piece in enumerate(sent, 1)]
    hidden, rank = gate_weight.shape[1], gate_out.shape[0]
    first, second, swap = halves(messages[1], messages[3], hidden + rank // 2, hidden // 2)
    far = [lax.ppermute(first, "x", shifted(NX, 1)), lax.ppermute(second, "x", shifted(NX, -1))]
    swaps = [lax.ppermute(piece, "sc", shifted(SEQ_PARTS[1], 1)) for piece in (swap, messages[2])]
    blocks = ring_z(pair)
    products = tail_stage(down_weight, gate_out, up_out, proj_down_out.T, right, messages, far, swaps, blocks)
    total = sum_everywhere(products.reshape(examples * 3, -1))
    return total.reshape(examples, 3, -1)


def solution(mesh):
    fine = Mesh(mesh.devices.reshape(SEQ_PARTS + FSDP_PARTS), ("sy", "sc", "x", "z", "yh"))
    seq, fsdp = ("sy", "sc"), ("x", "z", "yh")
    placed = (
        P(None, seq, None),
        P(None, seq, fsdp),
        P(None, fsdp),
        P(None, fsdp),
        P(fsdp, None),
        P(),
        P(fsdp, None),
        P(),
        P(fsdp, None),
        P(fsdp, None),
        P(),
        P(),
    )
    return jax.shard_map(
        shards, mesh=fine, in_specs=placed, out_specs=P(None, None, seq), check_vma=False
    )
```

```python
import jax
import jax.numpy as jnp
from jax import lax
from jax.experimental import pallas as pl
from jax.experimental.pallas import tpu as pltpu
from jax.sharding import Mesh, PartitionSpec as P

SEQ_PARTS = (2, 2)
FSDP_PARTS = (4, 8, 2)
NX, NZ, NY = FSDP_PARTS
FOLD = 16
MIB = 1024 * 1024
VMEM = pl.BlockSpec(memory_space=pltpu.VMEM)
HBM = pl.BlockSpec(memory_space=pltpu.HBM)


def shifted(count, step):
    return [(i, (i + step) % count) for i in range(count)]


def dot32(a, b, dims, precision=None):
    return lax.dot_general(a, b, (dims, ((), ())), preferred_element_type=jnp.float32, precision=precision)


def hold_kernel(*refs):
    pass


def hold(arrays):
    return pl.pallas_call(
        hold_kernel,
        out_shape=[jax.ShapeDtypeStruct(array.shape, array.dtype) for array in arrays],
        in_specs=[HBM] * len(arrays),
        out_specs=[HBM] * len(arrays),
        input_output_aliases={index: index for index in range(len(arrays))},
        compiler_params=pltpu.CompilerParams(vmem_limit_bytes=62 * MIB),
        name="hold",
    )(*arrays)


def pair_kernel(own_ref, other_ref, *refs):
    out_ref = refs[-1]
    piece = own_ref.shape[1]
    out_ref[:, :piece, :] = own_ref[...]
    out_ref[:, piece:, :] = other_ref[...]


def pair_up(own, other, messages):
    examples, piece, seq_dev = own.shape
    *messages, pair = pl.pallas_call(
        pair_kernel,
        out_shape=[
            *[jax.ShapeDtypeStruct(message.shape, message.dtype) for message in messages],
            jax.ShapeDtypeStruct((examples, NY * piece, seq_dev), own.dtype),
        ],
        in_specs=[VMEM, VMEM] + [HBM] * len(messages),
        out_specs=[HBM] * len(messages) + [VMEM],
        input_output_aliases={2 + index: index for index in range(len(messages))},
        compiler_params=pltpu.CompilerParams(vmem_limit_bytes=62 * MIB),
        name="pair_up",
    )(own, other, *messages)
    return pair, messages


def token_kernel(chunk, scale, lengths_ref, tokens_hbm, gate_hbm, up_hbm, gate_in_hbm, up_in_hbm, down_in_hbm, down_hbm, gate_out_hbm, up_out_hbm, *refs):
    messages, right_ref = refs[: NX - 1], refs[NX - 1]
    tokens_ref, weight_ref, in_ref, down_in_ref, out_ref, total_ref, sems = refs[NX:]
    rows, model_width = tokens_hbm.shape
    hidden = gate_hbm.shape[1]
    rank = gate_in_hbm.shape[0]
    examples = lengths_ref.shape[0]
    seq_dev = rows // examples
    groups, count = [], 0
    for start in range(0, model_width, chunk):
        part = pl.ds(start, chunk)
        pairs = [
            (tokens_hbm.at[:, part], tokens_ref.at[:, part]),
            (gate_hbm.at[part], weight_ref.at[part, pl.ds(0, hidden)]),
            (up_hbm.at[part], weight_ref.at[part, pl.ds(hidden, hidden)]),
            (gate_in_hbm.at[:, part], in_ref.at[pl.ds(0, rank), part]),
            (up_in_hbm.at[:, part], in_ref.at[pl.ds(rank, rank), part]),
        ]
        if start + chunk == model_width:
            pairs.append((down_in_hbm, down_in_ref))
        groups.append([pltpu.make_async_copy(a, b, sems.at[count + k]) for k, (a, b) in enumerate(pairs)])
        count += len(pairs)
        for copy in groups[-1]:
            copy.start()
    top = 2 * hidden + rank
    width, half = model_width // NX, hidden // 2
    core = lax.axis_index("sc")
    pairs = [(gate_out_hbm, out_ref.at[pl.ds(0, rank)]), (up_out_hbm, out_ref.at[pl.ds(rank, rank)])]
    for step, message in enumerate(messages, 1):
        start = pl.multiple_of(lax.rem(lax.axis_index("x") + step, NX) * width, width)
        bottom = message.shape[0] - half - FOLD
        pairs.append((down_hbm.at[pl.ds(core * half, half), pl.ds(start, width)], message.at[pl.ds(bottom, half)]))
    extra = [pltpu.make_async_copy(a, b, sems.at[count + k]) for k, (a, b) in enumerate(pairs)]
    for copy in extra:
        copy.start()
    for index, group in enumerate(groups):
        for copy in group:
            copy.wait()
        part = slice(index * chunk, (index + 1) * chunk)
        values = jnp.dot(tokens_ref[:, part], weight_ref[part, :], preferred_element_type=jnp.float32)
        right = dot32(tokens_ref[:, part], in_ref[:, part], ((1,), (1,)))
        if index == 0:
            total_ref[...] = values
            right_ref[...] = right
        else:
            total_ref[...] += values
            right_ref[...] += right

    tile = min(256, seq_dev)
    seq_index = lax.axis_index("sy") * SEQ_PARTS[1] + lax.axis_index("sc")
    for step in range(rows // tile):
        span = slice(step * tile, (step + 1) * tile)
        gate, up = total_ref[span, :hidden], total_ref[span, hidden:]
        sigmoid = 1.0 / (1.0 + jnp.exp(-gate))
        silu = gate * sigmoid
        factor_gate = up * sigmoid * (1.0 + gate * (1.0 - sigmoid))
        hidden_value = (silu * up).astype(jnp.bfloat16)
        factor_gate = factor_gate.T.astype(jnp.bfloat16)
        factor_up = silu.T.astype(jnp.bfloat16)

        first = seq_index * seq_dev + step * tile % seq_dev
        limit = lengths_ref[step * tile // seq_dev]
        columns = first + lax.broadcasted_iota(jnp.int32, (rank, tile), 1)
        right_down = dot32(down_in_ref[...], hidden_value, ((1,), (1,)))
        right_down = jnp.where(columns < limit, right_down * scale, 0.0).astype(jnp.bfloat16)
        for message in messages[::2]:
            message[:hidden, span] = factor_gate
            message[hidden : 2 * hidden, span] = factor_up
            message[2 * hidden : top, span] = right_down
        rows_at = first + lax.broadcasted_iota(jnp.int32, (tile, 2 * rank), 0)
        right_ref[span, :] = jnp.where(rows_at < limit, right_ref[span, :] * scale, 0.0)
    for copy in extra:
        copy.wait()
    for message in messages:
        for block in range(2 * rank // FOLD):
            rows_of = slice(block * FOLD, (block + 1) * FOLD)
            message[-FOLD:, block * hidden : (block + 1) * hidden] = out_ref[rows_of, :]


def token_stage(tokens, gate_weight, up_weight, gate_in, up_in, down_in, down_weight, gate_out, up_out, lengths, scale):
    rows, width = tokens.shape
    hidden = gate_weight.shape[1]
    rank = gate_in.shape[0]
    chunk = 512
    return pl.pallas_call(
        lambda *refs: token_kernel(chunk, scale, *refs),
        out_shape=[
            jax.ShapeDtypeStruct((2 * hidden + hidden // 2 + rank + FOLD, rows), jnp.bfloat16),
            jax.ShapeDtypeStruct((hidden // 2 + FOLD, rows), jnp.bfloat16),
            jax.ShapeDtypeStruct((2 * hidden + hidden // 2 + rank + FOLD, rows), jnp.bfloat16),
            jax.ShapeDtypeStruct((rows, 2 * rank), jnp.float32),
        ],
        in_specs=[pl.BlockSpec(memory_space=pltpu.SMEM)] + [HBM] * 9,
        out_specs=[VMEM] * NX,
        scratch_shapes=[
            pltpu.VMEM((rows, width), jnp.bfloat16),
            pltpu.VMEM((width, 2 * hidden), jnp.bfloat16),
            pltpu.VMEM((2 * rank, width), jnp.bfloat16),
            pltpu.VMEM((rank, hidden), jnp.bfloat16),
            pltpu.VMEM((2 * rank, hidden), jnp.bfloat16),
            pltpu.VMEM((rows, 2 * hidden), jnp.float32),
            pltpu.SemaphoreType.DMA((5 * (width // chunk) + 2 + NX,)),
        ],
        compiler_params=pltpu.CompilerParams(vmem_limit_bytes=61 * MIB),
        cost_estimate=pl.CostEstimate(
            flops=2 * rows * width * 512, bytes_accessed=16 * MIB, transcendentals=rows * hidden
        ),
        name="token_stage",
    )(lengths, tokens, gate_weight, up_weight, gate_in, up_in, down_in, down_weight, gate_out, up_out)


def forward_kernel(before_ref, after_ref, first_ref, second_ref, swap_ref):
    rows = first_ref.shape[0]
    half = swap_ref.shape[0] // 2
    first_ref[...] = before_ref[:rows, :]
    second_ref[...] = after_ref[rows : 2 * rows, :]
    swap_ref[:half, :] = before_ref[2 * rows : 2 * rows + half, :]
    swap_ref[half:, :] = after_ref[2 * rows : 2 * rows + half, :]


def halves(before, after, rows, half):
    shape = jax.ShapeDtypeStruct((rows, before.shape[1]), before.dtype)
    swap = jax.ShapeDtypeStruct((2 * half, before.shape[1]), before.dtype)
    return pl.pallas_call(
        forward_kernel,
        out_shape=[shape, shape, swap],
        in_specs=[VMEM] * 2,
        out_specs=[VMEM] * 3,
        compiler_params=pltpu.CompilerParams(vmem_limit_bytes=12 * MIB),
        name="halves",
    )(before, after)


def tail_kernel(weight_hbm, gate_out_hbm, up_out_hbm, down_out_hbm, right_hbm, *refs):
    messages, far_halves, swaps = refs[:NX], refs[NX : NX + 2], refs[NX + 2 : NX + 4]
    blocks, far_block = refs[NX + 4 : NX + 3 + NZ], refs[NX + 3 + NZ : NX + 5 + NZ]
    out_ref, weights, projs, folds, grads, factors, right_ref, total, sems = refs[NX + 5 + NZ :]
    hidden, model_width = weight_hbm.shape
    rank = gate_out_hbm.shape[0]
    width = model_width // NX
    examples, both, seq_dev = blocks[0].shape
    piece = both // NY
    top, half, core = 2 * hidden + rank, hidden // 2, lax.axis_index("sc")
    x_at, z_at, y_at = lax.axis_index("x"), lax.axis_index("z"), lax.axis_index("yh")

    start = pl.multiple_of(x_at * width, width)
    pairs = [
        (weight_hbm.at[:, pl.ds(start, width)], weights.at[pl.ds(0, hidden)]),
        (down_out_hbm.at[:, pl.ds(start, width)], weights.at[pl.ds(NX * hidden, rank)]),
    ]
    for step in range(1, NX):
        bottom = messages[step].shape[0] - half - FOLD
        mine = pl.ds(pl.multiple_of(step * hidden + core * half, half), half)
        pairs.append((messages[step].at[pl.ds(bottom, half)], weights.at[mine]))
        theirs = pl.ds(pl.multiple_of(step * hidden + (1 - core) * half, half), half)
        swapped = swaps[1].at[pl.ds(0, half)] if step == 2 else swaps[0].at[pl.ds(step // 2 * half, half)]
        pairs.append((swapped, weights.at[theirs]))
    count = examples // 2
    slots = [(slice(0, examples), step, blocks[step if step < NZ // 2 else step - 1]) for step in range(NZ) if step != NZ // 2]
    slots += [(slice(0, count), NZ // 2, far_block[0]), (slice(count, examples), NZ // 2, far_block[1])]
    for span, step, block in slots:
        base = lax.rem(z_at + step, NZ) * both
        for kind, y_of in enumerate((y_at, 1 - y_at)):
            rows = pl.ds(pl.multiple_of(base + y_of * piece, piece), piece)
            pairs.append((block.at[:, pl.ds(kind * piece, piece)], grads.at[span, rows]))
    early = len(pairs)
    pairs += [(gate_out_hbm, projs.at[pl.ds(0, rank), pl.ds(0, hidden)])]
    pairs += [(up_out_hbm, projs.at[pl.ds(rank, rank), pl.ds(0, hidden)])]
    for step, message in enumerate(messages):
        if step > 0:
            pairs.append((message.at[pl.ds(message.shape[0] - FOLD, FOLD)], folds.at[step - 1]))
        if step != 2:
            pairs.append((message.at[pl.ds(0, top)], factors.at[step]))
    for index, part in enumerate(far_halves):
        pairs.append((part, factors.at[2, pl.ds(index * part.shape[0], part.shape[0])]))
    pairs.append((right_hbm, right_ref))
    copies = [pltpu.make_async_copy(a, b, sems.at[k]) for k, (a, b) in enumerate(pairs)]
    for copy in copies:
        copy.start()
    for copy in copies[:early]:
        copy.wait()
    for example in range(examples):
        total[example] = jnp.dot(weights[...], grads[example], preferred_element_type=jnp.float32)
    for copy in copies[early:]:
        copy.wait()
    for step in range(1, NX):
        columns = slice(step * hidden, (step + 1) * hidden)
        for block in range(2 * rank // FOLD):
            projs[block * FOLD : (block + 1) * FOLD, columns] = folds[step - 1, :, block * hidden : (block + 1) * hidden]
    for example in range(examples):
        columns = slice(example * seq_dev, (example + 1) * seq_dev)
        left = []
        for kind in range(2):
            products = []
            for step in range(NX):
                factor = factors[step, kind * hidden : (kind + 1) * hidden, columns].astype(jnp.float32)
                products.append(total[example, step * hidden : (step + 1) * hidden] * factor)
            product = jnp.concatenate(products, axis=0)
            high = product.astype(jnp.bfloat16)
            low = (product - high.astype(jnp.float32)).astype(jnp.bfloat16)
            proj = projs[kind * rank : (kind + 1) * rank, :]
            left.append(
                jnp.dot(proj, high, preferred_element_type=jnp.float32)
                + jnp.dot(proj, low, preferred_element_type=jnp.float32)
            )
        sides = jnp.dot(
            jnp.concatenate(left, axis=0),
            right_ref[columns, :],
            precision=lax.Precision.HIGHEST,
            preferred_element_type=jnp.float32,
        )
        right_down = factors[0, 2 * hidden : top, columns].astype(jnp.float32)
        for step in range(1, NX):
            right_down = right_down + factors[step, 2 * hidden : top, columns].astype(jnp.float32)
        out_ref[3 * example] = sides[:rank, :rank]
        out_ref[3 * example + 1] = sides[rank:, rank:]
        out_ref[3 * example + 2] = dot32(
            total[example, NX * hidden :], right_down, ((1,), (1,)), precision=lax.Precision.HIGHEST
        )


def tail_stage(down_weight, gate_out, up_out, down_out, right, messages, far, swaps, blocks, far_block):
    hidden, model_width = down_weight.shape
    rank = gate_out.shape[0]
    examples, _, seq_dev = blocks[0].shape
    width = model_width // NX
    operands = [down_weight, gate_out, up_out, down_out, right, *messages, *far, *swaps, *blocks, *far_block]
    return pl.pallas_call(
        tail_kernel,
        out_shape=jax.ShapeDtypeStruct((examples * 3, rank, rank), jnp.float32),
        in_specs=[HBM] * len(operands),
        out_specs=VMEM,
        scratch_shapes=[
            pltpu.VMEM((NX * hidden + rank, width), jnp.bfloat16),
            pltpu.VMEM((2 * rank, NX * hidden), jnp.bfloat16),
            pltpu.VMEM((NX - 1, FOLD, examples * seq_dev), jnp.bfloat16),
            pltpu.VMEM((examples, width, seq_dev), jnp.bfloat16),
            pltpu.VMEM((NX, 2 * hidden + rank, examples * seq_dev), jnp.bfloat16),
            pltpu.VMEM(right.shape, jnp.float32),
            pltpu.VMEM((examples, NX * hidden + rank, seq_dev), jnp.float32),
            pltpu.SemaphoreType.DMA((2 + 2 * (NX - 1) + (NZ + 1) * NY + 2 + 2 * NX + 2,)),
        ],
        compiler_params=pltpu.CompilerParams(vmem_limit_bytes=62 * MIB),
        cost_estimate=pl.CostEstimate(flops=4 * 10**9, bytes_accessed=8 * MIB, transcendentals=0),
        name="tail_stage",
    )(*operands)


def cut_kernel(up_ref, down_ref, first_ref, second_ref):
    first_ref[...] = up_ref[: first_ref.shape[0]]
    second_ref[...] = down_ref[first_ref.shape[0] :]


def cut(up, down):
    shape = jax.ShapeDtypeStruct((up.shape[0] // 2,) + up.shape[1:], up.dtype)
    return pl.pallas_call(
        cut_kernel,
        out_shape=[shape] * 2,
        in_specs=[VMEM] * 2,
        out_specs=[VMEM] * 2,
        compiler_params=pltpu.CompilerParams(vmem_limit_bytes=4 * MIB),
        name="cut",
    )(up, down)


def ring_z(own):
    up, down = [own], [own]
    for _ in range(NZ // 2 - 1):
        up.append(lax.ppermute(up[-1], "z", shifted(NZ, -1)))
        down.append(lax.ppermute(down[-1], "z", shifted(NZ, 1)))
    first, second = cut(up[-1], down[-1])
    far = [lax.ppermute(first, "z", shifted(NZ, -1)), lax.ppermute(second, "z", shifted(NZ, 1))]
    return up + down[:0:-1], far


def sum_everywhere(partial):
    count, size = partial.shape
    parts = SEQ_PARTS[0] * SEQ_PARTS[1] * NZ
    width = size // parts
    pieces = partial.reshape(count, parts, width).transpose(1, 0, 2)
    pieces = lax.all_to_all(pieces, ("sy", "sc", "z"), 0, 0, tiled=True)
    own = jnp.sum(pieces, axis=0)
    spread = jnp.broadcast_to(own[None], (NX * NZ * NY,) + own.shape)
    blocks = lax.all_to_all(spread, ("x", "z", "yh"), 0, 0, tiled=True)
    blocks = blocks.reshape(NX, NZ, NY, count, width).sum(axis=(0, 2))
    return blocks.transpose(1, 0, 2).reshape(count, NZ * width)


def shards(
    tokens,
    out_grad,
    gate_weight,
    up_weight,
    down_weight,
    proj_gate_in,
    proj_gate_out,
    proj_up_in,
    proj_up_out,
    proj_down_in,
    proj_down_out,
    lengths,
):
    examples, seq_dev, model_width = tokens.shape
    scale = float(seq_dev * SEQ_PARTS[0] * SEQ_PARTS[1]) ** (-0.5)
    gate_out, up_out = proj_gate_out.T, proj_up_out.T

    own_grad = out_grad.transpose(0, 2, 1)
    other_grad = lax.ppermute(own_grad, "yh", shifted(NY, 1))
    flat_tokens = tokens.reshape(examples * seq_dev, model_width)
    sent = token_stage(
        flat_tokens,
        gate_weight,
        up_weight,
        proj_gate_in.T,
        proj_up_in.T,
        proj_down_in.T,
        down_weight,
        gate_out,
        up_out,
        lengths,
        scale,
    )
    sent, right = sent[: NX - 1], sent[NX - 1]
    pair, sent = pair_up(own_grad, other_grad, sent)
    messages = [sent[0]] + [lax.ppermute(piece, "x", shifted(NX, step)) for step, piece in enumerate(sent, 1)]
    hidden, rank = gate_weight.shape[1], gate_out.shape[0]
    first, second, swap = halves(messages[1], messages[3], hidden + rank // 2, hidden // 2)
    far = [lax.ppermute(first, "x", shifted(NX, 1)), lax.ppermute(second, "x", shifted(NX, -1))]
    swaps = [lax.ppermute(piece, "sc", shifted(SEQ_PARTS[1], 1)) for piece in (swap, messages[2])]
    blocks, far_block = ring_z(pair)
    products = tail_stage(down_weight, gate_out, up_out, proj_down_out.T, right, messages, far, swaps, blocks, far_block)
    total = sum_everywhere(products.reshape(examples * 3, -1))
    return total.reshape(examples, 3, -1)


def solution(mesh):
    fine = Mesh(mesh.devices.reshape(SEQ_PARTS + FSDP_PARTS), ("sy", "sc", "x", "z", "yh"))
    seq, fsdp = ("sy", "sc"), ("x", "z", "yh")
    placed = (
        P(None, seq, None),
        P(None, seq, fsdp),
        P(None, fsdp),
        P(None, fsdp),
        P(fsdp, None),
        P(),
        P(fsdp, None),
        P(),
        P(fsdp, None),
        P(fsdp, None),
        P(),
        P(),
    )
    return jax.shard_map(
        shards, mesh=fine, in_specs=placed, out_specs=P(None, None, seq), check_vma=False
    )
```

```python
import jax
import jax.numpy as jnp
from jax import lax
from jax.experimental import pallas as pl
from jax.experimental.pallas import tpu as pltpu
from jax.sharding import Mesh, PartitionSpec as P

SEQ_PARTS = (2, 2)
FSDP_PARTS = (4, 8, 2)
NX, NZ, NY = FSDP_PARTS
FOLD = 16
MIB = 1024 * 1024
VMEM = pl.BlockSpec(memory_space=pltpu.VMEM)
HBM = pl.BlockSpec(memory_space=pltpu.HBM)


def shifted(count, step):
    return [(i, (i + step) % count) for i in range(count)]


def dot32(a, b, dims, precision=None):
    return lax.dot_general(a, b, (dims, ((), ())), preferred_element_type=jnp.float32, precision=precision)


def pair_kernel(own_ref, other_ref, *refs):
    out_ref = refs[-1]
    piece = own_ref.shape[1]
    out_ref[:, :piece, :] = own_ref[...]
    out_ref[:, piece:, :] = other_ref[...]


def pair_up(own, other, messages):
    examples, piece, seq_dev = own.shape
    *messages, pair = pl.pallas_call(
        pair_kernel,
        out_shape=[
            *[jax.ShapeDtypeStruct(message.shape, message.dtype) for message in messages],
            jax.ShapeDtypeStruct((examples, NY * piece, seq_dev), own.dtype),
        ],
        in_specs=[VMEM, VMEM] + [HBM] * len(messages),
        out_specs=[HBM] * len(messages) + [VMEM],
        input_output_aliases={2 + index: index for index in range(len(messages))},
        compiler_params=pltpu.CompilerParams(vmem_limit_bytes=62 * MIB),
        name="pair_up",
    )(own, other, *messages)
    return pair, messages


def token_kernel(chunk, scale, lengths_ref, tokens_hbm, gate_hbm, up_hbm, gate_in_hbm, up_in_hbm, down_in_hbm, down_hbm, gate_out_hbm, up_out_hbm, *refs):
    messages, right_ref = refs[: NX - 1], refs[NX - 1]
    tokens_ref, weight_ref, in_ref, down_in_ref, out_ref, total_ref, sems = refs[NX:]
    rows, model_width = tokens_hbm.shape
    hidden = gate_hbm.shape[1]
    rank = gate_in_hbm.shape[0]
    examples = lengths_ref.shape[0]
    seq_dev = rows // examples
    groups, count = [], 0
    for start in range(0, model_width, chunk):
        part = pl.ds(start, chunk)
        pairs = [
            (tokens_hbm.at[:, part], tokens_ref.at[:, part]),
            (gate_hbm.at[part], weight_ref.at[part, pl.ds(0, hidden)]),
            (up_hbm.at[part], weight_ref.at[part, pl.ds(hidden, hidden)]),
            (gate_in_hbm.at[:, part], in_ref.at[pl.ds(0, rank), part]),
            (up_in_hbm.at[:, part], in_ref.at[pl.ds(rank, rank), part]),
        ]
        if start + chunk == model_width:
            pairs.append((down_in_hbm, down_in_ref))
        groups.append([pltpu.make_async_copy(a, b, sems.at[count + k]) for k, (a, b) in enumerate(pairs)])
        count += len(pairs)
        for copy in groups[-1]:
            copy.start()
    top = 2 * hidden + rank
    width, half = model_width // NX, hidden // 2
    core = lax.axis_index("sc")
    pairs = [(gate_out_hbm, out_ref.at[pl.ds(0, rank)]), (up_out_hbm, out_ref.at[pl.ds(rank, rank)])]
    for step, message in enumerate(messages, 1):
        start = pl.multiple_of(lax.rem(lax.axis_index("x") + step, NX) * width, width)
        columns = pl.ds(start, width)
        if step == 2:
            pairs.append((down_hbm.at[:, columns], message.at[pl.ds(0, hidden)]))
        else:
            pairs.append((down_hbm.at[pl.ds(core * half, half), columns], message.at[pl.ds(top, half)]))
    extra = [pltpu.make_async_copy(a, b, sems.at[count + k]) for k, (a, b) in enumerate(pairs)]
    for copy in extra:
        copy.start()
    for index, group in enumerate(groups):
        for copy in group:
            copy.wait()
        part = slice(index * chunk, (index + 1) * chunk)
        values = jnp.dot(tokens_ref[:, part], weight_ref[part, :], preferred_element_type=jnp.float32)
        right = dot32(tokens_ref[:, part], in_ref[:, part], ((1,), (1,)))
        if index == 0:
            total_ref[...] = values
            right_ref[...] = right
        else:
            total_ref[...] += values
            right_ref[...] += right

    tile = min(256, seq_dev)
    seq_index = lax.axis_index("sy") * SEQ_PARTS[1] + lax.axis_index("sc")
    for step in range(rows // tile):
        span = slice(step * tile, (step + 1) * tile)
        gate, up = total_ref[span, :hidden], total_ref[span, hidden:]
        sigmoid = 1.0 / (1.0 + jnp.exp(-gate))
        silu = gate * sigmoid
        factor_gate = up * sigmoid * (1.0 + gate * (1.0 - sigmoid))
        hidden_value = (silu * up).astype(jnp.bfloat16)
        factor_gate = factor_gate.T.astype(jnp.bfloat16)
        factor_up = silu.T.astype(jnp.bfloat16)

        first = seq_index * seq_dev + step * tile % seq_dev
        limit = lengths_ref[step * tile // seq_dev]
        columns = first + lax.broadcasted_iota(jnp.int32, (rank, tile), 1)
        right_down = dot32(down_in_ref[...], hidden_value, ((1,), (1,)))
        right_down = jnp.where(columns < limit, right_down * scale, 0.0).astype(jnp.bfloat16)
        for message in messages[::2]:
            message[:hidden, span] = factor_gate
            message[hidden : 2 * hidden, span] = factor_up
            message[2 * hidden : top, span] = right_down
        rows_at = first + lax.broadcasted_iota(jnp.int32, (tile, 2 * rank), 0)
        right_ref[span, :] = jnp.where(rows_at < limit, right_ref[span, :] * scale, 0.0)
    for copy in extra:
        copy.wait()
    for message in messages:
        for block in range(2 * rank // FOLD):
            rows_of = slice(block * FOLD, (block + 1) * FOLD)
            message[-FOLD:, block * hidden : (block + 1) * hidden] = out_ref[rows_of, :]


def token_stage(tokens, gate_weight, up_weight, gate_in, up_in, down_in, down_weight, gate_out, up_out, lengths, scale):
    rows, width = tokens.shape
    hidden = gate_weight.shape[1]
    rank = gate_in.shape[0]
    chunk = 512
    return pl.pallas_call(
        lambda *refs: token_kernel(chunk, scale, *refs),
        out_shape=[
            jax.ShapeDtypeStruct((2 * hidden + hidden // 2 + rank + FOLD, rows), jnp.bfloat16),
            jax.ShapeDtypeStruct((hidden + FOLD, rows), jnp.bfloat16),
            jax.ShapeDtypeStruct((2 * hidden + hidden // 2 + rank + FOLD, rows), jnp.bfloat16),
            jax.ShapeDtypeStruct((rows, 2 * rank), jnp.float32),
        ],
        in_specs=[pl.BlockSpec(memory_space=pltpu.SMEM)] + [HBM] * 9,
        out_specs=[VMEM] * NX,
        scratch_shapes=[
            pltpu.VMEM((rows, width), jnp.bfloat16),
            pltpu.VMEM((width, 2 * hidden), jnp.bfloat16),
            pltpu.VMEM((2 * rank, width), jnp.bfloat16),
            pltpu.VMEM((rank, hidden), jnp.bfloat16),
            pltpu.VMEM((2 * rank, hidden), jnp.bfloat16),
            pltpu.VMEM((rows, 2 * hidden), jnp.float32),
            pltpu.SemaphoreType.DMA((5 * (width // chunk) + 2 + NX,)),
        ],
        compiler_params=pltpu.CompilerParams(vmem_limit_bytes=61 * MIB),
        cost_estimate=pl.CostEstimate(
            flops=2 * rows * width * 512, bytes_accessed=16 * MIB, transcendentals=rows * hidden
        ),
        name="token_stage",
    )(lengths, tokens, gate_weight, up_weight, gate_in, up_in, down_in, down_weight, gate_out, up_out)


def forward_kernel(before_ref, after_ref, first_ref, second_ref, swap_ref):
    rows = first_ref.shape[0]
    half = swap_ref.shape[0] // 2
    first_ref[...] = before_ref[:rows, :]
    second_ref[...] = after_ref[rows : 2 * rows, :]
    swap_ref[:half, :] = before_ref[2 * rows : 2 * rows + half, :]
    swap_ref[half:, :] = after_ref[2 * rows : 2 * rows + half, :]


def halves(before, after, rows, half):
    shape = jax.ShapeDtypeStruct((rows, before.shape[1]), before.dtype)
    swap = jax.ShapeDtypeStruct((2 * half, before.shape[1]), before.dtype)
    return pl.pallas_call(
        forward_kernel,
        out_shape=[shape, shape, swap],
        in_specs=[VMEM] * 2,
        out_specs=[VMEM] * 3,
        compiler_params=pltpu.CompilerParams(vmem_limit_bytes=8 * MIB),
        name="halves",
    )(before, after)


def keep_kernel(message_ref, right_ref, pair_ref, factors_out, right_out, pair_out):
    factors_out[...] = message_ref[: factors_out.shape[0], :]
    right_out[...] = right_ref[...]
    pair_out[...] = pair_ref[...]


def keep(message, right, pair, rows):
    return pl.pallas_call(
        keep_kernel,
        out_shape=[
            jax.ShapeDtypeStruct((rows, message.shape[1]), message.dtype),
            jax.ShapeDtypeStruct(right.shape, right.dtype),
            jax.ShapeDtypeStruct(pair.shape, pair.dtype),
        ],
        in_specs=[VMEM] * 3,
        out_specs=[VMEM] * 3,
        compiler_params=pltpu.CompilerParams(vmem_limit_bytes=8 * MIB),
        name="keep",
    )(message, right, pair)


def tail_kernel(weight_ref, gate_out_ref, up_out_ref, down_out_ref, right_ref, *refs):
    own_ref, messages, far_halves, swap_ref = refs[0], refs[1:NX], refs[NX : NX + 2], refs[NX + 2]
    blocks, far_block = refs[NX + 3 : NX + 2 + NZ], refs[NX + 2 + NZ : NX + 4 + NZ]
    out_ref, weights, projs, grads = refs[NX + 4 + NZ :]
    hidden, model_width = weight_ref.shape
    rank = gate_out_ref.shape[0]
    width = model_width // NX
    examples, both, seq_dev = blocks[0].shape
    piece = both // NY
    top, half, core = 2 * hidden + rank, hidden // 2, lax.axis_index("sc")
    x_at, z_at, y_at = lax.axis_index("x"), lax.axis_index("z"), lax.axis_index("yh")

    start = pl.multiple_of(x_at * width, width)
    weights[:hidden, :] = weight_ref[:, pl.ds(start, width)]
    weights[NX * hidden :, :] = down_out_ref[:, pl.ds(start, width)]
    projs[:rank, :hidden] = gate_out_ref[...]
    projs[rank:, :hidden] = up_out_ref[...]
    for step, message in enumerate(messages, 1):
        if step == 2:
            weights[step * hidden : (step + 1) * hidden, :] = message[:hidden, :]
        else:
            mine = pl.ds(pl.multiple_of(step * hidden + core * half, half), half)
            theirs = pl.ds(pl.multiple_of(step * hidden + (1 - core) * half, half), half)
            weights[mine, :] = message[top : top + half, :]
            weights[theirs, :] = swap_ref[step // 2 * half : (step // 2 + 1) * half, :]
        columns = slice(step * hidden, (step + 1) * hidden)
        for block in range(2 * rank // FOLD):
            folded = message[-FOLD:, block * hidden : (block + 1) * hidden]
            projs[block * FOLD : (block + 1) * FOLD, columns] = folded

    def factor_rows(step, first, last, columns):
        if step != 2:
            return (own_ref if step == 0 else messages[step - 1])[first:last, columns]
        rows = far_halves[0].shape[0]
        parts = [far_halves[0][first : min(last, rows), columns]] if first < rows else []
        if last > rows:
            parts.append(far_halves[1][max(first - rows, 0) : last - rows, columns])
        return jnp.concatenate(parts, axis=0)

    for example in range(examples):
        for step in range(NZ):
            if step == NZ // 2:
                count = examples // 2
                block = far_block[example // count][example % count]
            else:
                block = blocks[step if step < NZ // 2 else step - 1][example]
            base = lax.rem(z_at + step, NZ) * both
            for kind, y_of in enumerate((y_at, 1 - y_at)):
                rows = pl.ds(pl.multiple_of(base + y_of * piece, piece), piece)
                grads[rows, :] = block[kind * piece : (kind + 1) * piece]
        columns = slice(example * seq_dev, (example + 1) * seq_dev)
        total = jnp.dot(weights[...], grads[...], preferred_element_type=jnp.float32)
        left = []
        for kind in range(2):
            factor = jnp.concatenate(
                [factor_rows(step, kind * hidden, (kind + 1) * hidden, columns) for step in range(NX)], axis=0
            )
            product = total[: NX * hidden] * factor.astype(jnp.float32)
            high = product.astype(jnp.bfloat16)
            low = (product - high.astype(jnp.float32)).astype(jnp.bfloat16)
            proj = projs[kind * rank : (kind + 1) * rank, :]
            left.append(
                jnp.dot(proj, high, preferred_element_type=jnp.float32)
                + jnp.dot(proj, low, preferred_element_type=jnp.float32)
            )
        sides = jnp.dot(
            jnp.concatenate(left, axis=0),
            right_ref[columns, :],
            precision=lax.Precision.HIGHEST,
            preferred_element_type=jnp.float32,
        )
        right_down = factor_rows(0, 2 * hidden, top, columns).astype(jnp.float32)
        for step in range(1, NX):
            right_down = right_down + factor_rows(step, 2 * hidden, top, columns).astype(jnp.float32)
        out_ref[3 * example] = sides[:rank, :rank]
        out_ref[3 * example + 1] = sides[rank:, rank:]
        out_ref[3 * example + 2] = dot32(
            total[NX * hidden :], right_down, ((1,), (1,)), precision=lax.Precision.HIGHEST
        )


def tail_stage(down_weight, gate_out, up_out, down_out, right, factors, messages, far, swap, blocks, far_block):
    hidden, model_width = down_weight.shape
    rank = gate_out.shape[0]
    examples, _, seq_dev = blocks[0].shape
    width = model_width // NX
    operands = [down_weight, gate_out, up_out, down_out, right, factors, *messages, *far, swap, *blocks, *far_block]
    return pl.pallas_call(
        tail_kernel,
        out_shape=jax.ShapeDtypeStruct((examples * 3, rank, rank), jnp.float32),
        in_specs=[VMEM] * len(operands),
        out_specs=VMEM,
        scratch_shapes=[
            pltpu.VMEM((NX * hidden + rank, width), jnp.bfloat16),
            pltpu.VMEM((2 * rank, NX * hidden), jnp.bfloat16),
            pltpu.VMEM((width, seq_dev), jnp.bfloat16),
        ],
        compiler_params=pltpu.CompilerParams(vmem_limit_bytes=20 * MIB),
        cost_estimate=pl.CostEstimate(flops=4 * 10**9, bytes_accessed=8 * MIB, transcendentals=0),
        name="tail_stage",
    )(*operands)


def cut_kernel(up_ref, down_ref, first_ref, second_ref):
    first_ref[...] = up_ref[: first_ref.shape[0]]
    second_ref[...] = down_ref[first_ref.shape[0] :]


def cut(up, down):
    shape = jax.ShapeDtypeStruct((up.shape[0] // 2,) + up.shape[1:], up.dtype)
    return pl.pallas_call(
        cut_kernel,
        out_shape=[shape] * 2,
        in_specs=[VMEM] * 2,
        out_specs=[VMEM] * 2,
        compiler_params=pltpu.CompilerParams(vmem_limit_bytes=4 * MIB),
        name="cut",
    )(up, down)


def ring_z(own):
    up, down = [own], [own]
    for _ in range(NZ // 2 - 1):
        up.append(lax.ppermute(up[-1], "z", shifted(NZ, -1)))
        down.append(lax.ppermute(down[-1], "z", shifted(NZ, 1)))
    first, second = cut(up[-1], down[-1])
    far = [lax.ppermute(first, "z", shifted(NZ, -1)), lax.ppermute(second, "z", shifted(NZ, 1))]
    return up + down[:0:-1], far


def sum_everywhere(partial):
    count, size = partial.shape
    parts = SEQ_PARTS[0] * SEQ_PARTS[1] * NZ
    width = size // parts
    pieces = partial.reshape(count, parts, width).transpose(1, 0, 2)
    pieces = lax.all_to_all(pieces, ("sy", "sc", "z"), 0, 0, tiled=True)
    own = jnp.sum(pieces, axis=0)
    spread = jnp.broadcast_to(own[None], (NX * NZ * NY,) + own.shape)
    blocks = lax.all_to_all(spread, ("x", "z", "yh"), 0, 0, tiled=True)
    blocks = blocks.reshape(NX, NZ, NY, count, width).sum(axis=(0, 2))
    return blocks.transpose(1, 0, 2).reshape(count, NZ * width)


def shards(
    tokens,
    out_grad,
    gate_weight,
    up_weight,
    down_weight,
    proj_gate_in,
    proj_gate_out,
    proj_up_in,
    proj_up_out,
    proj_down_in,
    proj_down_out,
    lengths,
):
    examples, seq_dev, model_width = tokens.shape
    scale = float(seq_dev * SEQ_PARTS[0] * SEQ_PARTS[1]) ** (-0.5)
    gate_out, up_out = proj_gate_out.T, proj_up_out.T

    own_grad = out_grad.transpose(0, 2, 1)
    other_grad = lax.ppermute(own_grad, "yh", shifted(NY, 1))
    flat_tokens = tokens.reshape(examples * seq_dev, model_width)
    sent = token_stage(
        flat_tokens,
        gate_weight,
        up_weight,
        proj_gate_in.T,
        proj_up_in.T,
        proj_down_in.T,
        down_weight,
        gate_out,
        up_out,
        lengths,
        scale,
    )
    sent, right = sent[: NX - 1], sent[NX - 1]
    pair, sent = pair_up(own_grad, other_grad, sent)
    messages = [lax.ppermute(piece, "x", shifted(NX, step)) for step, piece in enumerate(sent, 1)]
    hidden, rank = gate_weight.shape[1], gate_out.shape[0]
    rows = 2 * hidden + rank
    first, second, swap = halves(messages[0], messages[2], rows // 2, hidden // 2)
    swap = lax.ppermute(swap, "sc", shifted(SEQ_PARTS[1], 1))
    far = [lax.ppermute(first, "x", shifted(NX, 1)), lax.ppermute(second, "x", shifted(NX, -1))]
    blocks, far_block = ring_z(pair)
    factors, right, blocks[0] = keep(sent[0], right, pair, rows)
    products = tail_stage(
        down_weight, gate_out, up_out, proj_down_out.T, right, factors, messages, far, swap, blocks, far_block
    )
    total = sum_everywhere(products.reshape(examples * 3, -1))
    return total.reshape(examples, 3, -1)


def solution(mesh):
    fine = Mesh(mesh.devices.reshape(SEQ_PARTS + FSDP_PARTS), ("sy", "sc", "x", "z", "yh"))
    seq, fsdp = ("sy", "sc"), ("x", "z", "yh")
    placed = (
        P(None, seq, None),
        P(None, seq, fsdp),
        P(None, fsdp),
        P(None, fsdp),
        P(fsdp, None),
        P(),
        P(fsdp, None),
        P(),
        P(fsdp, None),
        P(fsdp, None),
        P(),
        P(),
    )
    return jax.shard_map(
        shards, mesh=fine, in_specs=placed, out_specs=P(None, None, seq), check_vma=False
    )
```

```python
import jax
import jax.numpy as jnp
from jax import lax
from jax.experimental import pallas as pl
from jax.experimental.pallas import tpu as pltpu
from jax.sharding import Mesh, PartitionSpec as P

SEQ_PARTS = (2, 2)
FSDP_PARTS = (4, 8, 2)
NX, NZ, NY = FSDP_PARTS
FOLD = 16
MIB = 1024 * 1024
VMEM = pl.BlockSpec(memory_space=pltpu.VMEM)
HBM = pl.BlockSpec(memory_space=pltpu.HBM)


def shifted(count, step):
    return [(i, (i + step) % count) for i in range(count)]


def dot32(a, b, dims, precision=None):
    return lax.dot_general(a, b, (dims, ((), ())), preferred_element_type=jnp.float32, precision=precision)


def pair_kernel(other_hbm, own_hbm, *refs):
    out_ref, sem = refs[-2:]
    piece = other_hbm.shape[1]
    copy = pltpu.make_async_copy(other_hbm, out_ref.at[:, pl.ds(piece, piece)], sem)
    copy.start()
    copy.wait()


def pair_up(pair, other, messages):
    arrays = [pair, *messages]
    *messages, pair = pl.pallas_call(
        pair_kernel,
        out_shape=[jax.ShapeDtypeStruct(array.shape, array.dtype) for array in [*messages, pair]],
        in_specs=[HBM] * (1 + len(arrays)),
        out_specs=[HBM] * len(arrays),
        scratch_shapes=[pltpu.SemaphoreType.DMA],
        input_output_aliases={1: len(messages)} | {2 + index: index for index in range(len(messages))},
        compiler_params=pltpu.CompilerParams(vmem_limit_bytes=62 * MIB),
        name="pair_up",
    )(other, *arrays)
    return pair, messages


def token_kernel(chunk, scale, lengths_ref, tokens_hbm, gate_hbm, up_hbm, gate_in_hbm, up_in_hbm, down_in_hbm, down_hbm, gate_out_hbm, up_out_hbm, grad_hbm, *refs):
    messages, (right_ref, pair_ref) = refs[: NX - 1], refs[NX - 1 : NX + 1]
    tokens_ref, weight_ref, in_ref, down_in_ref, out_ref, total_ref, sems = refs[NX + 1 :]
    rows, model_width = tokens_hbm.shape
    hidden = gate_hbm.shape[1]
    rank = gate_in_hbm.shape[0]
    examples = lengths_ref.shape[0]
    seq_dev = rows // examples
    groups, count = [], 0
    for start in range(0, model_width, chunk):
        part = pl.ds(start, chunk)
        pairs = [
            (tokens_hbm.at[:, part], tokens_ref.at[:, part]),
            (gate_hbm.at[part], weight_ref.at[part, pl.ds(0, hidden)]),
            (up_hbm.at[part], weight_ref.at[part, pl.ds(hidden, hidden)]),
            (gate_in_hbm.at[:, part], in_ref.at[pl.ds(0, rank), part]),
            (up_in_hbm.at[:, part], in_ref.at[pl.ds(rank, rank), part]),
        ]
        if start + chunk == model_width:
            pairs.append((down_in_hbm, down_in_ref))
        groups.append([pltpu.make_async_copy(a, b, sems.at[count + k]) for k, (a, b) in enumerate(pairs)])
        count += len(pairs)
        for copy in groups[-1]:
            copy.start()
    top = 2 * hidden + rank
    width, half = model_width // NX, hidden // 2
    core = lax.axis_index("sc")
    pairs = [(gate_out_hbm, out_ref.at[pl.ds(0, rank)]), (up_out_hbm, out_ref.at[pl.ds(rank, rank)])]
    pairs.append((grad_hbm, pair_ref.at[:, pl.ds(0, grad_hbm.shape[1])]))
    for step, message in enumerate(messages, 1):
        start = pl.multiple_of(lax.rem(lax.axis_index("x") + step, NX) * width, width)
        bottom = message.shape[0] - half - FOLD
        pairs.append((down_hbm.at[pl.ds(core * half, half), pl.ds(start, width)], message.at[pl.ds(bottom, half)]))
    extra = [pltpu.make_async_copy(a, b, sems.at[count + k]) for k, (a, b) in enumerate(pairs)]
    for copy in extra:
        copy.start()
    for index, group in enumerate(groups):
        for copy in group:
            copy.wait()
        part = slice(index * chunk, (index + 1) * chunk)
        values = jnp.dot(tokens_ref[:, part], weight_ref[part, :], preferred_element_type=jnp.float32)
        right = dot32(tokens_ref[:, part], in_ref[:, part], ((1,), (1,)))
        if index == 0:
            total_ref[...] = values
            right_ref[...] = right
        else:
            total_ref[...] += values
            right_ref[...] += right

    tile = min(256, seq_dev)
    seq_index = lax.axis_index("sy") * SEQ_PARTS[1] + lax.axis_index("sc")
    for step in range(rows // tile):
        span = slice(step * tile, (step + 1) * tile)
        gate, up = total_ref[span, :hidden], total_ref[span, hidden:]
        sigmoid = 1.0 / (1.0 + jnp.exp(-gate))
        silu = gate * sigmoid
        factor_gate = up * sigmoid * (1.0 + gate * (1.0 - sigmoid))
        hidden_value = (silu * up).astype(jnp.bfloat16)
        factor_gate = factor_gate.T.astype(jnp.bfloat16)
        factor_up = silu.T.astype(jnp.bfloat16)

        first = seq_index * seq_dev + step * tile % seq_dev
        limit = lengths_ref[step * tile // seq_dev]
        columns = first + lax.broadcasted_iota(jnp.int32, (rank, tile), 1)
        right_down = dot32(down_in_ref[...], hidden_value, ((1,), (1,)))
        right_down = jnp.where(columns < limit, right_down * scale, 0.0).astype(jnp.bfloat16)
        for message in messages[::2]:
            message[:hidden, span] = factor_gate
            message[hidden : 2 * hidden, span] = factor_up
            message[2 * hidden : top, span] = right_down
        rows_at = first + lax.broadcasted_iota(jnp.int32, (tile, 2 * rank), 0)
        right_ref[span, :] = jnp.where(rows_at < limit, right_ref[span, :] * scale, 0.0)
    for copy in extra:
        copy.wait()
    for message in messages:
        for block in range(2 * rank // FOLD):
            rows_of = slice(block * FOLD, (block + 1) * FOLD)
            message[-FOLD:, block * hidden : (block + 1) * hidden] = out_ref[rows_of, :]


def token_stage(tokens, gate_weight, up_weight, gate_in, up_in, down_in, down_weight, gate_out, up_out, own_grad, lengths, scale):
    rows, width = tokens.shape
    hidden = gate_weight.shape[1]
    rank = gate_in.shape[0]
    chunk = 512
    return pl.pallas_call(
        lambda *refs: token_kernel(chunk, scale, *refs),
        out_shape=[
            jax.ShapeDtypeStruct((2 * hidden + hidden // 2 + rank + FOLD, rows), jnp.bfloat16),
            jax.ShapeDtypeStruct((hidden // 2 + FOLD, rows), jnp.bfloat16),
            jax.ShapeDtypeStruct((2 * hidden + hidden // 2 + rank + FOLD, rows), jnp.bfloat16),
            jax.ShapeDtypeStruct((rows, 2 * rank), jnp.float32),
            jax.ShapeDtypeStruct((own_grad.shape[0], NY * own_grad.shape[1], own_grad.shape[2]), own_grad.dtype),
        ],
        in_specs=[pl.BlockSpec(memory_space=pltpu.SMEM)] + [HBM] * 10,
        out_specs=[VMEM] * NX + [HBM],
        scratch_shapes=[
            pltpu.VMEM((rows, width), jnp.bfloat16),
            pltpu.VMEM((width, 2 * hidden), jnp.bfloat16),
            pltpu.VMEM((2 * rank, width), jnp.bfloat16),
            pltpu.VMEM((rank, hidden), jnp.bfloat16),
            pltpu.VMEM((2 * rank, hidden), jnp.bfloat16),
            pltpu.VMEM((rows, 2 * hidden), jnp.float32),
            pltpu.SemaphoreType.DMA((5 * (width // chunk) + 3 + NX,)),
        ],
        compiler_params=pltpu.CompilerParams(vmem_limit_bytes=61 * MIB),
        cost_estimate=pl.CostEstimate(
            flops=2 * rows * width * 512, bytes_accessed=16 * MIB, transcendentals=rows * hidden
        ),
        name="token_stage",
    )(lengths, tokens, gate_weight, up_weight, gate_in, up_in, down_in, down_weight, gate_out, up_out, own_grad)


def forward_kernel(*refs):
    messages, (first_ref, second_ref, swap_ref) = refs[:-3], refs[-3:]
    rows = first_ref.shape[0]
    half = swap_ref.shape[0] // len(messages)
    first_ref[...] = messages[0][:rows, :]
    second_ref[...] = messages[-1][rows : 2 * rows, :]
    for index, message in enumerate(messages):
        bottom = message.shape[0] - half - FOLD
        swap_ref[index * half : (index + 1) * half, :] = message[bottom : bottom + half, :]


def halves(messages, rows, half):
    columns = messages[0].shape[1]
    shape = jax.ShapeDtypeStruct((rows, columns), messages[0].dtype)
    swap = jax.ShapeDtypeStruct((len(messages) * half, columns), messages[0].dtype)
    return pl.pallas_call(
        forward_kernel,
        out_shape=[shape, shape, swap],
        in_specs=[VMEM] * len(messages),
        out_specs=[VMEM] * 3,
        compiler_params=pltpu.CompilerParams(vmem_limit_bytes=8 * MIB),
        name="halves",
    )(*messages)


def keep_kernel(message_ref, right_ref, pair_ref, factors_out, right_out, pair_out):
    factors_out[...] = message_ref[: factors_out.shape[0], :]
    right_out[...] = right_ref[...]
    pair_out[...] = pair_ref[...]


def keep(message, right, pair, rows):
    return pl.pallas_call(
        keep_kernel,
        out_shape=[
            jax.ShapeDtypeStruct((rows, message.shape[1]), message.dtype),
            jax.ShapeDtypeStruct(right.shape, right.dtype),
            jax.ShapeDtypeStruct(pair.shape, pair.dtype),
        ],
        in_specs=[VMEM] * 3,
        out_specs=[VMEM] * 3,
        compiler_params=pltpu.CompilerParams(vmem_limit_bytes=8 * MIB),
        name="keep",
    )(message, right, pair)


def tail_kernel(weight_ref, gate_out_ref, up_out_ref, down_out_ref, right_ref, *refs):
    own_ref, messages, far_halves, swap_ref = refs[0], refs[1:NX], refs[NX : NX + 2], refs[NX + 2]
    blocks, far_block = refs[NX + 3 : NX + 2 + NZ], refs[NX + 2 + NZ : NX + 4 + NZ]
    out_ref, weights, projs, grads = refs[NX + 4 + NZ :]
    hidden, model_width = weight_ref.shape
    rank = gate_out_ref.shape[0]
    width = model_width // NX
    examples, both, seq_dev = blocks[0].shape
    piece = both // NY
    top, half, core = 2 * hidden + rank, hidden // 2, lax.axis_index("sc")
    x_at, z_at, y_at = lax.axis_index("x"), lax.axis_index("z"), lax.axis_index("yh")

    start = pl.multiple_of(x_at * width, width)
    weights[:hidden, :] = weight_ref[:, pl.ds(start, width)]
    weights[NX * hidden :, :] = down_out_ref[:, pl.ds(start, width)]
    projs[:rank, :hidden] = gate_out_ref[...]
    projs[rank:, :hidden] = up_out_ref[...]
    for step, message in enumerate(messages, 1):
        bottom = message.shape[0] - half - FOLD
        mine = pl.ds(pl.multiple_of(step * hidden + core * half, half), half)
        theirs = pl.ds(pl.multiple_of(step * hidden + (1 - core) * half, half), half)
        weights[mine, :] = message[bottom : bottom + half, :]
        weights[theirs, :] = swap_ref[(step - 1) * half : step * half, :]
        columns = slice(step * hidden, (step + 1) * hidden)
        for block in range(2 * rank // FOLD):
            folded = message[-FOLD:, block * hidden : (block + 1) * hidden]
            projs[block * FOLD : (block + 1) * FOLD, columns] = folded

    def factor_rows(step, first, last, columns):
        if step != 2:
            return (own_ref if step == 0 else messages[step - 1])[first:last, columns]
        rows = far_halves[0].shape[0]
        parts = [far_halves[0][first : min(last, rows), columns]] if first < rows else []
        if last > rows:
            parts.append(far_halves[1][max(first - rows, 0) : last - rows, columns])
        return jnp.concatenate(parts, axis=0)

    for example in range(examples):
        for step in range(NZ):
            if step == NZ // 2:
                count = examples // 2
                block = far_block[example // count][example % count]
            else:
                block = blocks[step if step < NZ // 2 else step - 1][example]
            base = lax.rem(z_at + step, NZ) * both
            for kind, y_of in enumerate((y_at, 1 - y_at)):
                rows = pl.ds(pl.multiple_of(base + y_of * piece, piece), piece)
                grads[rows, :] = block[kind * piece : (kind + 1) * piece]
        columns = slice(example * seq_dev, (example + 1) * seq_dev)
        total = jnp.dot(weights[...], grads[...], preferred_element_type=jnp.float32)
        left = []
        for kind in range(2):
            factor = jnp.concatenate(
                [factor_rows(step, kind * hidden, (kind + 1) * hidden, columns) for step in range(NX)], axis=0
            )
            product = total[: NX * hidden] * factor.astype(jnp.float32)
            high = product.astype(jnp.bfloat16)
            low = (product - high.astype(jnp.float32)).astype(jnp.bfloat16)
            proj = projs[kind * rank : (kind + 1) * rank, :]
            left.append(
                jnp.dot(proj, high, preferred_element_type=jnp.float32)
                + jnp.dot(proj, low, preferred_element_type=jnp.float32)
            )
        sides = jnp.dot(
            jnp.concatenate(left, axis=0),
            right_ref[columns, :],
            precision=lax.Precision.HIGHEST,
            preferred_element_type=jnp.float32,
        )
        right_down = factor_rows(0, 2 * hidden, top, columns).astype(jnp.float32)
        for step in range(1, NX):
            right_down = right_down + factor_rows(step, 2 * hidden, top, columns).astype(jnp.float32)
        out_ref[3 * example] = sides[:rank, :rank]
        out_ref[3 * example + 1] = sides[rank:, rank:]
        out_ref[3 * example + 2] = dot32(
            total[NX * hidden :], right_down, ((1,), (1,)), precision=lax.Precision.HIGHEST
        )


def tail_stage(down_weight, gate_out, up_out, down_out, right, factors, messages, far, swap, blocks, far_block):
    hidden, model_width = down_weight.shape
    rank = gate_out.shape[0]
    examples, _, seq_dev = blocks[0].shape
    width = model_width // NX
    operands = [down_weight, gate_out, up_out, down_out, right, factors, *messages, *far, swap, *blocks, *far_block]
    return pl.pallas_call(
        tail_kernel,
        out_shape=jax.ShapeDtypeStruct((examples * 3, rank, rank), jnp.float32),
        in_specs=[VMEM] * len(operands),
        out_specs=VMEM,
        scratch_shapes=[
            pltpu.VMEM((NX * hidden + rank, width), jnp.bfloat16),
            pltpu.VMEM((2 * rank, NX * hidden), jnp.bfloat16),
            pltpu.VMEM((width, seq_dev), jnp.bfloat16),
        ],
        compiler_params=pltpu.CompilerParams(vmem_limit_bytes=20 * MIB),
        cost_estimate=pl.CostEstimate(flops=4 * 10**9, bytes_accessed=8 * MIB, transcendentals=0),
        name="tail_stage",
    )(*operands)


def cut_kernel(up_ref, down_ref, first_ref, second_ref):
    first_ref[...] = up_ref[: first_ref.shape[0]]
    second_ref[...] = down_ref[first_ref.shape[0] :]


def cut(up, down):
    shape = jax.ShapeDtypeStruct((up.shape[0] // 2,) + up.shape[1:], up.dtype)
    return pl.pallas_call(
        cut_kernel,
        out_shape=[shape] * 2,
        in_specs=[VMEM] * 2,
        out_specs=[VMEM] * 2,
        compiler_params=pltpu.CompilerParams(vmem_limit_bytes=4 * MIB),
        name="cut",
    )(up, down)


def ring_z(own):
    up, down = [own], [own]
    for _ in range(NZ // 2 - 1):
        up.append(lax.ppermute(up[-1], "z", shifted(NZ, -1)))
        down.append(lax.ppermute(down[-1], "z", shifted(NZ, 1)))
    first, second = cut(up[-1], down[-1])
    far = [lax.ppermute(first, "z", shifted(NZ, -1)), lax.ppermute(second, "z", shifted(NZ, 1))]
    return up + down[:0:-1], far


def sum_everywhere(partial):
    count, size = partial.shape
    parts = SEQ_PARTS[0] * SEQ_PARTS[1] * NZ
    width = size // parts
    pieces = partial.reshape(count, parts, width).transpose(1, 0, 2)
    pieces = lax.all_to_all(pieces, ("sy", "sc", "z"), 0, 0, tiled=True)
    own = jnp.sum(pieces, axis=0)
    spread = jnp.broadcast_to(own[None], (NX * NZ * NY,) + own.shape)
    blocks = lax.all_to_all(spread, ("x", "z", "yh"), 0, 0, tiled=True)
    blocks = blocks.reshape(NX, NZ, NY, count, width).sum(axis=(0, 2))
    return blocks.transpose(1, 0, 2).reshape(count, NZ * width)


def shards(
    tokens,
    out_grad,
    gate_weight,
    up_weight,
    down_weight,
    proj_gate_in,
    proj_gate_out,
    proj_up_in,
    proj_up_out,
    proj_down_in,
    proj_down_out,
    lengths,
):
    examples, seq_dev, model_width = tokens.shape
    scale = float(seq_dev * SEQ_PARTS[0] * SEQ_PARTS[1]) ** (-0.5)
    gate_out, up_out = proj_gate_out.T, proj_up_out.T

    own_grad = out_grad.transpose(0, 2, 1)
    other_grad = lax.ppermute(own_grad, "yh", shifted(NY, 1))
    flat_tokens = tokens.reshape(examples * seq_dev, model_width)
    sent = token_stage(
        flat_tokens,
        gate_weight,
        up_weight,
        proj_gate_in.T,
        proj_up_in.T,
        proj_down_in.T,
        down_weight,
        gate_out,
        up_out,
        own_grad,
        lengths,
        scale,
    )
    sent, (right, pair) = sent[: NX - 1], sent[NX - 1 :]
    pair, sent = pair_up(pair, other_grad, sent)
    messages = [lax.ppermute(piece, "x", shifted(NX, step)) for step, piece in enumerate(sent, 1)]
    hidden, rank = gate_weight.shape[1], gate_out.shape[0]
    rows = 2 * hidden + rank
    first, second, swap = halves(messages, rows // 2, hidden // 2)
    swap = lax.ppermute(swap, "sc", shifted(SEQ_PARTS[1], 1))
    far = [lax.ppermute(first, "x", shifted(NX, 1)), lax.ppermute(second, "x", shifted(NX, -1))]
    blocks, far_block = ring_z(pair)
    factors, right, blocks[0] = keep(sent[0], right, pair, rows)
    products = tail_stage(
        down_weight, gate_out, up_out, proj_down_out.T, right, factors, messages, far, swap, blocks, far_block
    )
    total = sum_everywhere(products.reshape(examples * 3, -1))
    return total.reshape(examples, 3, -1)


def solution(mesh):
    fine = Mesh(mesh.devices.reshape(SEQ_PARTS + FSDP_PARTS), ("sy", "sc", "x", "z", "yh"))
    seq, fsdp = ("sy", "sc"), ("x", "z", "yh")
    placed = (
        P(None, seq, None),
        P(None, seq, fsdp),
        P(None, fsdp),
        P(None, fsdp),
        P(fsdp, None),
        P(),
        P(fsdp, None),
        P(),
        P(fsdp, None),
        P(fsdp, None),
        P(),
        P(),
    )
    return jax.shard_map(
        shards, mesh=fine, in_specs=placed, out_specs=P(None, None, seq), check_vma=False
    )
```

```python
import jax
import jax.numpy as jnp
from jax import lax
from jax.experimental import pallas as pl
from jax.experimental.pallas import tpu as pltpu
from jax.sharding import Mesh, PartitionSpec as P

SEQ_PARTS = (2, 2)
FSDP_PARTS = (4, 8, 2)
NX, NZ, NY = FSDP_PARTS
FOLD = 16
MIB = 1024 * 1024
VMEM = pl.BlockSpec(memory_space=pltpu.VMEM)
HBM = pl.BlockSpec(memory_space=pltpu.HBM)


def shifted(count, step):
    return [(i, (i + step) % count) for i in range(count)]


def dot32(a, b, dims, precision=None):
    return lax.dot_general(a, b, (dims, ((), ())), preferred_element_type=jnp.float32, precision=precision)


def hold_kernel(*refs):
    pass


def hold(arrays):
    return pl.pallas_call(
        hold_kernel,
        out_shape=[jax.ShapeDtypeStruct(array.shape, array.dtype) for array in arrays],
        in_specs=[HBM] * len(arrays),
        out_specs=[HBM] * len(arrays),
        input_output_aliases={index: index for index in range(len(arrays))},
        compiler_params=pltpu.CompilerParams(vmem_limit_bytes=62 * MIB),
        name="hold",
    )(*arrays)


def pair_kernel(own_ref, other_ref, out_ref):
    piece = own_ref.shape[1]
    out_ref[:, :piece, :] = own_ref[...]
    out_ref[:, piece:, :] = other_ref[...]


def pair_up(own, other):
    examples, piece, seq_dev = own.shape
    return pl.pallas_call(
        pair_kernel,
        out_shape=jax.ShapeDtypeStruct((examples, NY * piece, seq_dev), own.dtype),
        in_specs=[VMEM] * 2,
        out_specs=VMEM,
        compiler_params=pltpu.CompilerParams(vmem_limit_bytes=4 * MIB),
        name="pair_up",
    )(own, other)


def token_kernel(chunk, scale, lengths_ref, tokens_hbm, gate_hbm, up_hbm, gate_in_hbm, up_in_hbm, down_in_hbm, down_hbm, gate_out_hbm, up_out_hbm, *refs):
    messages, right_ref = refs[: NX - 1], refs[NX - 1]
    tokens_ref, weight_ref, in_ref, down_in_ref, out_ref, total_ref, sems = refs[NX:]
    rows, model_width = tokens_hbm.shape
    hidden = gate_hbm.shape[1]
    rank = gate_in_hbm.shape[0]
    examples = lengths_ref.shape[0]
    seq_dev = rows // examples
    groups, count = [], 0
    for start in range(0, model_width, chunk):
        part = pl.ds(start, chunk)
        pairs = [
            (tokens_hbm.at[:, part], tokens_ref.at[:, part]),
            (gate_hbm.at[part], weight_ref.at[part, pl.ds(0, hidden)]),
            (up_hbm.at[part], weight_ref.at[part, pl.ds(hidden, hidden)]),
            (gate_in_hbm.at[:, part], in_ref.at[pl.ds(0, rank), part]),
            (up_in_hbm.at[:, part], in_ref.at[pl.ds(rank, rank), part]),
        ]
        if start + chunk == model_width:
            pairs.append((down_in_hbm, down_in_ref))
        groups.append([pltpu.make_async_copy(a, b, sems.at[count + k]) for k, (a, b) in enumerate(pairs)])
        count += len(pairs)
        for copy in groups[-1]:
            copy.start()
    top = 2 * hidden + rank
    width, half = model_width // NX, hidden // 2
    core = lax.axis_index("sc")
    pairs = [(gate_out_hbm, out_ref.at[pl.ds(0, rank)]), (up_out_hbm, out_ref.at[pl.ds(rank, rank)])]
    for step, message in enumerate(messages, 1):
        start = pl.multiple_of(lax.rem(lax.axis_index("x") + step, NX) * width, width)
        columns = pl.ds(start, width)
        if step == 2:
            pairs.append((down_hbm.at[:, columns], message.at[pl.ds(0, hidden)]))
        else:
            pairs.append((down_hbm.at[pl.ds(core * half, half), columns], message.at[pl.ds(top, half)]))
    extra = [pltpu.make_async_copy(a, b, sems.at[count + k]) for k, (a, b) in enumerate(pairs)]
    for copy in extra:
        copy.start()
    for index, group in enumerate(groups):
        for copy in group:
            copy.wait()
        part = slice(index * chunk, (index + 1) * chunk)
        values = jnp.dot(tokens_ref[:, part], weight_ref[part, :], preferred_element_type=jnp.float32)
        right = dot32(tokens_ref[:, part], in_ref[:, part], ((1,), (1,)))
        if index == 0:
            total_ref[...] = values
            right_ref[...] = right
        else:
            total_ref[...] += values
            right_ref[...] += right

    tile = min(256, seq_dev)
    seq_index = lax.axis_index("sy") * SEQ_PARTS[1] + lax.axis_index("sc")
    for step in range(rows // tile):
        span = slice(step * tile, (step + 1) * tile)
        gate, up = total_ref[span, :hidden], total_ref[span, hidden:]
        sigmoid = 1.0 / (1.0 + jnp.exp(-gate))
        silu = gate * sigmoid
        factor_gate = up * sigmoid * (1.0 + gate * (1.0 - sigmoid))
        hidden_value = (silu * up).astype(jnp.bfloat16)
        factor_gate = factor_gate.T.astype(jnp.bfloat16)
        factor_up = silu.T.astype(jnp.bfloat16)

        first = seq_index * seq_dev + step * tile % seq_dev
        limit = lengths_ref[step * tile // seq_dev]
        columns = first + lax.broadcasted_iota(jnp.int32, (rank, tile), 1)
        right_down = dot32(down_in_ref[...], hidden_value, ((1,), (1,)))
        right_down = jnp.where(columns < limit, right_down * scale, 0.0).astype(jnp.bfloat16)
        for message in messages[::2]:
            message[:hidden, span] = factor_gate
            message[hidden : 2 * hidden, span] = factor_up
            message[2 * hidden : top, span] = right_down
        rows_at = first + lax.broadcasted_iota(jnp.int32, (tile, 2 * rank), 0)
        right_ref[span, :] = jnp.where(rows_at < limit, right_ref[span, :] * scale, 0.0)
    for copy in extra:
        copy.wait()
    for message in messages:
        for block in range(2 * rank // FOLD):
            rows_of = slice(block * FOLD, (block + 1) * FOLD)
            message[-FOLD:, block * hidden : (block + 1) * hidden] = out_ref[rows_of, :]


def token_stage(tokens, gate_weight, up_weight, gate_in, up_in, down_in, down_weight, gate_out, up_out, lengths, scale):
    rows, width = tokens.shape
    hidden = gate_weight.shape[1]
    rank = gate_in.shape[0]
    chunk = 512
    return pl.pallas_call(
        lambda *refs: token_kernel(chunk, scale, *refs),
        out_shape=[
            jax.ShapeDtypeStruct((2 * hidden + hidden // 2 + rank + FOLD, rows), jnp.bfloat16),
            jax.ShapeDtypeStruct((hidden + FOLD, rows), jnp.bfloat16),
            jax.ShapeDtypeStruct((2 * hidden + hidden // 2 + rank + FOLD, rows), jnp.bfloat16),
            jax.ShapeDtypeStruct((rows, 2 * rank), jnp.float32),
        ],
        in_specs=[pl.BlockSpec(memory_space=pltpu.SMEM)] + [HBM] * 9,
        out_specs=[VMEM] * NX,
        scratch_shapes=[
            pltpu.VMEM((rows, width), jnp.bfloat16),
            pltpu.VMEM((width, 2 * hidden), jnp.bfloat16),
            pltpu.VMEM((2 * rank, width), jnp.bfloat16),
            pltpu.VMEM((rank, hidden), jnp.bfloat16),
            pltpu.VMEM((2 * rank, hidden), jnp.bfloat16),
            pltpu.VMEM((rows, 2 * hidden), jnp.float32),
            pltpu.SemaphoreType.DMA((5 * (width // chunk) + 2 + NX,)),
        ],
        compiler_params=pltpu.CompilerParams(vmem_limit_bytes=61 * MIB),
        cost_estimate=pl.CostEstimate(
            flops=2 * rows * width * 512, bytes_accessed=16 * MIB, transcendentals=rows * hidden
        ),
        name="token_stage",
    )(lengths, tokens, gate_weight, up_weight, gate_in, up_in, down_in, down_weight, gate_out, up_out)


def forward_kernel(before_ref, after_ref, first_ref, second_ref, swap_ref):
    rows = first_ref.shape[0]
    half = swap_ref.shape[0] // 2
    first_ref[...] = before_ref[:rows, :]
    second_ref[...] = after_ref[rows : 2 * rows, :]
    swap_ref[:half, :] = before_ref[2 * rows : 2 * rows + half, :]
    swap_ref[half:, :] = after_ref[2 * rows : 2 * rows + half, :]


def halves(before, after, rows, half):
    shape = jax.ShapeDtypeStruct((rows, before.shape[1]), before.dtype)
    swap = jax.ShapeDtypeStruct((2 * half, before.shape[1]), before.dtype)
    return pl.pallas_call(
        forward_kernel,
        out_shape=[shape, shape, swap],
        in_specs=[VMEM] * 2,
        out_specs=[VMEM] * 3,
        compiler_params=pltpu.CompilerParams(vmem_limit_bytes=8 * MIB),
        name="halves",
    )(before, after)


def keep_kernel(message_ref, right_ref, factors_out, right_out):
    factors_out[...] = message_ref[: factors_out.shape[0], :]
    right_out[...] = right_ref[...]


def keep(message, right, rows):
    return pl.pallas_call(
        keep_kernel,
        out_shape=[
            jax.ShapeDtypeStruct((rows, message.shape[1]), message.dtype),
            jax.ShapeDtypeStruct(right.shape, right.dtype),
        ],
        in_specs=[VMEM] * 2,
        out_specs=[VMEM] * 2,
        compiler_params=pltpu.CompilerParams(vmem_limit_bytes=8 * MIB),
        name="keep",
    )(message, right)


def tail_kernel(weight_ref, gate_out_ref, up_out_ref, down_out_ref, right_ref, *refs):
    own_ref, messages, far_halves, swap_ref = refs[0], refs[1:NX], refs[NX : NX + 2], refs[NX + 2]
    blocks, far_block = refs[NX + 3 : NX + 2 + NZ], refs[NX + 2 + NZ : NX + 4 + NZ]
    out_ref, weights, projs, grads = refs[NX + 4 + NZ :]
    hidden, model_width = weight_ref.shape
    rank = gate_out_ref.shape[0]
    width = model_width // NX
    examples, both, seq_dev = blocks[0].shape
    piece = both // NY
    top, half, core = 2 * hidden + rank, hidden // 2, lax.axis_index("sc")
    x_at, z_at, y_at = lax.axis_index("x"), lax.axis_index("z"), lax.axis_index("yh")

    start = pl.multiple_of(x_at * width, width)
    weights[:hidden, :] = weight_ref[:, pl.ds(start, width)]
    weights[NX * hidden :, :] = down_out_ref[:, pl.ds(start, width)]
    projs[:rank, :hidden] = gate_out_ref[...]
    projs[rank:, :hidden] = up_out_ref[...]
    for step, message in enumerate(messages, 1):
        if step == 2:
            weights[step * hidden : (step + 1) * hidden, :] = message[:hidden, :]
        else:
            mine = pl.ds(pl.multiple_of(step * hidden + core * half, half), half)
            theirs = pl.ds(pl.multiple_of(step * hidden + (1 - core) * half, half), half)
            weights[mine, :] = message[top : top + half, :]
            weights[theirs, :] = swap_ref[step // 2 * half : (step // 2 + 1) * half, :]
        columns = slice(step * hidden, (step + 1) * hidden)
        for block in range(2 * rank // FOLD):
            folded = message[-FOLD:, block * hidden : (block + 1) * hidden]
            projs[block * FOLD : (block + 1) * FOLD, columns] = folded

    def factor_rows(step, first, last, columns):
        if step != 2:
            return (own_ref if step == 0 else messages[step - 1])[first:last, columns]
        rows = far_halves[0].shape[0]
        parts = [far_halves[0][first : min(last, rows), columns]] if first < rows else []
        if last > rows:
            parts.append(far_halves[1][max(first - rows, 0) : last - rows, columns])
        return jnp.concatenate(parts, axis=0)

    for example in range(examples):
        for step in range(NZ):
            if step == NZ // 2:
                count = examples // 2
                block = far_block[example // count][example % count]
            else:
                block = blocks[step if step < NZ // 2 else step - 1][example]
            base = lax.rem(z_at + step, NZ) * both
            for kind, y_of in enumerate((y_at, 1 - y_at)):
                rows = pl.ds(pl.multiple_of(base + y_of * piece, piece), piece)
                grads[rows, :] = block[kind * piece : (kind + 1) * piece]
        columns = slice(example * seq_dev, (example + 1) * seq_dev)
        total = jnp.dot(weights[...], grads[...], preferred_element_type=jnp.float32)
        left = []
        for kind in range(2):
            factor = jnp.concatenate(
                [factor_rows(step, kind * hidden, (kind + 1) * hidden, columns) for step in range(NX)], axis=0
            )
            product = total[: NX * hidden] * factor.astype(jnp.float32)
            high = product.astype(jnp.bfloat16)
            low = (product - high.astype(jnp.float32)).astype(jnp.bfloat16)
            proj = projs[kind * rank : (kind + 1) * rank, :]
            left.append(
                jnp.dot(proj, high, preferred_element_type=jnp.float32)
                + jnp.dot(proj, low, preferred_element_type=jnp.float32)
            )
        sides = jnp.dot(
            jnp.concatenate(left, axis=0),
            right_ref[columns, :],
            precision=lax.Precision.HIGHEST,
            preferred_element_type=jnp.float32,
        )
        right_down = factor_rows(0, 2 * hidden, top, columns).astype(jnp.float32)
        for step in range(1, NX):
            right_down = right_down + factor_rows(step, 2 * hidden, top, columns).astype(jnp.float32)
        out_ref[3 * example] = sides[:rank, :rank]
        out_ref[3 * example + 1] = sides[rank:, rank:]
        out_ref[3 * example + 2] = dot32(
            total[NX * hidden :], right_down, ((1,), (1,)), precision=lax.Precision.HIGHEST
        )


def tail_stage(down_weight, gate_out, up_out, down_out, right, factors, messages, far, swap, blocks, far_block):
    hidden, model_width = down_weight.shape
    rank = gate_out.shape[0]
    examples, _, seq_dev = blocks[0].shape
    width = model_width // NX
    operands = [down_weight, gate_out, up_out, down_out, right, factors, *messages, *far, swap, *blocks, *far_block]
    return pl.pallas_call(
        tail_kernel,
        out_shape=jax.ShapeDtypeStruct((examples * 3, rank, rank), jnp.float32),
        in_specs=[VMEM] * len(operands),
        out_specs=VMEM,
        scratch_shapes=[
            pltpu.VMEM((NX * hidden + rank, width), jnp.bfloat16),
            pltpu.VMEM((2 * rank, NX * hidden), jnp.bfloat16),
            pltpu.VMEM((width, seq_dev), jnp.bfloat16),
        ],
        compiler_params=pltpu.CompilerParams(vmem_limit_bytes=20 * MIB),
        cost_estimate=pl.CostEstimate(flops=4 * 10**9, bytes_accessed=8 * MIB, transcendentals=0),
        name="tail_stage",
    )(*operands)


def cut_kernel(up_ref, down_ref, first_ref, second_ref):
    first_ref[...] = up_ref[: first_ref.shape[0]]
    second_ref[...] = down_ref[first_ref.shape[0] :]


def cut(up, down):
    shape = jax.ShapeDtypeStruct((up.shape[0] // 2,) + up.shape[1:], up.dtype)
    return pl.pallas_call(
        cut_kernel,
        out_shape=[shape] * 2,
        in_specs=[VMEM] * 2,
        out_specs=[VMEM] * 2,
        compiler_params=pltpu.CompilerParams(vmem_limit_bytes=4 * MIB),
        name="cut",
    )(up, down)


def ring_z(own):
    up, down = [own], [own]
    for _ in range(NZ // 2 - 1):
        up.append(lax.ppermute(up[-1], "z", shifted(NZ, -1)))
        down.append(lax.ppermute(down[-1], "z", shifted(NZ, 1)))
    first, second = cut(up[-1], down[-1])
    far = [lax.ppermute(first, "z", shifted(NZ, -1)), lax.ppermute(second, "z", shifted(NZ, 1))]
    return up + down[:0:-1], far


def sum_everywhere(partial):
    count, size = partial.shape
    parts = SEQ_PARTS[0] * SEQ_PARTS[1] * NZ
    width = size // parts
    pieces = partial.reshape(count, parts, width).transpose(1, 0, 2)
    pieces = lax.all_to_all(pieces, ("sy", "sc", "z"), 0, 0, tiled=True)
    own = jnp.sum(pieces, axis=0)
    spread = jnp.broadcast_to(own[None], (NX * NZ * NY,) + own.shape)
    blocks = lax.all_to_all(spread, ("x", "z", "yh"), 0, 0, tiled=True)
    blocks = blocks.reshape(NX, NZ, NY, count, width).sum(axis=(0, 2))
    return blocks.transpose(1, 0, 2).reshape(count, NZ * width)


def shards(
    tokens,
    out_grad,
    gate_weight,
    up_weight,
    down_weight,
    proj_gate_in,
    proj_gate_out,
    proj_up_in,
    proj_up_out,
    proj_down_in,
    proj_down_out,
    lengths,
):
    examples, seq_dev, model_width = tokens.shape
    scale = float(seq_dev * SEQ_PARTS[0] * SEQ_PARTS[1]) ** (-0.5)
    gate_out, up_out = proj_gate_out.T, proj_up_out.T

    own_grad = out_grad.transpose(0, 2, 1)
    other_grad = lax.ppermute(own_grad, "yh", shifted(NY, 1))
    flat_tokens = tokens.reshape(examples * seq_dev, model_width)
    sent = token_stage(
        flat_tokens,
        gate_weight,
        up_weight,
        proj_gate_in.T,
        proj_up_in.T,
        proj_down_in.T,
        down_weight,
        gate_out,
        up_out,
        lengths,
        scale,
    )
    sent, right = sent[: NX - 1], sent[NX - 1]
    *sent, _ = hold([*sent, other_grad])
    pair = pair_up(own_grad, other_grad)
    messages = [lax.ppermute(piece, "x", shifted(NX, step)) for step, piece in enumerate(sent, 1)]
    hidden, rank = gate_weight.shape[1], gate_out.shape[0]
    rows = 2 * hidden + rank
    first, second, swap = halves(messages[0], messages[2], rows // 2, hidden // 2)
    swap = lax.ppermute(swap, "sc", shifted(SEQ_PARTS[1], 1))
    far = [lax.ppermute(first, "x", shifted(NX, 1)), lax.ppermute(second, "x", shifted(NX, -1))]
    blocks, far_block = ring_z(pair)
    factors, right = keep(sent[0], right, rows)
    products = tail_stage(
        down_weight, gate_out, up_out, proj_down_out.T, right, factors, messages, far, swap, blocks, far_block
    )
    total = sum_everywhere(products.reshape(examples * 3, -1))
    return total.reshape(examples, 3, -1)


def solution(mesh):
    fine = Mesh(mesh.devices.reshape(SEQ_PARTS + FSDP_PARTS), ("sy", "sc", "x", "z", "yh"))
    seq, fsdp = ("sy", "sc"), ("x", "z", "yh")
    placed = (
        P(None, seq, None),
        P(None, seq, fsdp),
        P(None, fsdp),
        P(None, fsdp),
        P(fsdp, None),
        P(),
        P(fsdp, None),
        P(),
        P(fsdp, None),
        P(fsdp, None),
        P(),
        P(),
    )
    return jax.shard_map(
        shards, mesh=fine, in_specs=placed, out_specs=P(None, None, seq), check_vma=False
    )
```

```python
import jax
import jax.numpy as jnp
from jax import lax
from jax.experimental import pallas as pl
from jax.experimental.pallas import tpu as pltpu
from jax.sharding import Mesh, PartitionSpec as P

SEQ_PARTS = (2, 2)
FSDP_PARTS = (4, 8, 2)
NX, NZ, NY = FSDP_PARTS
FOLD = 16
MIB = 1024 * 1024
VMEM = pl.BlockSpec(memory_space=pltpu.VMEM)
HBM = pl.BlockSpec(memory_space=pltpu.HBM)


def shifted(count, step):
    return [(i, (i + step) % count) for i in range(count)]


def dot32(a, b, dims, precision=None):
    return lax.dot_general(a, b, (dims, ((), ())), preferred_element_type=jnp.float32, precision=precision)


def hold_kernel(*refs):
    pass


def hold(arrays):
    return pl.pallas_call(
        hold_kernel,
        out_shape=[jax.ShapeDtypeStruct(array.shape, array.dtype) for array in arrays],
        in_specs=[HBM] * len(arrays),
        out_specs=[HBM] * len(arrays),
        input_output_aliases={index: index for index in range(len(arrays))},
        compiler_params=pltpu.CompilerParams(vmem_limit_bytes=62 * MIB),
        name="hold",
    )(*arrays)


def pair_kernel(own_ref, other_ref, out_ref):
    piece = own_ref.shape[1]
    out_ref[:, :piece, :] = own_ref[...]
    out_ref[:, piece:, :] = other_ref[...]


def pair_up(own, other):
    examples, piece, seq_dev = own.shape
    return pl.pallas_call(
        pair_kernel,
        out_shape=jax.ShapeDtypeStruct((examples, NY * piece, seq_dev), own.dtype),
        in_specs=[VMEM] * 2,
        out_specs=VMEM,
        compiler_params=pltpu.CompilerParams(vmem_limit_bytes=4 * MIB),
        name="pair_up",
    )(own, other)


def token_kernel(chunk, scale, lengths_ref, tokens_hbm, gate_hbm, up_hbm, gate_in_hbm, up_in_hbm, down_in_hbm, down_hbm, gate_out_hbm, up_out_hbm, *refs):
    messages, right_ref = refs[: NX - 1], refs[NX - 1]
    tokens_ref, weight_ref, in_ref, down_in_ref, out_ref, total_ref, sems = refs[NX:]
    rows, model_width = tokens_hbm.shape
    hidden = gate_hbm.shape[1]
    rank = gate_in_hbm.shape[0]
    examples = lengths_ref.shape[0]
    seq_dev = rows // examples
    groups, count = [], 0
    for start in range(0, model_width, chunk):
        part = pl.ds(start, chunk)
        pairs = [
            (tokens_hbm.at[:, part], tokens_ref.at[:, part]),
            (gate_hbm.at[part], weight_ref.at[part, pl.ds(0, hidden)]),
            (up_hbm.at[part], weight_ref.at[part, pl.ds(hidden, hidden)]),
            (gate_in_hbm.at[:, part], in_ref.at[pl.ds(0, rank), part]),
            (up_in_hbm.at[:, part], in_ref.at[pl.ds(rank, rank), part]),
        ]
        if start + chunk == model_width:
            pairs.append((down_in_hbm, down_in_ref))
        groups.append([pltpu.make_async_copy(a, b, sems.at[count + k]) for k, (a, b) in enumerate(pairs)])
        count += len(pairs)
        for copy in groups[-1]:
            copy.start()
    top = 2 * hidden + rank
    width, half = model_width // NX, hidden // 2
    core = lax.axis_index("sc")
    pairs = [(gate_out_hbm, out_ref.at[pl.ds(0, rank)]), (up_out_hbm, out_ref.at[pl.ds(rank, rank)])]
    for step, message in enumerate(messages, 1):
        start = pl.multiple_of(lax.rem(lax.axis_index("x") + step, NX) * width, width)
        columns = pl.ds(start, width)
        if step == 2:
            pairs.append((down_hbm.at[:, columns], message.at[pl.ds(0, hidden)]))
        else:
            pairs.append((down_hbm.at[pl.ds(core * half, half), columns], message.at[pl.ds(top, half)]))
    extra = [pltpu.make_async_copy(a, b, sems.at[count + k]) for k, (a, b) in enumerate(pairs)]
    for copy in extra:
        copy.start()
    for index, group in enumerate(groups):
        for copy in group:
            copy.wait()
        part = slice(index * chunk, (index + 1) * chunk)
        values = jnp.dot(tokens_ref[:, part], weight_ref[part, :], preferred_element_type=jnp.float32)
        right = dot32(tokens_ref[:, part], in_ref[:, part], ((1,), (1,)))
        if index == 0:
            total_ref[...] = values
            right_ref[...] = right
        else:
            total_ref[...] += values
            right_ref[...] += right

    tile = min(256, seq_dev)
    seq_index = lax.axis_index("sy") * SEQ_PARTS[1] + lax.axis_index("sc")
    for step in range(rows // tile):
        span = slice(step * tile, (step + 1) * tile)
        gate, up = total_ref[span, :hidden], total_ref[span, hidden:]
        sigmoid = 1.0 / (1.0 + jnp.exp(-gate))
        silu = gate * sigmoid
        factor_gate = up * sigmoid * (1.0 + gate * (1.0 - sigmoid))
        hidden_value = (silu * up).astype(jnp.bfloat16)
        factor_gate = factor_gate.T.astype(jnp.bfloat16)
        factor_up = silu.T.astype(jnp.bfloat16)

        first = seq_index * seq_dev + step * tile % seq_dev
        limit = lengths_ref[step * tile // seq_dev]
        columns = first + lax.broadcasted_iota(jnp.int32, (rank, tile), 1)
        right_down = dot32(down_in_ref[...], hidden_value, ((1,), (1,)))
        right_down = jnp.where(columns < limit, right_down * scale, 0.0).astype(jnp.bfloat16)
        for message in messages[::2]:
            message[:hidden, span] = factor_gate
            message[hidden : 2 * hidden, span] = factor_up
            message[2 * hidden : top, span] = right_down
        rows_at = first + lax.broadcasted_iota(jnp.int32, (tile, 2 * rank), 0)
        right_ref[span, :] = jnp.where(rows_at < limit, right_ref[span, :] * scale, 0.0)
    for copy in extra:
        copy.wait()
    for message in messages:
        for block in range(2 * rank // FOLD):
            rows_of = slice(block * FOLD, (block + 1) * FOLD)
            message[-FOLD:, block * hidden : (block + 1) * hidden] = out_ref[rows_of, :]


def token_stage(tokens, gate_weight, up_weight, gate_in, up_in, down_in, down_weight, gate_out, up_out, lengths, scale):
    rows, width = tokens.shape
    hidden = gate_weight.shape[1]
    rank = gate_in.shape[0]
    chunk = 512
    return pl.pallas_call(
        lambda *refs: token_kernel(chunk, scale, *refs),
        out_shape=[
            jax.ShapeDtypeStruct((2 * hidden + hidden // 2 + rank + FOLD, rows), jnp.bfloat16),
            jax.ShapeDtypeStruct((hidden + FOLD, rows), jnp.bfloat16),
            jax.ShapeDtypeStruct((2 * hidden + hidden // 2 + rank + FOLD, rows), jnp.bfloat16),
            jax.ShapeDtypeStruct((rows, 2 * rank), jnp.float32),
        ],
        in_specs=[pl.BlockSpec(memory_space=pltpu.SMEM)] + [HBM] * 9,
        out_specs=[VMEM] * NX,
        scratch_shapes=[
            pltpu.VMEM((rows, width), jnp.bfloat16),
            pltpu.VMEM((width, 2 * hidden), jnp.bfloat16),
            pltpu.VMEM((2 * rank, width), jnp.bfloat16),
            pltpu.VMEM((rank, hidden), jnp.bfloat16),
            pltpu.VMEM((2 * rank, hidden), jnp.bfloat16),
            pltpu.VMEM((rows, 2 * hidden), jnp.float32),
            pltpu.SemaphoreType.DMA((5 * (width // chunk) + 2 + NX,)),
        ],
        compiler_params=pltpu.CompilerParams(vmem_limit_bytes=61 * MIB),
        cost_estimate=pl.CostEstimate(
            flops=2 * rows * width * 512, bytes_accessed=16 * MIB, transcendentals=rows * hidden
        ),
        name="token_stage",
    )(lengths, tokens, gate_weight, up_weight, gate_in, up_in, down_in, down_weight, gate_out, up_out)


def forward_kernel(before_ref, after_ref, first_ref, second_ref, swap_ref):
    rows = first_ref.shape[0]
    half = swap_ref.shape[0] // 2
    first_ref[...] = before_ref[:rows, :]
    second_ref[...] = after_ref[rows : 2 * rows, :]
    swap_ref[:half, :] = before_ref[2 * rows : 2 * rows + half, :]
    swap_ref[half:, :] = after_ref[2 * rows : 2 * rows + half, :]


def halves(before, after, rows, half):
    shape = jax.ShapeDtypeStruct((rows, before.shape[1]), before.dtype)
    swap = jax.ShapeDtypeStruct((2 * half, before.shape[1]), before.dtype)
    return pl.pallas_call(
        forward_kernel,
        out_shape=[shape, shape, swap],
        in_specs=[VMEM] * 2,
        out_specs=[VMEM] * 3,
        compiler_params=pltpu.CompilerParams(vmem_limit_bytes=8 * MIB),
        name="halves",
    )(before, after)


def early_kernel(weight_ref, gate_out_ref, up_out_ref, down_out_ref, right_ref, own_ref, *refs):
    messages, swap_ref, blocks = refs[: NX - 1], refs[NX - 1], refs[NX : NX + NZ - 1]
    total_ref, far_ref, projs, right_out, factors_out, weights, grads = refs[NX + NZ - 1 :]
    hidden, model_width = weight_ref.shape
    rank = gate_out_ref.shape[0]
    width = model_width // NX
    examples, both, _ = blocks[0].shape
    piece = both // NY
    half, core = hidden // 2, lax.axis_index("sc")
    x_at, z_at, y_at = lax.axis_index("x"), lax.axis_index("z"), lax.axis_index("yh")

    factors_out[...] = own_ref[: factors_out.shape[0], :]
    right_out[...] = right_ref[...]
    start = pl.multiple_of(x_at * width, width)
    weights[:hidden, :] = weight_ref[:, pl.ds(start, width)]
    weights[NX * hidden :, :] = down_out_ref[:, pl.ds(start, width)]
    projs[:rank, :hidden] = gate_out_ref[...]
    projs[rank:, :hidden] = up_out_ref[...]
    for step, message in enumerate(messages, 1):
        top = message.shape[0] - FOLD
        if step == 2:
            weights[step * hidden : (step + 1) * hidden, :] = message[top - hidden : top, :]
        else:
            mine = pl.ds(pl.multiple_of(step * hidden + core * half, half), half)
            theirs = pl.ds(pl.multiple_of(step * hidden + (1 - core) * half, half), half)
            weights[mine, :] = message[top - half : top, :]
            weights[theirs, :] = swap_ref[step // 2 * half : (step // 2 + 1) * half, :]
        columns = slice(step * hidden, (step + 1) * hidden)
        for block in range(2 * rank // FOLD):
            folded = message[top:, block * hidden : (block + 1) * hidden]
            projs[block * FOLD : (block + 1) * FOLD, columns] = folded
    far_base = pl.multiple_of(lax.rem(z_at + NZ // 2, NZ) * both, both)
    far_ref[...] = weights[:, pl.ds(far_base, both)]
    for example in range(examples):
        grads[example, pl.ds(far_base, both), :] = jnp.zeros((both, grads.shape[2]), grads.dtype)
        for step, block in enumerate(blocks):
            base = lax.rem(z_at + step + step // (NZ // 2), NZ) * both
            for kind, y_of in enumerate((y_at, 1 - y_at)):
                rows = pl.ds(pl.multiple_of(base + y_of * piece, piece), piece)
                grads[example, rows, :] = block[example, kind * piece : (kind + 1) * piece]
    for example in range(examples):
        total_ref[example] = jnp.dot(weights[...], grads[example], preferred_element_type=jnp.float32)


def early_stage(down_weight, gate_out, up_out, down_out, right, message, messages, swap, blocks):
    hidden, model_width = down_weight.shape
    rank = gate_out.shape[0]
    examples, both, seq_dev = blocks[0].shape
    width = model_width // NX
    rows = NX * hidden + rank
    operands = [down_weight, gate_out, up_out, down_out, right, message, *messages, swap, *blocks]
    return pl.pallas_call(
        early_kernel,
        out_shape=[
            jax.ShapeDtypeStruct((examples, rows, seq_dev), jnp.float32),
            jax.ShapeDtypeStruct((rows, both), jnp.bfloat16),
            jax.ShapeDtypeStruct((2 * rank, NX * hidden), jnp.bfloat16),
            jax.ShapeDtypeStruct(right.shape, right.dtype),
            jax.ShapeDtypeStruct((2 * hidden + rank, message.shape[1]), message.dtype),
        ],
        in_specs=[VMEM] * len(operands),
        out_specs=[VMEM] * 5,
        scratch_shapes=[
            pltpu.VMEM((rows, width), jnp.bfloat16),
            pltpu.VMEM((examples, width, seq_dev), jnp.bfloat16),
        ],
        compiler_params=pltpu.CompilerParams(vmem_limit_bytes=20 * MIB),
        cost_estimate=pl.CostEstimate(flops=2 * 10**9, bytes_accessed=4 * MIB, transcendentals=0),
        name="early_stage",
    )(*operands)


def tail_kernel(total_ref, far_ref, projs, right_ref, own_ref, *refs):
    near, far_halves, far_block, (out_ref, grads) = refs[:2], refs[2:4], refs[4:6], refs[6:]
    examples = total_ref.shape[0]
    seq_dev = total_ref.shape[2]
    rank, hidden = projs.shape[0] // 2, projs.shape[1] // NX
    top = 2 * hidden + rank
    piece = grads.shape[1] // NY
    y_at = lax.axis_index("yh")

    def factor_rows(step, first, last, columns):
        if step != 2:
            return (own_ref, near[0], None, near[1])[step][first:last, columns]
        rows = far_halves[0].shape[0]
        parts = [far_halves[0][first : min(last, rows), columns]] if first < rows else []
        if last > rows:
            parts.append(far_halves[1][max(first - rows, 0) : last - rows, columns])
        return jnp.concatenate(parts, axis=0)

    for example in range(examples):
        count = examples // 2
        for kind, y_of in enumerate((y_at, 1 - y_at)):
            rows = pl.ds(pl.multiple_of(y_of * piece, piece), piece)
            grads[example, rows, :] = far_block[example // count][example % count, kind * piece : (kind + 1) * piece]
    for example in range(examples):
        columns = slice(example * seq_dev, (example + 1) * seq_dev)
        total = total_ref[example] + jnp.dot(far_ref[...], grads[example], preferred_element_type=jnp.float32)
        left = []
        for kind in range(2):
            factor = jnp.concatenate(
                [factor_rows(step, kind * hidden, (kind + 1) * hidden, columns) for step in range(NX)], axis=0
            )
            product = total[: NX * hidden] * factor.astype(jnp.float32)
            high = product.astype(jnp.bfloat16)
            low = (product - high.astype(jnp.float32)).astype(jnp.bfloat16)
            proj = projs[kind * rank : (kind + 1) * rank, :]
            left.append(
                jnp.dot(proj, high, preferred_element_type=jnp.float32)
                + jnp.dot(proj, low, preferred_element_type=jnp.float32)
            )
        sides = jnp.dot(
            jnp.concatenate(left, axis=0),
            right_ref[columns, :],
            precision=lax.Precision.HIGHEST,
            preferred_element_type=jnp.float32,
        )
        right_down = factor_rows(0, 2 * hidden, top, columns).astype(jnp.float32)
        for step in range(1, NX):
            right_down = right_down + factor_rows(step, 2 * hidden, top, columns).astype(jnp.float32)
        out_ref[3 * example] = sides[:rank, :rank]
        out_ref[3 * example + 1] = sides[rank:, rank:]
        out_ref[3 * example + 2] = dot32(
            total[NX * hidden :], right_down, ((1,), (1,)), precision=lax.Precision.HIGHEST
        )


def tail_stage(total, far_weight, projs, right, factors, near, far, far_block):
    examples, _, seq_dev = total.shape
    rank = projs.shape[0] // 2
    operands = [total, far_weight, projs, right, factors, *near, *far, *far_block]
    return pl.pallas_call(
        tail_kernel,
        out_shape=jax.ShapeDtypeStruct((examples * 3, rank, rank), jnp.float32),
        in_specs=[VMEM] * len(operands),
        out_specs=VMEM,
        scratch_shapes=[pltpu.VMEM((examples, far_weight.shape[1], seq_dev), jnp.bfloat16)],
        compiler_params=pltpu.CompilerParams(vmem_limit_bytes=16 * MIB),
        cost_estimate=pl.CostEstimate(flops=2 * 10**9, bytes_accessed=4 * MIB, transcendentals=0),
        name="tail_stage",
    )(*operands)


def cut_kernel(up_ref, down_ref, first_ref, second_ref):
    first_ref[...] = up_ref[: first_ref.shape[0]]
    second_ref[...] = down_ref[first_ref.shape[0] :]


def cut(up, down):
    shape = jax.ShapeDtypeStruct((up.shape[0] // 2,) + up.shape[1:], up.dtype)
    return pl.pallas_call(
        cut_kernel,
        out_shape=[shape] * 2,
        in_specs=[VMEM] * 2,
        out_specs=[VMEM] * 2,
        compiler_params=pltpu.CompilerParams(vmem_limit_bytes=4 * MIB),
        name="cut",
    )(up, down)


def ring_z(own):
    up, down = [own], [own]
    for _ in range(NZ // 2 - 1):
        up.append(lax.ppermute(up[-1], "z", shifted(NZ, -1)))
        down.append(lax.ppermute(down[-1], "z", shifted(NZ, 1)))
    first, second = cut(up[-1], down[-1])
    far = [lax.ppermute(first, "z", shifted(NZ, -1)), lax.ppermute(second, "z", shifted(NZ, 1))]
    return up + down[:0:-1], far


def sum_everywhere(partial):
    count, size = partial.shape
    parts = SEQ_PARTS[0] * SEQ_PARTS[1] * NZ
    width = size // parts
    pieces = partial.reshape(count, parts, width).transpose(1, 0, 2)
    pieces = lax.all_to_all(pieces, ("sy", "sc", "z"), 0, 0, tiled=True)
    own = jnp.sum(pieces, axis=0)
    spread = jnp.broadcast_to(own[None], (NX * NZ * NY,) + own.shape)
    blocks = lax.all_to_all(spread, ("x", "z", "yh"), 0, 0, tiled=True)
    blocks = blocks.reshape(NX, NZ, NY, count, width).sum(axis=(0, 2))
    return blocks.transpose(1, 0, 2).reshape(count, NZ * width)


def shards(
    tokens,
    out_grad,
    gate_weight,
    up_weight,
    down_weight,
    proj_gate_in,
    proj_gate_out,
    proj_up_in,
    proj_up_out,
    proj_down_in,
    proj_down_out,
    lengths,
):
    examples, seq_dev, model_width = tokens.shape
    scale = float(seq_dev * SEQ_PARTS[0] * SEQ_PARTS[1]) ** (-0.5)
    gate_out, up_out = proj_gate_out.T, proj_up_out.T

    own_grad = out_grad.transpose(0, 2, 1)
    other_grad = lax.ppermute(own_grad, "yh", shifted(NY, 1))
    flat_tokens = tokens.reshape(examples * seq_dev, model_width)
    sent = token_stage(
        flat_tokens,
        gate_weight,
        up_weight,
        proj_gate_in.T,
        proj_up_in.T,
        proj_down_in.T,
        down_weight,
        gate_out,
        up_out,
        lengths,
        scale,
    )
    sent, right = sent[: NX - 1], sent[NX - 1]
    *sent, _ = hold([*sent, other_grad])
    pair = pair_up(own_grad, other_grad)
    messages = [lax.ppermute(piece, "x", shifted(NX, step)) for step, piece in enumerate(sent, 1)]
    hidden, rank = gate_weight.shape[1], gate_out.shape[0]
    rows = 2 * hidden + rank
    first, second, swap = halves(messages[0], messages[2], rows // 2, hidden // 2)
    swap = lax.ppermute(swap, "sc", shifted(SEQ_PARTS[1], 1))
    far = [lax.ppermute(first, "x", shifted(NX, 1)), lax.ppermute(second, "x", shifted(NX, -1))]
    blocks, far_block = ring_z(pair)
    total, far_weight, projs, right, factors = early_stage(
        down_weight, gate_out, up_out, proj_down_out.T, right, sent[0], messages, swap, blocks
    )
    products = tail_stage(total, far_weight, projs, right, factors, messages[::2], far, far_block)
    total = sum_everywhere(products.reshape(examples * 3, -1))
    return total.reshape(examples, 3, -1)


def solution(mesh):
    fine = Mesh(mesh.devices.reshape(SEQ_PARTS + FSDP_PARTS), ("sy", "sc", "x", "z", "yh"))
    seq, fsdp = ("sy", "sc"), ("x", "z", "yh")
    placed = (
        P(None, seq, None),
        P(None, seq, fsdp),
        P(None, fsdp),
        P(None, fsdp),
        P(fsdp, None),
        P(),
        P(fsdp, None),
        P(),
        P(fsdp, None),
        P(fsdp, None),
        P(),
        P(),
    )
    return jax.shard_map(
        shards, mesh=fine, in_specs=placed, out_specs=P(None, None, seq), check_vma=False
    )
```

```python
import jax
import jax.numpy as jnp
from jax import lax
from jax.experimental import pallas as pl
from jax.experimental.pallas import tpu as pltpu
from jax.sharding import Mesh, PartitionSpec as P

SEQ_PARTS = (2, 2)
FSDP_PARTS = (4, 8, 2)
NX, NZ, NY = FSDP_PARTS
FOLD = 16
MIB = 1024 * 1024
VMEM = pl.BlockSpec(memory_space=pltpu.VMEM)
HBM = pl.BlockSpec(memory_space=pltpu.HBM)


def shifted(count, step):
    return [(i, (i + step) % count) for i in range(count)]


def dot32(a, b, dims, precision=None):
    return lax.dot_general(a, b, (dims, ((), ())), preferred_element_type=jnp.float32, precision=precision)


def hold_kernel(*refs):
    pass


def hold(arrays):
    return pl.pallas_call(
        hold_kernel,
        out_shape=[jax.ShapeDtypeStruct(array.shape, array.dtype) for array in arrays],
        in_specs=[HBM] * len(arrays),
        out_specs=[HBM] * len(arrays),
        input_output_aliases={index: index for index in range(len(arrays))},
        compiler_params=pltpu.CompilerParams(vmem_limit_bytes=62 * MIB),
        name="hold",
    )(*arrays)


def pair_kernel(own_ref, other_ref, out_ref):
    piece = own_ref.shape[1]
    out_ref[:, :piece, :] = own_ref[...]
    out_ref[:, piece:, :] = other_ref[...]


def pair_up(own, other):
    examples, piece, seq_dev = own.shape
    return pl.pallas_call(
        pair_kernel,
        out_shape=jax.ShapeDtypeStruct((examples, NY * piece, seq_dev), own.dtype),
        in_specs=[VMEM] * 2,
        out_specs=VMEM,
        compiler_params=pltpu.CompilerParams(vmem_limit_bytes=4 * MIB),
        name="pair_up",
    )(own, other)


def token_kernel(chunk, scale, lengths_ref, tokens_hbm, gate_hbm, up_hbm, gate_in_hbm, up_in_hbm, down_in_hbm, down_hbm, gate_out_hbm, up_out_hbm, *refs):
    messages, right_ref = refs[: NX - 1], refs[NX - 1]
    tokens_ref, weight_ref, in_ref, down_in_ref, out_ref, total_ref, sems = refs[NX:]
    rows, model_width = tokens_hbm.shape
    hidden = gate_hbm.shape[1]
    rank = gate_in_hbm.shape[0]
    examples = lengths_ref.shape[0]
    seq_dev = rows // examples
    groups, count = [], 0
    for start in range(0, model_width, chunk):
        part = pl.ds(start, chunk)
        pairs = [
            (tokens_hbm.at[:, part], tokens_ref.at[:, part]),
            (gate_hbm.at[part], weight_ref.at[part, pl.ds(0, hidden)]),
            (up_hbm.at[part], weight_ref.at[part, pl.ds(hidden, hidden)]),
            (gate_in_hbm.at[:, part], in_ref.at[pl.ds(0, rank), part]),
            (up_in_hbm.at[:, part], in_ref.at[pl.ds(rank, rank), part]),
        ]
        if start + chunk == model_width:
            pairs.append((down_in_hbm, down_in_ref))
        groups.append([pltpu.make_async_copy(a, b, sems.at[count + k]) for k, (a, b) in enumerate(pairs)])
        count += len(pairs)
        for copy in groups[-1]:
            copy.start()
    top = 2 * hidden + rank
    width, half = model_width // NX, hidden // 2
    core = lax.axis_index("sc")
    pairs = [(gate_out_hbm, out_ref.at[pl.ds(0, rank)]), (up_out_hbm, out_ref.at[pl.ds(rank, rank)])]
    for step, message in enumerate(messages, 1):
        start = pl.multiple_of(lax.rem(lax.axis_index("x") + step, NX) * width, width)
        columns = pl.ds(start, width)
        if step == 2:
            pairs.append((down_hbm.at[:, columns], message.at[pl.ds(0, hidden)]))
        else:
            pairs.append((down_hbm.at[pl.ds(core * half, half), columns], message.at[pl.ds(top, half)]))
    extra = [pltpu.make_async_copy(a, b, sems.at[count + k]) for k, (a, b) in enumerate(pairs)]
    for copy in extra:
        copy.start()
    for index, group in enumerate(groups):
        for copy in group:
            copy.wait()
        part = slice(index * chunk, (index + 1) * chunk)
        values = jnp.dot(tokens_ref[:, part], weight_ref[part, :], preferred_element_type=jnp.float32)
        right = dot32(tokens_ref[:, part], in_ref[:, part], ((1,), (1,)))
        if index == 0:
            total_ref[...] = values
            right_ref[...] = right
        else:
            total_ref[...] += values
            right_ref[...] += right

    tile = min(256, seq_dev)
    seq_index = lax.axis_index("sy") * SEQ_PARTS[1] + lax.axis_index("sc")
    for step in range(rows // tile):
        span = slice(step * tile, (step + 1) * tile)
        gate, up = total_ref[span, :hidden], total_ref[span, hidden:]
        sigmoid = 1.0 / (1.0 + jnp.exp(-gate))
        silu = gate * sigmoid
        factor_gate = up * sigmoid * (1.0 + gate * (1.0 - sigmoid))
        hidden_value = (silu * up).astype(jnp.bfloat16)
        factor_gate = factor_gate.T.astype(jnp.bfloat16)
        factor_up = silu.T.astype(jnp.bfloat16)

        first = seq_index * seq_dev + step * tile % seq_dev
        limit = lengths_ref[step * tile // seq_dev]
        columns = first + lax.broadcasted_iota(jnp.int32, (rank, tile), 1)
        right_down = dot32(down_in_ref[...], hidden_value, ((1,), (1,)))
        right_down = jnp.where(columns < limit, right_down * scale, 0.0).astype(jnp.bfloat16)
        for message in messages[::2]:
            message[:hidden, span] = factor_gate
            message[hidden : 2 * hidden, span] = factor_up
            message[2 * hidden : top, span] = right_down
        rows_at = first + lax.broadcasted_iota(jnp.int32, (tile, 2 * rank), 0)
        right_ref[span, :] = jnp.where(rows_at < limit, right_ref[span, :] * scale, 0.0)
    for copy in extra:
        copy.wait()
    for message in messages:
        for block in range(2 * rank // FOLD):
            rows_of = slice(block * FOLD, (block + 1) * FOLD)
            message[-FOLD:, block * hidden : (block + 1) * hidden] = out_ref[rows_of, :]


def token_stage(tokens, gate_weight, up_weight, gate_in, up_in, down_in, down_weight, gate_out, up_out, lengths, scale):
    rows, width = tokens.shape
    hidden = gate_weight.shape[1]
    rank = gate_in.shape[0]
    chunk = 512
    return pl.pallas_call(
        lambda *refs: token_kernel(chunk, scale, *refs),
        out_shape=[
            jax.ShapeDtypeStruct((2 * hidden + hidden // 2 + rank + FOLD, rows), jnp.bfloat16),
            jax.ShapeDtypeStruct((hidden + FOLD, rows), jnp.bfloat16),
            jax.ShapeDtypeStruct((2 * hidden + hidden // 2 + rank + FOLD, rows), jnp.bfloat16),
            jax.ShapeDtypeStruct((rows, 2 * rank), jnp.float32),
        ],
        in_specs=[pl.BlockSpec(memory_space=pltpu.SMEM)] + [HBM] * 9,
        out_specs=[VMEM] * NX,
        scratch_shapes=[
            pltpu.VMEM((rows, width), jnp.bfloat16),
            pltpu.VMEM((width, 2 * hidden), jnp.bfloat16),
            pltpu.VMEM((2 * rank, width), jnp.bfloat16),
            pltpu.VMEM((rank, hidden), jnp.bfloat16),
            pltpu.VMEM((2 * rank, hidden), jnp.bfloat16),
            pltpu.VMEM((rows, 2 * hidden), jnp.float32),
            pltpu.SemaphoreType.DMA((5 * (width // chunk) + 2 + NX,)),
        ],
        compiler_params=pltpu.CompilerParams(vmem_limit_bytes=61 * MIB),
        cost_estimate=pl.CostEstimate(
            flops=2 * rows * width * 512, bytes_accessed=16 * MIB, transcendentals=rows * hidden
        ),
        name="token_stage",
    )(lengths, tokens, gate_weight, up_weight, gate_in, up_in, down_in, down_weight, gate_out, up_out)


def forward_kernel(before_ref, after_ref, first_ref, second_ref):
    rows = first_ref.shape[0]
    first_ref[...] = before_ref[:rows, :]
    second_ref[...] = after_ref[rows : 2 * rows, :]


def halves(before, after, rows):
    shape = jax.ShapeDtypeStruct((rows, before.shape[1]), before.dtype)
    return pl.pallas_call(
        forward_kernel,
        out_shape=[shape] * 2,
        in_specs=[VMEM] * 2,
        out_specs=[VMEM] * 2,
        compiler_params=pltpu.CompilerParams(vmem_limit_bytes=8 * MIB),
        name="halves",
    )(before, after)


def early_kernel(weight_ref, gate_out_ref, up_out_ref, down_out_ref, right_ref, own_ref, *refs):
    messages, swap_ref, blocks = refs[: NX - 1], refs[NX - 1], refs[NX : NX + NZ - 1]
    total_ref, far_ref, projs, right_out, factors_out, weights, grads = refs[NX + NZ - 1 :]
    hidden, model_width = weight_ref.shape
    rank = gate_out_ref.shape[0]
    width = model_width // NX
    examples, both, _ = blocks[0].shape
    piece = both // NY
    half, core = hidden // 2, lax.axis_index("sc")
    x_at, z_at, y_at = lax.axis_index("x"), lax.axis_index("z"), lax.axis_index("yh")

    factors_out[...] = own_ref[: factors_out.shape[0], :]
    right_out[...] = right_ref[...]
    start = pl.multiple_of(x_at * width, width)
    weights[:hidden, :] = weight_ref[:, pl.ds(start, width)]
    weights[NX * hidden :, :] = down_out_ref[:, pl.ds(start, width)]
    projs[:rank, :hidden] = gate_out_ref[...]
    projs[rank:, :hidden] = up_out_ref[...]
    for step, message in enumerate(messages, 1):
        top = message.shape[0] - FOLD
        if step == 2:
            weights[step * hidden : (step + 1) * hidden, :] = message[top - hidden : top, :]
        else:
            mine = pl.ds(pl.multiple_of(step * hidden + core * half, half), half)
            theirs = pl.ds(pl.multiple_of(step * hidden + (1 - core) * half, half), half)
            weights[mine, :] = message[top - half : top, :]
            weights[theirs, :] = swap_ref[step // 2 * half : (step // 2 + 1) * half, :]
        columns = slice(step * hidden, (step + 1) * hidden)
        for block in range(2 * rank // FOLD):
            folded = message[top:, block * hidden : (block + 1) * hidden]
            projs[block * FOLD : (block + 1) * FOLD, columns] = folded
    far_base = pl.multiple_of(lax.rem(z_at + NZ // 2, NZ) * both, both)
    far_ref[...] = weights[:, pl.ds(far_base, both)]
    for example in range(examples):
        grads[example, pl.ds(far_base, both), :] = jnp.zeros((both, grads.shape[2]), grads.dtype)
        for step, block in enumerate(blocks):
            base = lax.rem(z_at + step + step // (NZ // 2), NZ) * both
            for kind, y_of in enumerate((y_at, 1 - y_at)):
                rows = pl.ds(pl.multiple_of(base + y_of * piece, piece), piece)
                grads[example, rows, :] = block[example, kind * piece : (kind + 1) * piece]
    for example in range(examples):
        total_ref[example] = jnp.dot(weights[...], grads[example], preferred_element_type=jnp.float32)


def early_stage(down_weight, gate_out, up_out, down_out, right, message, messages, swap, blocks):
    hidden, model_width = down_weight.shape
    rank = gate_out.shape[0]
    examples, both, seq_dev = blocks[0].shape
    width = model_width // NX
    rows = NX * hidden + rank
    operands = [down_weight, gate_out, up_out, down_out, right, message, *messages, swap, *blocks]
    return pl.pallas_call(
        early_kernel,
        out_shape=[
            jax.ShapeDtypeStruct((examples, rows, seq_dev), jnp.float32),
            jax.ShapeDtypeStruct((rows, both), jnp.bfloat16),
            jax.ShapeDtypeStruct((2 * rank, NX * hidden), jnp.bfloat16),
            jax.ShapeDtypeStruct(right.shape, right.dtype),
            jax.ShapeDtypeStruct((2 * hidden + rank, message.shape[1]), message.dtype),
        ],
        in_specs=[VMEM] * len(operands),
        out_specs=[VMEM] * 5,
        scratch_shapes=[
            pltpu.VMEM((rows, width), jnp.bfloat16),
            pltpu.VMEM((examples, width, seq_dev), jnp.bfloat16),
        ],
        compiler_params=pltpu.CompilerParams(vmem_limit_bytes=20 * MIB),
        cost_estimate=pl.CostEstimate(flops=2 * 10**9, bytes_accessed=4 * MIB, transcendentals=0),
        name="early_stage",
    )(*operands)


def tail_kernel(total_ref, far_ref, projs, right_ref, own_ref, *refs):
    near, far_halves, far_block, (out_ref, grads) = refs[:2], refs[2:4], refs[4:6], refs[6:]
    examples = total_ref.shape[0]
    seq_dev = total_ref.shape[2]
    rank, hidden = projs.shape[0] // 2, projs.shape[1] // NX
    top = 2 * hidden + rank
    piece = grads.shape[1] // NY
    y_at = lax.axis_index("yh")

    def factor_rows(step, first, last, columns):
        if step != 2:
            return (own_ref, near[0], None, near[1])[step][first:last, columns]
        rows = far_halves[0].shape[0]
        parts = [far_halves[0][first : min(last, rows), columns]] if first < rows else []
        if last > rows:
            parts.append(far_halves[1][max(first - rows, 0) : last - rows, columns])
        return jnp.concatenate(parts, axis=0)

    for example in range(examples):
        count = examples // 2
        for kind, y_of in enumerate((y_at, 1 - y_at)):
            rows = pl.ds(pl.multiple_of(y_of * piece, piece), piece)
            grads[example, rows, :] = far_block[example // count][example % count, kind * piece : (kind + 1) * piece]
    for example in range(examples):
        columns = slice(example * seq_dev, (example + 1) * seq_dev)
        total = total_ref[example] + jnp.dot(far_ref[...], grads[example], preferred_element_type=jnp.float32)
        left = []
        for kind in range(2):
            factor = jnp.concatenate(
                [factor_rows(step, kind * hidden, (kind + 1) * hidden, columns) for step in range(NX)], axis=0
            )
            product = total[: NX * hidden] * factor.astype(jnp.float32)
            high = product.astype(jnp.bfloat16)
            low = (product - high.astype(jnp.float32)).astype(jnp.bfloat16)
            proj = projs[kind * rank : (kind + 1) * rank, :]
            left.append(
                jnp.dot(proj, high, preferred_element_type=jnp.float32)
                + jnp.dot(proj, low, preferred_element_type=jnp.float32)
            )
        sides = jnp.dot(
            jnp.concatenate(left, axis=0),
            right_ref[columns, :],
            precision=lax.Precision.HIGHEST,
            preferred_element_type=jnp.float32,
        )
        right_down = factor_rows(0, 2 * hidden, top, columns).astype(jnp.float32)
        for step in range(1, NX):
            right_down = right_down + factor_rows(step, 2 * hidden, top, columns).astype(jnp.float32)
        out_ref[3 * example] = sides[:rank, :rank]
        out_ref[3 * example + 1] = sides[rank:, rank:]
        out_ref[3 * example + 2] = dot32(
            total[NX * hidden :], right_down, ((1,), (1,)), precision=lax.Precision.HIGHEST
        )


def tail_stage(total, far_weight, projs, right, factors, near, far, far_block):
    examples, _, seq_dev = total.shape
    rank = projs.shape[0] // 2
    operands = [total, far_weight, projs, right, factors, *near, *far, *far_block]
    return pl.pallas_call(
        tail_kernel,
        out_shape=jax.ShapeDtypeStruct((examples * 3, rank, rank), jnp.float32),
        in_specs=[VMEM] * len(operands),
        out_specs=VMEM,
        scratch_shapes=[pltpu.VMEM((examples, far_weight.shape[1], seq_dev), jnp.bfloat16)],
        compiler_params=pltpu.CompilerParams(vmem_limit_bytes=16 * MIB),
        cost_estimate=pl.CostEstimate(flops=2 * 10**9, bytes_accessed=4 * MIB, transcendentals=0),
        name="tail_stage",
    )(*operands)


def cut_kernel(up_ref, down_ref, before_ref, after_ref, sent_ref, first_ref, second_ref, swap_ref):
    first_ref[...] = up_ref[: first_ref.shape[0]]
    second_ref[...] = down_ref[first_ref.shape[0] :]
    half = swap_ref.shape[0] // 2
    top = before_ref.shape[0] - FOLD
    swap_ref[:half, :] = before_ref[top - half : top, :]
    swap_ref[half:, :] = after_ref[top - half : top, :]


def cut(up, down, before, after, sent, half):
    shape = jax.ShapeDtypeStruct((up.shape[0] // 2,) + up.shape[1:], up.dtype)
    return pl.pallas_call(
        cut_kernel,
        out_shape=[shape, shape, jax.ShapeDtypeStruct((2 * half, before.shape[1]), before.dtype)],
        in_specs=[VMEM] * 5,
        out_specs=[VMEM] * 3,
        compiler_params=pltpu.CompilerParams(vmem_limit_bytes=8 * MIB),
        name="cut",
    )(up, down, before, after, sent)


def ring_z(own, before, after, sent, half):
    up, down = [own], [own]
    for _ in range(NZ // 2 - 1):
        up.append(lax.ppermute(up[-1], "z", shifted(NZ, -1)))
        down.append(lax.ppermute(down[-1], "z", shifted(NZ, 1)))
    first, second, swap = cut(up[-1], down[-1], before, after, sent, half)
    swap = lax.ppermute(swap, "sc", shifted(SEQ_PARTS[1], 1))
    far = [lax.ppermute(first, "z", shifted(NZ, -1)), lax.ppermute(second, "z", shifted(NZ, 1))]
    return up + down[:0:-1], far, swap


def sum_everywhere(partial):
    count, size = partial.shape
    parts = SEQ_PARTS[0] * SEQ_PARTS[1] * NZ
    width = size // parts
    pieces = partial.reshape(count, parts, width).transpose(1, 0, 2)
    pieces = lax.all_to_all(pieces, ("sy", "sc", "z"), 0, 0, tiled=True)
    own = jnp.sum(pieces, axis=0)
    spread = jnp.broadcast_to(own[None], (NX * NZ * NY,) + own.shape)
    blocks = lax.all_to_all(spread, ("x", "z", "yh"), 0, 0, tiled=True)
    blocks = blocks.reshape(NX, NZ, NY, count, width).sum(axis=(0, 2))
    return blocks.transpose(1, 0, 2).reshape(count, NZ * width)


def shards(
    tokens,
    out_grad,
    gate_weight,
    up_weight,
    down_weight,
    proj_gate_in,
    proj_gate_out,
    proj_up_in,
    proj_up_out,
    proj_down_in,
    proj_down_out,
    lengths,
):
    examples, seq_dev, model_width = tokens.shape
    scale = float(seq_dev * SEQ_PARTS[0] * SEQ_PARTS[1]) ** (-0.5)
    gate_out, up_out = proj_gate_out.T, proj_up_out.T

    own_grad = out_grad.transpose(0, 2, 1)
    other_grad = lax.ppermute(own_grad, "yh", shifted(NY, 1))
    flat_tokens = tokens.reshape(examples * seq_dev, model_width)
    sent = token_stage(
        flat_tokens,
        gate_weight,
        up_weight,
        proj_gate_in.T,
        proj_up_in.T,
        proj_down_in.T,
        down_weight,
        gate_out,
        up_out,
        lengths,
        scale,
    )
    sent, right = sent[: NX - 1], sent[NX - 1]
    *sent, _ = hold([*sent, other_grad])
    pair = pair_up(own_grad, other_grad)
    messages = [lax.ppermute(piece, "x", shifted(NX, step)) for step, piece in enumerate(sent, 1)]
    hidden, rank = gate_weight.shape[1], gate_out.shape[0]
    rows = 2 * hidden + rank
    first, second = halves(messages[0], messages[2], rows // 2)
    far = [lax.ppermute(first, "x", shifted(NX, 1)), lax.ppermute(second, "x", shifted(NX, -1))]
    blocks, far_block, swap = ring_z(pair, messages[0], messages[2], first, hidden // 2)
    total, far_weight, projs, right, factors = early_stage(
        down_weight, gate_out, up_out, proj_down_out.T, right, sent[0], messages, swap, blocks
    )
    products = tail_stage(total, far_weight, projs, right, factors, messages[::2], far, far_block)
    total = sum_everywhere(products.reshape(examples * 3, -1))
    return total.reshape(examples, 3, -1)


def solution(mesh):
    fine = Mesh(mesh.devices.reshape(SEQ_PARTS + FSDP_PARTS), ("sy", "sc", "x", "z", "yh"))
    seq, fsdp = ("sy", "sc"), ("x", "z", "yh")
    placed = (
        P(None, seq, None),
        P(None, seq, fsdp),
        P(None, fsdp),
        P(None, fsdp),
        P(fsdp, None),
        P(),
        P(fsdp, None),
        P(),
        P(fsdp, None),
        P(fsdp, None),
        P(),
        P(),
    )
    return jax.shard_map(
        shards, mesh=fine, in_specs=placed, out_specs=P(None, None, seq), check_vma=False
    )
```

```python
import jax
import jax.numpy as jnp
from jax import lax
from jax.experimental import pallas as pl
from jax.experimental.pallas import tpu as pltpu
from jax.sharding import Mesh, PartitionSpec as P

SEQ_PARTS = (2, 2)
FSDP_PARTS = (4, 8, 2)
NX, NZ, NY = FSDP_PARTS
FOLD = 16
MIB = 1024 * 1024
VMEM = pl.BlockSpec(memory_space=pltpu.VMEM)
HBM = pl.BlockSpec(memory_space=pltpu.HBM)


def shifted(count, step):
    return [(i, (i + step) % count) for i in range(count)]


def dot32(a, b, dims, precision=None):
    return lax.dot_general(a, b, (dims, ((), ())), preferred_element_type=jnp.float32, precision=precision)


def hold_kernel(*refs):
    pass


def hold(arrays):
    return pl.pallas_call(
        hold_kernel,
        out_shape=[jax.ShapeDtypeStruct(array.shape, array.dtype) for array in arrays],
        in_specs=[HBM] * len(arrays),
        out_specs=[HBM] * len(arrays),
        input_output_aliases={index: index for index in range(len(arrays))},
        compiler_params=pltpu.CompilerParams(vmem_limit_bytes=62 * MIB),
        name="hold",
    )(*arrays)


def pair_kernel(own_ref, other_ref, out_ref):
    piece = own_ref.shape[1]
    out_ref[:, :piece, :] = own_ref[...]
    out_ref[:, piece:, :] = other_ref[...]


def pair_up(own, other):
    examples, piece, seq_dev = own.shape
    return pl.pallas_call(
        pair_kernel,
        out_shape=jax.ShapeDtypeStruct((examples, NY * piece, seq_dev), own.dtype),
        in_specs=[VMEM] * 2,
        out_specs=VMEM,
        compiler_params=pltpu.CompilerParams(vmem_limit_bytes=4 * MIB),
        name="pair_up",
    )(own, other)


def token_kernel(chunk, scale, lengths_ref, tokens_hbm, gate_hbm, up_hbm, gate_in_hbm, up_in_hbm, down_in_hbm, down_hbm, gate_out_hbm, up_out_hbm, *refs):
    messages, right_ref = refs[: NX - 1], refs[NX - 1]
    tokens_ref, weight_ref, in_ref, down_in_ref, out_ref, total_ref, sems = refs[NX:]
    rows, model_width = tokens_hbm.shape
    hidden = gate_hbm.shape[1]
    rank = gate_in_hbm.shape[0]
    examples = lengths_ref.shape[0]
    seq_dev = rows // examples
    groups, count = [], 0
    for start in range(0, model_width, chunk):
        part = pl.ds(start, chunk)
        pairs = [
            (tokens_hbm.at[:, part], tokens_ref.at[:, part]),
            (gate_hbm.at[part], weight_ref.at[part, pl.ds(0, hidden)]),
            (up_hbm.at[part], weight_ref.at[part, pl.ds(hidden, hidden)]),
            (gate_in_hbm.at[:, part], in_ref.at[pl.ds(0, rank), part]),
            (up_in_hbm.at[:, part], in_ref.at[pl.ds(rank, rank), part]),
        ]
        if start + chunk == model_width:
            pairs.append((down_in_hbm, down_in_ref))
        groups.append([pltpu.make_async_copy(a, b, sems.at[count + k]) for k, (a, b) in enumerate(pairs)])
        count += len(pairs)
        for copy in groups[-1]:
            copy.start()
    top = 2 * hidden + rank
    width, half = model_width // NX, hidden // 2
    core = lax.axis_index("sc")
    pairs = [(gate_out_hbm, out_ref.at[pl.ds(0, rank)]), (up_out_hbm, out_ref.at[pl.ds(rank, rank)])]
    for step, message in enumerate(messages, 1):
        start = pl.multiple_of(lax.rem(lax.axis_index("x") + step, NX) * width, width)
        columns = pl.ds(start, width)
        if step == 2:
            pairs.append((down_hbm.at[:, columns], message.at[pl.ds(0, hidden)]))
        else:
            pairs.append((down_hbm.at[pl.ds(core * half, half), columns], message.at[pl.ds(top, half)]))
    extra = [pltpu.make_async_copy(a, b, sems.at[count + k]) for k, (a, b) in enumerate(pairs)]
    for copy in extra:
        copy.start()
    for index, group in enumerate(groups):
        for copy in group:
            copy.wait()
        part = slice(index * chunk, (index + 1) * chunk)
        values = jnp.dot(tokens_ref[:, part], weight_ref[part, :], preferred_element_type=jnp.float32)
        right = dot32(tokens_ref[:, part], in_ref[:, part], ((1,), (1,)))
        if index == 0:
            total_ref[...] = values
            right_ref[...] = right
        else:
            total_ref[...] += values
            right_ref[...] += right

    tile = min(256, seq_dev)
    seq_index = lax.axis_index("sy") * SEQ_PARTS[1] + lax.axis_index("sc")
    for step in range(rows // tile):
        span = slice(step * tile, (step + 1) * tile)
        gate, up = total_ref[span, :hidden], total_ref[span, hidden:]
        sigmoid = 1.0 / (1.0 + jnp.exp(-gate))
        silu = gate * sigmoid
        factor_gate = up * sigmoid * (1.0 + gate * (1.0 - sigmoid))
        hidden_value = (silu * up).astype(jnp.bfloat16)
        factor_gate = factor_gate.T.astype(jnp.bfloat16)
        factor_up = silu.T.astype(jnp.bfloat16)

        first = seq_index * seq_dev + step * tile % seq_dev
        limit = lengths_ref[step * tile // seq_dev]
        columns = first + lax.broadcasted_iota(jnp.int32, (rank, tile), 1)
        right_down = dot32(down_in_ref[...], hidden_value, ((1,), (1,)))
        right_down = jnp.where(columns < limit, right_down * scale, 0.0).astype(jnp.bfloat16)
        for message in messages[::2]:
            message[:hidden, span] = factor_gate
            message[hidden : 2 * hidden, span] = factor_up
            message[2 * hidden : top, span] = right_down
        rows_at = first + lax.broadcasted_iota(jnp.int32, (tile, 2 * rank), 0)
        right_ref[span, :] = jnp.where(rows_at < limit, right_ref[span, :] * scale, 0.0)
    for copy in extra:
        copy.wait()
    for message in messages:
        for block in range(2 * rank // FOLD):
            rows_of = slice(block * FOLD, (block + 1) * FOLD)
            message[-FOLD:, block * hidden : (block + 1) * hidden] = out_ref[rows_of, :]


def token_stage(tokens, gate_weight, up_weight, gate_in, up_in, down_in, down_weight, gate_out, up_out, lengths, scale):
    rows, width = tokens.shape
    hidden = gate_weight.shape[1]
    rank = gate_in.shape[0]
    chunk = 512
    return pl.pallas_call(
        lambda *refs: token_kernel(chunk, scale, *refs),
        out_shape=[
            jax.ShapeDtypeStruct((2 * hidden + hidden // 2 + rank + FOLD, rows), jnp.bfloat16),
            jax.ShapeDtypeStruct((hidden + FOLD, rows), jnp.bfloat16),
            jax.ShapeDtypeStruct((2 * hidden + hidden // 2 + rank + FOLD, rows), jnp.bfloat16),
            jax.ShapeDtypeStruct((rows, 2 * rank), jnp.float32),
        ],
        in_specs=[pl.BlockSpec(memory_space=pltpu.SMEM)] + [HBM] * 9,
        out_specs=[VMEM] * NX,
        scratch_shapes=[
            pltpu.VMEM((rows, width), jnp.bfloat16),
            pltpu.VMEM((width, 2 * hidden), jnp.bfloat16),
            pltpu.VMEM((2 * rank, width), jnp.bfloat16),
            pltpu.VMEM((rank, hidden), jnp.bfloat16),
            pltpu.VMEM((2 * rank, hidden), jnp.bfloat16),
            pltpu.VMEM((rows, 2 * hidden), jnp.float32),
            pltpu.SemaphoreType.DMA((5 * (width // chunk) + 2 + NX,)),
        ],
        compiler_params=pltpu.CompilerParams(vmem_limit_bytes=61 * MIB),
        cost_estimate=pl.CostEstimate(
            flops=2 * rows * width * 512, bytes_accessed=16 * MIB, transcendentals=rows * hidden
        ),
        name="token_stage",
    )(lengths, tokens, gate_weight, up_weight, gate_in, up_in, down_in, down_weight, gate_out, up_out)


def forward_kernel(before_ref, after_ref, first_ref, second_ref, swap_ref):
    rows = first_ref.shape[0]
    half = swap_ref.shape[0] // 2
    first_ref[...] = before_ref[:rows, :]
    second_ref[...] = after_ref[rows : 2 * rows, :]
    swap_ref[:half, :] = before_ref[2 * rows : 2 * rows + half, :]
    swap_ref[half:, :] = after_ref[2 * rows : 2 * rows + half, :]


def halves(before, after, rows, half):
    shape = jax.ShapeDtypeStruct((rows, before.shape[1]), before.dtype)
    swap = jax.ShapeDtypeStruct((2 * half, before.shape[1]), before.dtype)
    return pl.pallas_call(
        forward_kernel,
        out_shape=[shape, shape, swap],
        in_specs=[VMEM] * 2,
        out_specs=[VMEM] * 3,
        compiler_params=pltpu.CompilerParams(vmem_limit_bytes=8 * MIB),
        name="halves",
    )(before, after)


def keep_kernel(message_ref, right_ref, factors_out, right_out):
    factors_out[...] = message_ref[: factors_out.shape[0], :]
    right_out[...] = right_ref[...]


def keep(message, right, rows):
    return pl.pallas_call(
        keep_kernel,
        out_shape=[
            jax.ShapeDtypeStruct((rows, message.shape[1]), message.dtype),
            jax.ShapeDtypeStruct(right.shape, right.dtype),
        ],
        in_specs=[VMEM] * 2,
        out_specs=[VMEM] * 2,
        compiler_params=pltpu.CompilerParams(vmem_limit_bytes=8 * MIB),
        name="keep",
    )(message, right)


def tail_kernel(weight_ref, gate_out_ref, up_out_ref, down_out_ref, right_ref, *refs):
    own_ref, messages, far_halves, swap_ref = refs[0], refs[1:NX], refs[NX : NX + 2], refs[NX + 2]
    blocks, far_block = refs[NX + 3 : NX + 2 + NZ], refs[NX + 2 + NZ : NX + 4 + NZ]
    out_ref, weights, projs, grads = refs[NX + 4 + NZ :]
    hidden, model_width = weight_ref.shape
    rank = gate_out_ref.shape[0]
    width = model_width // NX
    examples, both, seq_dev = blocks[0].shape
    piece = both // NY
    top, half, core = 2 * hidden + rank, hidden // 2, lax.axis_index("sc")
    x_at, z_at, y_at = lax.axis_index("x"), lax.axis_index("z"), lax.axis_index("yh")

    start = pl.multiple_of(x_at * width, width)
    weights[:hidden, :] = weight_ref[:, pl.ds(start, width)]
    weights[NX * hidden :, :] = down_out_ref[:, pl.ds(start, width)]
    projs[:rank, :hidden] = gate_out_ref[...]
    projs[rank:, :hidden] = up_out_ref[...]
    for step, message in enumerate(messages, 1):
        if step == 2:
            weights[step * hidden : (step + 1) * hidden, :] = message[:hidden, :]
        else:
            mine = pl.ds(pl.multiple_of(step * hidden + core * half, half), half)
            theirs = pl.ds(pl.multiple_of(step * hidden + (1 - core) * half, half), half)
            weights[mine, :] = message[top : top + half, :]
            weights[theirs, :] = swap_ref[step // 2 * half : (step // 2 + 1) * half, :]
        columns = slice(step * hidden, (step + 1) * hidden)
        for block in range(2 * rank // FOLD):
            folded = message[-FOLD:, block * hidden : (block + 1) * hidden]
            projs[block * FOLD : (block + 1) * FOLD, columns] = folded

    def factor_rows(step, first, last, columns):
        if step != 2:
            return (own_ref if step == 0 else messages[step - 1])[first:last, columns]
        rows = far_halves[0].shape[0]
        parts = [far_halves[0][first : min(last, rows), columns]] if first < rows else []
        if last > rows:
            parts.append(far_halves[1][max(first - rows, 0) : last - rows, columns])
        return jnp.concatenate(parts, axis=0)

    for example in range(examples):
        for step in range(NZ):
            if step == NZ // 2:
                count = examples // 2
                block = far_block[example // count][example % count]
            else:
                block = blocks[step if step < NZ // 2 else step - 1][example]
            base = lax.rem(z_at + step, NZ) * both
            for kind, y_of in enumerate((y_at, 1 - y_at)):
                rows = pl.ds(pl.multiple_of(base + y_of * piece, piece), piece)
                grads[example, rows, :] = block[kind * piece : (kind + 1) * piece]
    for example in range(examples):
        columns = slice(example * seq_dev, (example + 1) * seq_dev)
        total = jnp.dot(weights[...], grads[example], preferred_element_type=jnp.float32)
        left = []
        for kind in range(2):
            factor = jnp.concatenate(
                [factor_rows(step, kind * hidden, (kind + 1) * hidden, columns) for step in range(NX)], axis=0
            )
            product = total[: NX * hidden] * factor.astype(jnp.float32)
            high = product.astype(jnp.bfloat16)
            low = (product - high.astype(jnp.float32)).astype(jnp.bfloat16)
            proj = projs[kind * rank : (kind + 1) * rank, :]
            left.append(
                jnp.dot(proj, high, preferred_element_type=jnp.float32)
                + jnp.dot(proj, low, preferred_element_type=jnp.float32)
            )
        sides = jnp.dot(
            jnp.concatenate(left, axis=0),
            right_ref[columns, :],
            precision=lax.Precision.HIGHEST,
            preferred_element_type=jnp.float32,
        )
        right_down = factor_rows(0, 2 * hidden, top, columns).astype(jnp.float32)
        for step in range(1, NX):
            right_down = right_down + factor_rows(step, 2 * hidden, top, columns).astype(jnp.float32)
        out_ref[3 * example] = sides[:rank, :rank]
        out_ref[3 * example + 1] = sides[rank:, rank:]
        out_ref[3 * example + 2] = dot32(
            total[NX * hidden :], right_down, ((1,), (1,)), precision=lax.Precision.HIGHEST
        )


def tail_stage(down_weight, gate_out, up_out, down_out, right, factors, messages, far, swap, blocks, far_block):
    hidden, model_width = down_weight.shape
    rank = gate_out.shape[0]
    examples, _, seq_dev = blocks[0].shape
    width = model_width // NX
    operands = [down_weight, gate_out, up_out, down_out, right, factors, *messages, *far, swap, *blocks, *far_block]
    return pl.pallas_call(
        tail_kernel,
        out_shape=jax.ShapeDtypeStruct((examples * 3, rank, rank), jnp.float32),
        in_specs=[VMEM] * len(operands),
        out_specs=VMEM,
        scratch_shapes=[
            pltpu.VMEM((NX * hidden + rank, width), jnp.bfloat16),
            pltpu.VMEM((2 * rank, NX * hidden), jnp.bfloat16),
            pltpu.VMEM((examples, width, seq_dev), jnp.bfloat16),
        ],
        compiler_params=pltpu.CompilerParams(vmem_limit_bytes=20 * MIB),
        cost_estimate=pl.CostEstimate(flops=4 * 10**9, bytes_accessed=8 * MIB, transcendentals=0),
        name="tail_stage",
    )(*operands)


def cut_kernel(up_ref, down_ref, first_ref, second_ref):
    first_ref[...] = up_ref[: first_ref.shape[0]]
    second_ref[...] = down_ref[first_ref.shape[0] :]


def cut(up, down):
    shape = jax.ShapeDtypeStruct((up.shape[0] // 2,) + up.shape[1:], up.dtype)
    return pl.pallas_call(
        cut_kernel,
        out_shape=[shape] * 2,
        in_specs=[VMEM] * 2,
        out_specs=[VMEM] * 2,
        compiler_params=pltpu.CompilerParams(vmem_limit_bytes=4 * MIB),
        name="cut",
    )(up, down)


def ring_z(own):
    up, down = [own], [own]
    for _ in range(NZ // 2 - 1):
        up.append(lax.ppermute(up[-1], "z", shifted(NZ, -1)))
        down.append(lax.ppermute(down[-1], "z", shifted(NZ, 1)))
    first, second = cut(up[-1], down[-1])
    far = [lax.ppermute(first, "z", shifted(NZ, -1)), lax.ppermute(second, "z", shifted(NZ, 1))]
    return up + down[:0:-1], far


def sum_everywhere(partial):
    count, size = partial.shape
    parts = SEQ_PARTS[0] * SEQ_PARTS[1] * NZ
    width = size // parts
    pieces = partial.reshape(count, parts, width).transpose(1, 0, 2)
    pieces = lax.all_to_all(pieces, ("sy", "sc", "z"), 0, 0, tiled=True)
    own = jnp.sum(pieces, axis=0)
    spread = jnp.broadcast_to(own[None], (NX * NZ * NY,) + own.shape)
    blocks = lax.all_to_all(spread, ("x", "z", "yh"), 0, 0, tiled=True)
    blocks = blocks.reshape(NX, NZ, NY, count, width).sum(axis=(0, 2))
    return blocks.transpose(1, 0, 2).reshape(count, NZ * width)


def shards(
    tokens,
    out_grad,
    gate_weight,
    up_weight,
    down_weight,
    proj_gate_in,
    proj_gate_out,
    proj_up_in,
    proj_up_out,
    proj_down_in,
    proj_down_out,
    lengths,
):
    examples, seq_dev, model_width = tokens.shape
    scale = float(seq_dev * SEQ_PARTS[0] * SEQ_PARTS[1]) ** (-0.5)
    gate_out, up_out = proj_gate_out.T, proj_up_out.T

    own_grad = out_grad.transpose(0, 2, 1)
    other_grad = lax.ppermute(own_grad, "yh", shifted(NY, 1))
    flat_tokens = tokens.reshape(examples * seq_dev, model_width)
    sent = token_stage(
        flat_tokens,
        gate_weight,
        up_weight,
        proj_gate_in.T,
        proj_up_in.T,
        proj_down_in.T,
        down_weight,
        gate_out,
        up_out,
        lengths,
        scale,
    )
    sent, right = sent[: NX - 1], sent[NX - 1]
    *sent, _ = hold([*sent, other_grad])
    pair = pair_up(own_grad, other_grad)
    messages = [lax.ppermute(piece, "x", shifted(NX, step)) for step, piece in enumerate(sent, 1)]
    hidden, rank = gate_weight.shape[1], gate_out.shape[0]
    rows = 2 * hidden + rank
    first, second, swap = halves(messages[0], messages[2], rows // 2, hidden // 2)
    swap = lax.ppermute(swap, "sc", shifted(SEQ_PARTS[1], 1))
    far = [lax.ppermute(first, "x", shifted(NX, 1)), lax.ppermute(second, "x", shifted(NX, -1))]
    blocks, far_block = ring_z(pair)
    factors, right = keep(sent[0], right, rows)
    products = tail_stage(
        down_weight, gate_out, up_out, proj_down_out.T, right, factors, messages, far, swap, blocks, far_block
    )
    total = sum_everywhere(products.reshape(examples * 3, -1))
    return total.reshape(examples, 3, -1)


def solution(mesh):
    fine = Mesh(mesh.devices.reshape(SEQ_PARTS + FSDP_PARTS), ("sy", "sc", "x", "z", "yh"))
    seq, fsdp = ("sy", "sc"), ("x", "z", "yh")
    placed = (
        P(None, seq, None),
        P(None, seq, fsdp),
        P(None, fsdp),
        P(None, fsdp),
        P(fsdp, None),
        P(),
        P(fsdp, None),
        P(),
        P(fsdp, None),
        P(fsdp, None),
        P(),
        P(),
    )
    return jax.shard_map(
        shards, mesh=fine, in_specs=placed, out_specs=P(None, None, seq), check_vma=False
    )
```

```python
import jax
import jax.numpy as jnp
from jax import lax
from jax.experimental import pallas as pl
from jax.experimental.pallas import tpu as pltpu
from jax.sharding import Mesh, PartitionSpec as P

SEQ_PARTS = (2, 2)
FSDP_PARTS = (4, 8, 2)
NX, NZ, NY = FSDP_PARTS
FOLD = 16
MIB = 1024 * 1024
VMEM = pl.BlockSpec(memory_space=pltpu.VMEM)
HBM = pl.BlockSpec(memory_space=pltpu.HBM)


def shifted(count, step):
    return [(i, (i + step) % count) for i in range(count)]


def dot32(a, b, dims, precision=None):
    return lax.dot_general(a, b, (dims, ((), ())), preferred_element_type=jnp.float32, precision=precision)


def hold_kernel(*refs):
    pass


def hold(arrays):
    return pl.pallas_call(
        hold_kernel,
        out_shape=[jax.ShapeDtypeStruct(array.shape, array.dtype) for array in arrays],
        in_specs=[HBM] * len(arrays),
        out_specs=[HBM] * len(arrays),
        input_output_aliases={index: index for index in range(len(arrays))},
        compiler_params=pltpu.CompilerParams(vmem_limit_bytes=62 * MIB),
        name="hold",
    )(*arrays)


def pair_kernel(own_ref, other_ref, out_ref):
    piece = own_ref.shape[1]
    out_ref[:, :piece, :] = own_ref[...]
    out_ref[:, piece:, :] = other_ref[...]


def pair_up(own, other):
    examples, piece, seq_dev = own.shape
    return pl.pallas_call(
        pair_kernel,
        out_shape=jax.ShapeDtypeStruct((examples, NY * piece, seq_dev), own.dtype),
        in_specs=[VMEM] * 2,
        out_specs=VMEM,
        compiler_params=pltpu.CompilerParams(vmem_limit_bytes=4 * MIB),
        name="pair_up",
    )(own, other)


def token_kernel(chunk, scale, lengths_ref, tokens_hbm, gate_hbm, up_hbm, gate_in_hbm, up_in_hbm, down_in_hbm, down_hbm, gate_out_hbm, up_out_hbm, *refs):
    messages, right_ref = refs[: NX - 1], refs[NX - 1]
    tokens_ref, weight_ref, in_ref, down_in_ref, out_ref, total_ref, sems = refs[NX:]
    rows, model_width = tokens_hbm.shape
    hidden = gate_hbm.shape[1]
    rank = gate_in_hbm.shape[0]
    examples = lengths_ref.shape[0]
    seq_dev = rows // examples
    groups, count = [], 0
    for start in range(0, model_width, chunk):
        part = pl.ds(start, chunk)
        pairs = [
            (tokens_hbm.at[:, part], tokens_ref.at[:, part]),
            (gate_hbm.at[part], weight_ref.at[part, pl.ds(0, hidden)]),
            (up_hbm.at[part], weight_ref.at[part, pl.ds(hidden, hidden)]),
            (gate_in_hbm.at[:, part], in_ref.at[pl.ds(0, rank), part]),
            (up_in_hbm.at[:, part], in_ref.at[pl.ds(rank, rank), part]),
        ]
        if start + chunk == model_width:
            pairs.append((down_in_hbm, down_in_ref))
        groups.append([pltpu.make_async_copy(a, b, sems.at[count + k]) for k, (a, b) in enumerate(pairs)])
        count += len(pairs)
        for copy in groups[-1]:
            copy.start()
    top = 2 * hidden + rank
    width, half = model_width // NX, hidden // 2
    core = lax.axis_index("sc")
    pairs = [(gate_out_hbm, out_ref.at[pl.ds(0, rank)]), (up_out_hbm, out_ref.at[pl.ds(rank, rank)])]
    for step, message in enumerate(messages, 1):
        start = pl.multiple_of(lax.rem(lax.axis_index("x") + step, NX) * width, width)
        columns = pl.ds(start, width)
        if step == 2:
            pairs.append((down_hbm.at[:, columns], message.at[pl.ds(0, hidden)]))
        else:
            pairs.append((down_hbm.at[pl.ds(core * half, half), columns], message.at[pl.ds(top, half)]))
    extra = [pltpu.make_async_copy(a, b, sems.at[count + k]) for k, (a, b) in enumerate(pairs)]
    for copy in extra:
        copy.start()
    for index, group in enumerate(groups):
        for copy in group:
            copy.wait()
        part = slice(index * chunk, (index + 1) * chunk)
        values = jnp.dot(tokens_ref[:, part], weight_ref[part, :], preferred_element_type=jnp.float32)
        right = dot32(tokens_ref[:, part], in_ref[:, part], ((1,), (1,)))
        if index == 0:
            total_ref[...] = values
            right_ref[...] = right
        else:
            total_ref[...] += values
            right_ref[...] += right

    tile = min(256, seq_dev)
    seq_index = lax.axis_index("sy") * SEQ_PARTS[1] + lax.axis_index("sc")
    for step in range(rows // tile):
        span = slice(step * tile, (step + 1) * tile)
        gate, up = total_ref[span, :hidden], total_ref[span, hidden:]
        sigmoid = 1.0 / (1.0 + jnp.exp(-gate))
        silu = gate * sigmoid
        factor_gate = up * sigmoid * (1.0 + gate * (1.0 - sigmoid))
        hidden_value = (silu * up).astype(jnp.bfloat16)
        factor_gate = factor_gate.T.astype(jnp.bfloat16)
        factor_up = silu.T.astype(jnp.bfloat16)

        first = seq_index * seq_dev + step * tile % seq_dev
        limit = lengths_ref[step * tile // seq_dev]
        columns = first + lax.broadcasted_iota(jnp.int32, (rank, tile), 1)
        right_down = dot32(down_in_ref[...], hidden_value, ((1,), (1,)))
        right_down = jnp.where(columns < limit, right_down * scale, 0.0).astype(jnp.bfloat16)
        for message in messages[::2]:
            message[:hidden, span] = factor_gate
            message[hidden : 2 * hidden, span] = factor_up
            message[2 * hidden : top, span] = right_down
        rows_at = first + lax.broadcasted_iota(jnp.int32, (tile, 2 * rank), 0)
        right_ref[span, :] = jnp.where(rows_at < limit, right_ref[span, :] * scale, 0.0)
    for copy in extra:
        copy.wait()
    for message in messages:
        for block in range(2 * rank // FOLD):
            rows_of = slice(block * FOLD, (block + 1) * FOLD)
            message[-FOLD:, block * hidden : (block + 1) * hidden] = out_ref[rows_of, :]


def token_stage(tokens, gate_weight, up_weight, gate_in, up_in, down_in, down_weight, gate_out, up_out, lengths, scale):
    rows, width = tokens.shape
    hidden = gate_weight.shape[1]
    rank = gate_in.shape[0]
    chunk = 512
    return pl.pallas_call(
        lambda *refs: token_kernel(chunk, scale, *refs),
        out_shape=[
            jax.ShapeDtypeStruct((2 * hidden + hidden // 2 + rank + FOLD, rows), jnp.bfloat16),
            jax.ShapeDtypeStruct((hidden + FOLD, rows), jnp.bfloat16),
            jax.ShapeDtypeStruct((2 * hidden + hidden // 2 + rank + FOLD, rows), jnp.bfloat16),
            jax.ShapeDtypeStruct((rows, 2 * rank), jnp.float32),
        ],
        in_specs=[pl.BlockSpec(memory_space=pltpu.SMEM)] + [HBM] * 9,
        out_specs=[VMEM] * NX,
        scratch_shapes=[
            pltpu.VMEM((rows, width), jnp.bfloat16),
            pltpu.VMEM((width, 2 * hidden), jnp.bfloat16),
            pltpu.VMEM((2 * rank, width), jnp.bfloat16),
            pltpu.VMEM((rank, hidden), jnp.bfloat16),
            pltpu.VMEM((2 * rank, hidden), jnp.bfloat16),
            pltpu.VMEM((rows, 2 * hidden), jnp.float32),
            pltpu.SemaphoreType.DMA((5 * (width // chunk) + 2 + NX,)),
        ],
        compiler_params=pltpu.CompilerParams(vmem_limit_bytes=61 * MIB),
        cost_estimate=pl.CostEstimate(
            flops=2 * rows * width * 512, bytes_accessed=16 * MIB, transcendentals=rows * hidden
        ),
        name="token_stage",
    )(lengths, tokens, gate_weight, up_weight, gate_in, up_in, down_in, down_weight, gate_out, up_out)


def forward_kernel(before_ref, after_ref, first_ref, second_ref, swap_ref):
    rows = first_ref.shape[0]
    half = swap_ref.shape[0] // 2
    first_ref[...] = before_ref[:rows, :]
    second_ref[...] = after_ref[rows : 2 * rows, :]
    swap_ref[:half, :] = before_ref[2 * rows : 2 * rows + half, :]
    swap_ref[half:, :] = after_ref[2 * rows : 2 * rows + half, :]


def halves(before, after, rows, half):
    shape = jax.ShapeDtypeStruct((rows, before.shape[1]), before.dtype)
    swap = jax.ShapeDtypeStruct((2 * half, before.shape[1]), before.dtype)
    return pl.pallas_call(
        forward_kernel,
        out_shape=[shape, shape, swap],
        in_specs=[VMEM] * 2,
        out_specs=[VMEM] * 3,
        compiler_params=pltpu.CompilerParams(vmem_limit_bytes=8 * MIB),
        name="halves",
    )(before, after)


def keep_kernel(message_ref, right_ref, factors_out, right_out):
    factors_out[...] = message_ref[: factors_out.shape[0], :]
    right_out[...] = right_ref[...]


def keep(message, right, rows):
    return pl.pallas_call(
        keep_kernel,
        out_shape=[
            jax.ShapeDtypeStruct((rows, message.shape[1]), message.dtype),
            jax.ShapeDtypeStruct(right.shape, right.dtype),
        ],
        in_specs=[VMEM] * 2,
        out_specs=[VMEM] * 2,
        compiler_params=pltpu.CompilerParams(vmem_limit_bytes=8 * MIB),
        name="keep",
    )(message, right)


def tail_kernel(weight_ref, gate_out_ref, up_out_ref, down_out_ref, right_ref, *refs):
    own_ref, messages, far_halves, swap_ref = refs[0], refs[1:NX], refs[NX : NX + 2], refs[NX + 2]
    blocks, far_block = refs[NX + 3 : NX + 2 + NZ], refs[NX + 2 + NZ : NX + 4 + NZ]
    out_ref, weights, projs, grads = refs[NX + 4 + NZ :]
    hidden, model_width = weight_ref.shape
    rank = gate_out_ref.shape[0]
    width = model_width // NX
    examples, both, seq_dev = blocks[0].shape
    piece = both // NY
    top, half, core = 2 * hidden + rank, hidden // 2, lax.axis_index("sc")
    x_at, z_at, y_at = lax.axis_index("x"), lax.axis_index("z"), lax.axis_index("yh")

    start = pl.multiple_of(x_at * width, width)
    weights[:hidden, :] = weight_ref[:, pl.ds(start, width)]
    weights[NX * hidden :, :] = down_out_ref[:, pl.ds(start, width)]
    projs[:rank, :hidden] = gate_out_ref[...]
    projs[rank:, :hidden] = up_out_ref[...]
    for step, message in enumerate(messages, 1):
        if step == 2:
            weights[step * hidden : (step + 1) * hidden, :] = message[:hidden, :]
        else:
            mine = pl.ds(pl.multiple_of(step * hidden + core * half, half), half)
            theirs = pl.ds(pl.multiple_of(step * hidden + (1 - core) * half, half), half)
            weights[mine, :] = message[top : top + half, :]
            weights[theirs, :] = swap_ref[step // 2 * half : (step // 2 + 1) * half, :]
        columns = slice(step * hidden, (step + 1) * hidden)
        for block in range(2 * rank // FOLD):
            folded = message[-FOLD:, block * hidden : (block + 1) * hidden]
            projs[block * FOLD : (block + 1) * FOLD, columns] = folded

    def factor_rows(step, first, last, columns):
        if step != 2:
            return (own_ref if step == 0 else messages[step - 1])[first:last, columns]
        rows = far_halves[0].shape[0]
        parts = [far_halves[0][first : min(last, rows), columns]] if first < rows else []
        if last > rows:
            parts.append(far_halves[1][max(first - rows, 0) : last - rows, columns])
        return jnp.concatenate(parts, axis=0)

    for example in range(examples):
        for step in range(NZ):
            if step == NZ // 2:
                count = examples // 2
                block = far_block[example // count][example % count]
            else:
                block = blocks[step if step < NZ // 2 else step - 1][example]
            base = lax.rem(z_at + step, NZ) * both
            for kind, y_of in enumerate((y_at, 1 - y_at)):
                rows = pl.ds(pl.multiple_of(base + y_of * piece, piece), piece)
                grads[example, rows, :] = block[kind * piece : (kind + 1) * piece]
    for example in range(examples):
        columns = slice(example * seq_dev, (example + 1) * seq_dev)
        total = jnp.dot(weights[...], grads[example], preferred_element_type=jnp.float32)
        left = []
        for kind in range(2):
            factor = jnp.concatenate(
                [factor_rows(step, kind * hidden, (kind + 1) * hidden, columns) for step in range(NX)], axis=0
            )
            product = total[: NX * hidden] * factor.astype(jnp.float32)
            high = product.astype(jnp.bfloat16)
            low = (product - high.astype(jnp.float32)).astype(jnp.bfloat16)
            proj = projs[kind * rank : (kind + 1) * rank, :]
            left.append(
                jnp.dot(proj, high, preferred_element_type=jnp.float32)
                + jnp.dot(proj, low, preferred_element_type=jnp.float32)
            )
        sides = jnp.dot(
            jnp.concatenate(left, axis=0),
            right_ref[columns, :],
            precision=lax.Precision.HIGHEST,
            preferred_element_type=jnp.float32,
        )
        right_down = factor_rows(0, 2 * hidden, top, columns).astype(jnp.float32)
        for step in range(1, NX):
            right_down = right_down + factor_rows(step, 2 * hidden, top, columns).astype(jnp.float32)
        out_ref[example] = sides[:rank, :rank]
        out_ref[1 * examples + example] = sides[rank:, rank:]
        out_ref[2 * examples + example] = dot32(
            total[NX * hidden :], right_down, ((1,), (1,)), precision=lax.Precision.HIGHEST
        )


def tail_stage(down_weight, gate_out, up_out, down_out, right, factors, messages, far, swap, blocks, far_block):
    hidden, model_width = down_weight.shape
    rank = gate_out.shape[0]
    examples, _, seq_dev = blocks[0].shape
    width = model_width // NX
    operands = [down_weight, gate_out, up_out, down_out, right, factors, *messages, *far, swap, *blocks, *far_block]
    return pl.pallas_call(
        tail_kernel,
        out_shape=jax.ShapeDtypeStruct((examples * 3, rank, rank), jnp.float32),
        in_specs=[VMEM] * len(operands),
        out_specs=VMEM,
        scratch_shapes=[
            pltpu.VMEM((NX * hidden + rank, width), jnp.bfloat16),
            pltpu.VMEM((2 * rank, NX * hidden), jnp.bfloat16),
            pltpu.VMEM((examples, width, seq_dev), jnp.bfloat16),
        ],
        compiler_params=pltpu.CompilerParams(vmem_limit_bytes=20 * MIB),
        cost_estimate=pl.CostEstimate(flops=4 * 10**9, bytes_accessed=8 * MIB, transcendentals=0),
        name="tail_stage",
    )(*operands)


def cut_kernel(up_ref, down_ref, first_ref, second_ref):
    first_ref[...] = up_ref[: first_ref.shape[0]]
    second_ref[...] = down_ref[first_ref.shape[0] :]


def cut(up, down):
    shape = jax.ShapeDtypeStruct((up.shape[0] // 2,) + up.shape[1:], up.dtype)
    return pl.pallas_call(
        cut_kernel,
        out_shape=[shape] * 2,
        in_specs=[VMEM] * 2,
        out_specs=[VMEM] * 2,
        compiler_params=pltpu.CompilerParams(vmem_limit_bytes=4 * MIB),
        name="cut",
    )(up, down)


def ring_z(own):
    up, down = [own], [own]
    for _ in range(NZ // 2 - 1):
        up.append(lax.ppermute(up[-1], "z", shifted(NZ, -1)))
        down.append(lax.ppermute(down[-1], "z", shifted(NZ, 1)))
    first, second = cut(up[-1], down[-1])
    far = [lax.ppermute(first, "z", shifted(NZ, -1)), lax.ppermute(second, "z", shifted(NZ, 1))]
    return up + down[:0:-1], far


def sum_everywhere(partial):
    count, size = partial.shape
    parts = SEQ_PARTS[0] * SEQ_PARTS[1] * NZ
    width = size // parts
    pieces = partial.reshape(count, parts, width).transpose(1, 0, 2)
    pieces = lax.all_to_all(pieces, ("sy", "sc", "z"), 0, 0, tiled=True)
    own = jnp.sum(pieces, axis=0)
    spread = jnp.broadcast_to(own[None], (NX * NZ * NY,) + own.shape)
    blocks = lax.all_to_all(spread, ("x", "z", "yh"), 0, 0, tiled=True)
    blocks = blocks.reshape(NX, NZ, NY, count, width).sum(axis=(0, 2))
    return blocks.transpose(1, 0, 2).reshape(count, NZ * width)


def shards(
    tokens,
    out_grad,
    gate_weight,
    up_weight,
    down_weight,
    proj_gate_in,
    proj_gate_out,
    proj_up_in,
    proj_up_out,
    proj_down_in,
    proj_down_out,
    lengths,
):
    examples, seq_dev, model_width = tokens.shape
    scale = float(seq_dev * SEQ_PARTS[0] * SEQ_PARTS[1]) ** (-0.5)
    gate_out, up_out = proj_gate_out.T, proj_up_out.T

    own_grad = out_grad.transpose(0, 2, 1)
    other_grad = lax.ppermute(own_grad, "yh", shifted(NY, 1))
    flat_tokens = tokens.reshape(examples * seq_dev, model_width)
    sent = token_stage(
        flat_tokens,
        gate_weight,
        up_weight,
        proj_gate_in.T,
        proj_up_in.T,
        proj_down_in.T,
        down_weight,
        gate_out,
        up_out,
        lengths,
        scale,
    )
    sent, right = sent[: NX - 1], sent[NX - 1]
    *sent, _ = hold([*sent, other_grad])
    pair = pair_up(own_grad, other_grad)
    messages = [lax.ppermute(piece, "x", shifted(NX, step)) for step, piece in enumerate(sent, 1)]
    hidden, rank = gate_weight.shape[1], gate_out.shape[0]
    rows = 2 * hidden + rank
    first, second, swap = halves(messages[0], messages[2], rows // 2, hidden // 2)
    swap = lax.ppermute(swap, "sc", shifted(SEQ_PARTS[1], 1))
    far = [lax.ppermute(first, "x", shifted(NX, 1)), lax.ppermute(second, "x", shifted(NX, -1))]
    blocks, far_block = ring_z(pair)
    factors, right = keep(sent[0], right, rows)
    products = tail_stage(
        down_weight, gate_out, up_out, proj_down_out.T, right, factors, messages, far, swap, blocks, far_block
    )
    total = sum_everywhere(products.reshape(examples * 3, -1))
    return total.reshape(3, examples, -1).transpose(1, 0, 2)


def solution(mesh):
    fine = Mesh(mesh.devices.reshape(SEQ_PARTS + FSDP_PARTS), ("sy", "sc", "x", "z", "yh"))
    seq, fsdp = ("sy", "sc"), ("x", "z", "yh")
    placed = (
        P(None, seq, None),
        P(None, seq, fsdp),
        P(None, fsdp),
        P(None, fsdp),
        P(fsdp, None),
        P(),
        P(fsdp, None),
        P(),
        P(fsdp, None),
        P(fsdp, None),
        P(),
        P(),
    )
    return jax.shard_map(
        shards, mesh=fine, in_specs=placed, out_specs=P(None, None, seq), check_vma=False
    )
```
